32 devices in a mesh: section: 2 (over y), batch: 16 (over z, x, core).
Axes of the slice: x: 2, y: 2, z: 4, core: 2. Of those that a mesh axis runs over, the one named last changes fastest.
Arguments:
- streams: bfloat16 [2, 13056, 768], P('section', 'batch'), may hold values from -6 to 6
- cotangent: bfloat16 [13056, 768], P('batch'), may hold values from -6 to 6
- counts: int32 [96], P('batch'), may hold values from 22 to 136, as said below
- positions: int32 [96, 136], P('batch'), may hold values from 0 to 224, as said below
- radar_counts: int32 [96], P('batch'), may hold values from 22 to 136, as said below
- radar_positions: int32 [96, 136], P('batch'), may hold values from 0 to 224, as said below
- qkv_weight: bfloat16 [2, 768, 2304], P('section'), may hold values from -0.21875 to 0.21875
- out_weight: bfloat16 [2, 768, 768], P('section'), may hold values from -0.875 to 0.875
- fc1_weight: bfloat16 [2, 768, 3072], P('section'), may hold values from -0.21875 to 0.21875
- fc2_weight: bfloat16 [2, 3072, 768], P('section'), may hold values from -0.15625 to 0.15625
- attn_bias: float32 [2, 2304], P('section'), may hold values from -3 to 3
- mlp_bias: float32 [2, 3840], P('section'), may hold values from -3 to 3
- norm_gains: float32 [2, 1536], P('section'), may hold values from 0.5 to 1.5
- norm_shifts: float32 [2, 1536], P('section'), may hold values from -2 to 2
- cross_qkv_weight: bfloat16 [768, 2304], replicated, may hold values from -0.21875 to 0.21875
- cross_out_weight: bfloat16 [768, 768], replicated, may hold values from -0.875 to 0.875
- cross_gain: float32 [768], replicated, may hold values from 0.5 to 1.5
- cross_bias: float32 [3072], replicated, may hold values from -2 to 2
Outputs:
- layer_out: float32 [2, 13056, 768], P('section', 'batch')
- input_grads: float32 [2, 13056, 768], P('section', 'batch')
- grad_qkv: float32 [2, 768, 2304], P('section', 'batch')
- grad_out: float32 [2, 768, 768], P('section', 'batch')
- grad_fc1: float32 [2, 768, 3072], P('section', 'batch')
- grad_fc2: float32 [2, 3072, 768], P('section', 'batch')
- grad_attn_bias: float32 [2, 2304], P('section', 'batch')
- grad_mlp_bias: float32 [2, 3840], P('section', 'batch')
- grad_norm_gains: float32 [2, 1536], P('section', 'batch')
- grad_norm_shifts: float32 [2, 1536], P('section', 'batch')
- grad_cross_qkv: float32 [768, 2304], P('batch')
- grad_cross_out: float32 [768, 768], P('batch')
- grad_cross_gain: float32 [768], P('batch')
- grad_cross_bias: float32 [3072], P('batch')
The draws below stay inside these ranges and needn't reach their ends.
Inputs may be any that keep to these rules, and one draw needn't show every extreme that they name: The first counts[i] optical slots of image i are live. `positions`: row * 15 + column of the patch in each optical slot; all different within an image. The first radar_counts[i] radar slots of image i are live. `radar_positions`: row * 15 + column of the patch in each radar slot; all different within an image.
All inputs are finite; a program needn't handle non-finite values.
Results may differ from the reference program's by a relative error of at most 0.019.
Values may be sent and summed in bfloat16 or wider, within the bound.
No kernel may reach another device: no remote copies, remote signals or barrier semaphores. Data moves between devices by JAX's collectives and lax.ppermute only.
A program may use at most 256 MiB of HBM per device.

```python
import jax
import jax.numpy as jnp
from jax import lax

D = 768
H = 12
HD = 64
FF = 3072
GRID = 15
PATCHES = 225
CAP = 136
MINVIS = 22
IMAGES = 96
TOKENS = 13056


def visible_counts(key):
    first_key, second_key, third_key = jax.random.split(key, 3)
    drawn = jax.random.randint(first_key, (IMAGES,), MINVIS, CAP + 1)
    fullest = jax.random.randint(second_key, (), 0, IMAGES)
    emptiest = (fullest + 1 + jax.random.randint(third_key, (), 0, IMAGES - 1)) % IMAGES
    places = jnp.arange(IMAGES)
    drawn = jnp.where(places == fullest, CAP, drawn)
    return jnp.where(places == emptiest, MINVIS, drawn).astype(jnp.int32)


def grid_slots(key):
    image_keys = jax.random.split(key, IMAGES)

    def one_image(image_key):
        return jax.random.permutation(image_key, PATCHES)[:CAP]
    return jax.vmap(one_image)(image_keys).astype(jnp.int32)


def draw_counts(key, part):
    key = jax.random.fold_in(key, 11)
    return visible_counts(key)


def draw_positions(key, part):
    key = jax.random.fold_in(key, 12)
    return grid_slots(key)


def draw_radar_counts(key, part):
    key = jax.random.fold_in(key, 13)
    return visible_counts(key)


def draw_radar_positions(key, part):
    key = jax.random.fold_in(key, 14)
    return grid_slots(key)


def levels(stream_key, extent, cuts, smallest, top_value):
    def one(position, shards_of):
        steps = jax.random.uniform(jax.random.fold_in(jax.random.fold_in(stream_key, 6), position), (shards_of,), jnp.float32, smallest / len(cuts), top_value / len(cuts))
        return jnp.repeat(jnp.exp(steps), extent[position] // shards_of).reshape((-1,) + (1,) * (len(extent) - position - 1))

    factor_of = one(*cuts[0])
    for cut in cuts[1:]:
        factor_of = factor_of * one(*cut)
    return factor_of


def gaussian(key, dims, deviation, limit, pieces=(), kind=jnp.bfloat16):
    values = deviation * jax.random.normal(key, dims, jnp.float32)
    if pieces:
        values = values * levels(key, dims, pieces, -0.22, 0.18)
    return jnp.clip(values, -limit, limit).astype(kind)


def setup_inputs(seed: int = 0) -> dict:
    arg_keys = jax.random.split(jax.random.key(seed), 19)
    return {
        "streams": gaussian(arg_keys[0], (2, TOKENS, D), 1.0, 6.0, ((0, 2), (1, 16))),
        "cotangent": gaussian(arg_keys[1], (TOKENS, D), 1.0, 6.0, ((0, 16),)),
        "counts": draw_counts(jax.random.fold_in(arg_keys[18], 71), 0),
        "positions": draw_positions(jax.random.fold_in(arg_keys[18], 71), 0),
        "radar_counts": draw_radar_counts(jax.random.fold_in(arg_keys[18], 71), 0),
        "radar_positions": draw_radar_positions(jax.random.fold_in(arg_keys[18], 71), 0),
        "qkv_weight": gaussian(arg_keys[6], (2, D, 3 * D), D ** -0.5, 0.21875, ((0, 2),)),
        "out_weight": gaussian(arg_keys[7], (2, D, D), (D // 16) ** -0.5, 0.875, ((0, 2),)),
        "fc1_weight": gaussian(arg_keys[8], (2, D, FF), D ** -0.5, 0.21875, ((0, 2),)),
        "fc2_weight": gaussian(arg_keys[9], (2, FF, D), (FF // 2) ** -0.5, 0.15625, ((0, 2),)),
        "attn_bias": gaussian(arg_keys[10], (2, 3 * D), 0.5, 3.0, ((0, 2),), jnp.float32),
        "mlp_bias": gaussian(arg_keys[11], (2, FF + D), 0.5, 3.0, ((0, 2),), jnp.float32),
        "norm_gains": jnp.clip(1.0 + 0.1 * jax.random.normal(arg_keys[12], (2, 2 * D), jnp.float32), 0.5, 1.5),
        "norm_shifts": gaussian(arg_keys[13], (2, 2 * D), 0.3, 2.0, ((0, 2),), jnp.float32),
        "cross_qkv_weight": gaussian(arg_keys[14], (D, 3 * D), D ** -0.5, 0.21875),
        "cross_out_weight": gaussian(arg_keys[15], (D, D), (D // 16) ** -0.5, 0.875),
        "cross_gain": jnp.clip(1.0 + 0.1 * jax.random.normal(arg_keys[16], (D,), jnp.float32), 0.5, 1.5),
        "cross_bias": gaussian(arg_keys[17], (4 * D,), 0.3, 2.0, (), jnp.float32),
    }


HIGHEST = lax.Precision.HIGHEST
SCORE_SCALE = 0.125
NORM_EPS = 1e-06
MASKED_SCORE = -1e+30

@jax.custom_vjp
def low(v):
    return lax.optimization_barrier(v.astype(jnp.bfloat16)).astype(jnp.float32)

@jax.custom_vjp
def low_back(v):
    return v

def low_keep(v):
    return (low(v), None)

def low_pass(kept, grad):
    return (grad,)

def back_keep(v):
    return (v, None)

def back_low(kept, grad):
    return (low(grad),)
low.defvjp(low_keep, low_pass)
low_back.defvjp(back_keep, back_low)

def both_ways(values_in):
    return low(low_back(values_in))

def product(left_mat, right_mat):
    return jnp.dot(left_mat, right_mat, precision=HIGHEST, preferred_element_type=jnp.float32)

def layer_norm(values_in, gain_vec, shift_vec):
    average = lax.optimization_barrier(jnp.mean(values_in, axis=-1, keepdims=True))
    centred = values_in - average
    spread = lax.optimization_barrier(jnp.mean(centred * centred, axis=-1, keepdims=True))
    return centred * lax.rsqrt(spread + NORM_EPS) * gain_vec + shift_vec

def alibi_bias(query_pos, key_pos):
    gap_row = (query_pos[:, None] // GRID - key_pos[None, :] // GRID).astype(jnp.float32)
    gap_col = (query_pos[:, None] % GRID - key_pos[None, :] % GRID).astype(jnp.float32)
    distance = jnp.sqrt(gap_row * gap_row + gap_col * gap_col)
    slopes = 2.0 ** (-8.0 * (jnp.arange(H, dtype=jnp.float32) + 1.0) / H)
    return -slopes[:, None, None] * distance[None, :, :]

def attend(queries, key_rows, value_rows, score_bias, is_live):
    head_q = queries.reshape(CAP, H, HD).transpose(1, 0, 2)
    head_k = key_rows.reshape(CAP, H, HD).transpose(1, 0, 2)
    head_v = value_rows.reshape(CAP, H, HD).transpose(1, 0, 2)
    raw_scores = jnp.einsum('hqd,hkd->hqk', head_q, head_k, precision=HIGHEST) * SCORE_SCALE
    scores = jnp.where(is_live[None, None, :], low_back(raw_scores) + score_bias, MASKED_SCORE)
    weights = low(jax.nn.softmax(scores, axis=-1))
    mixed_heads = jnp.einsum('hqk,hkd->hqd', weights, head_v, precision=HIGHEST)
    return mixed_heads.transpose(1, 0, 2).reshape(CAP, D)

def one_layer(current, weights, section_id, is_live, grid_pos, radar_rows, radar_live, radar_pos):
    qkv_mat, out_mat, fc1_mat, fc2_mat, attn_vec, mlp_vec, gain_vec, shift_vec, cross_mat, cross_proj, cross_gains, cross_vec = weights
    normed = low(layer_norm(current, gain_vec[section_id, :D], shift_vec[section_id, :D]))
    joined = product(normed, qkv_mat[section_id])
    queries = both_ways(joined[:, :D] + attn_vec[section_id, :D])
    key_rows = both_ways(joined[:, D:2 * D])
    value_rows = both_ways(joined[:, 2 * D:] + attn_vec[section_id, D:2 * D])
    attended = both_ways(attend(queries, key_rows, value_rows, alibi_bias(grid_pos, grid_pos), is_live))
    current = current + low_back(product(attended, out_mat[section_id]) + attn_vec[section_id, 2 * D:])
    if section_id == 1:
        normed_cross = low(layer_norm(current, cross_gains, cross_vec[3 * D:]))
        cross_q = both_ways(product(normed_cross, cross_mat[:, :D]) + cross_vec[:D])
        cross_k = both_ways(product(radar_rows, cross_mat[:, D:2 * D]))
        cross_v = both_ways(product(radar_rows, cross_mat[:, 2 * D:]) + cross_vec[D:2 * D])
        cross_att = both_ways(attend(cross_q, cross_k, cross_v, alibi_bias(grid_pos, radar_pos), radar_live))
        current = current + low_back(product(cross_att, cross_proj) + cross_vec[2 * D:3 * D])
    normed_two = low(layer_norm(current, gain_vec[section_id, D:], shift_vec[section_id, D:]))
    up_proj = low_back(product(normed_two, fc1_mat[section_id]) + mlp_vec[section_id, :FF])
    active = low(jax.nn.gelu(up_proj, approximate=False))
    current = current + low_back(product(active, fc2_mat[section_id]) + mlp_vec[section_id, FF:])
    return current * is_live.astype(current.dtype)[:, None]

def reference(streams, cotangent, counts, positions, radar_counts, radar_positions, qkv_weight, out_weight, fc1_weight, fc2_weight, attn_bias, mlp_bias, norm_gains, norm_shifts, cross_qkv_weight, cross_out_weight, cross_gain, cross_bias):
    params = tuple((weight_now.astype(jnp.float32) for weight_now in (qkv_weight, out_weight, fc1_weight, fc2_weight, attn_bias, mlp_bias, norm_gains, norm_shifts, cross_qkv_weight, cross_out_weight, cross_gain, cross_bias)))
    slot_ids = jnp.arange(CAP, dtype=jnp.int32)
    image_rows = streams[0].astype(jnp.float32).reshape(IMAGES, CAP, D)
    radar_all = streams[1].astype(jnp.float32).reshape(IMAGES, CAP, D)
    seed_rows = cotangent.astype(jnp.float32).reshape(IMAGES, CAP, D)

    def one_image(totals, inputs_now):
        image_now, radar_now, seed_now, count_now, grid_pos, radar_count, radar_pos = inputs_now
        is_live = slot_ids < count_now
        radar_live = slot_ids < radar_count

        def forward(weights, image_in, radar_in):
            first_out = one_layer(image_in, weights, 0, is_live, grid_pos, radar_in, radar_live, radar_pos)
            second_out = one_layer(both_ways(first_out), weights, 1, is_live, grid_pos, radar_in, radar_live, radar_pos)
            return (first_out, second_out)
        (first_out, second_out), pull_back = jax.vjp(forward, params, image_now, radar_now)
        grad_params, grad_image, grad_radar = pull_back((jnp.zeros_like(first_out), seed_now))
        totals = jax.tree.map(jnp.add, totals, grad_params)
        return (totals, (first_out, second_out, grad_image, grad_radar))
    zero_grads = jax.tree.map(jnp.zeros_like, params)
    totals, (first_all, second_all, grad_images, grad_radars) = lax.scan(one_image, zero_grads, (image_rows, radar_all, seed_rows, counts, positions, radar_counts, radar_positions))
    layer_out = jnp.stack([first_all.reshape(TOKENS, D), second_all.reshape(TOKENS, D)])
    input_grads = jnp.stack([grad_images.reshape(TOKENS, D), grad_radars.reshape(TOKENS, D)])
    return (layer_out, input_grads, totals[0], totals[1], totals[2], totals[3], totals[4], totals[5], totals[6], totals[7], totals[8], totals[9], totals[10], totals[11])
```

```python
import jax
import jax.numpy as jnp
from jax import lax
from jax.experimental import pallas as pl
from jax.experimental.pallas import tpu as pltpu
from jax.sharding import PartitionSpec as P

H = 12
HD = 64
PAIRS = H // 2
LANES = 2 * HD
GRID = 15
SCORE_SCALE = 0.125
NORM_EPS = 1e-06
FAR = 1e33
CHUNK = 16
BF = jnp.bfloat16
F32 = jnp.float32
VMEM_LIMIT = 60 << 20
CHEAP = pl.CostEstimate(flops=1, bytes_accessed=1, transcendentals=0)
ANY = pl.BlockSpec(memory_space=pl.ANY)
VM = pl.BlockSpec(memory_space=pltpu.VMEM)
SM = pl.BlockSpec(memory_space=pltpu.SMEM)


def dot_nn(left, right):
    return jnp.dot(left, right, preferred_element_type=F32)


def dot_tn(left, right):
    return lax.dot_general(left, right, (((0,), (0,)), ((), ())), preferred_element_type=F32)


def dot_nt(left, right):
    return lax.dot_general(left, right, (((1,), (1,)), ((), ())), preferred_element_type=F32)


class Copies:
    def __init__(self, sems):
        self.sems = sems
        self.used = 0

    def start(self, source, target):
        copy = pltpu.make_async_copy(source, target, self.sems.at[self.used])
        self.used += 1
        copy.start()
        return copy

    def reserve(self, count):
        first = self.used
        self.used += count
        return lambda at: self.sems.at[first + at]


def spans(rows):
    return [slice(at, at + CHUNK) for at in range(0, rows, CHUNK)]


def norm_parts(values):
    average = jnp.mean(values, axis=-1, keepdims=True)
    centred = values - average
    spread = jnp.mean(centred * centred, axis=-1, keepdims=True)
    scale = lax.rsqrt(spread + NORM_EPS)
    return centred * scale, scale


def norm_forward(source, gain, shift, target):
    for span in spans(source.shape[0]):
        unit, _ = norm_parts(source[span, :])
        target[span, :] = (unit * gain + shift).astype(BF)


def norm_backward(source, gain, upstream, residual, target):
    gain_sum = jnp.zeros((8, source.shape[1]), F32)
    shift_sum = jnp.zeros((8, source.shape[1]), F32)
    for span in spans(source.shape[0]):
        unit, scale = norm_parts(source[span, :])
        grad = upstream[span, :]
        product = grad * unit
        gain_sum = gain_sum + product[:8] + product[8:]
        shift_sum = shift_sum + grad[:8] + grad[8:]
        inner = grad * gain
        mean_one = jnp.mean(inner, axis=-1, keepdims=True)
        mean_two = jnp.mean(inner * unit, axis=-1, keepdims=True)
        target[span, :] = residual[span, :] + scale * (inner - mean_one - unit * mean_two)
    return (
        jnp.sum(gain_sum, axis=0, keepdims=True),
        jnp.sum(shift_sum, axis=0, keepdims=True),
    )


def gelu_both(values):
    cdf = 0.5 + 0.5 * lax.erf(values * 0.7071067811865476)
    density = 0.3989422804014327 * jnp.exp(-0.5 * values * values)
    return values * cdf, cdf + values * density


def place(positions):
    values = positions
    row = jnp.floor((values + 0.5) * (1.0 / GRID))
    return row, values - GRID * row


def distances(key_col, query_row, live_keys):
    row_q, col_q = place(query_row)
    row_k, col_k = place(key_col)
    gap_row = row_q - row_k
    gap_col = col_q - col_k
    distance = jnp.sqrt(gap_row * gap_row + gap_col * gap_col)
    slot = lax.broadcasted_iota(jnp.int32, distance.shape, 0)
    return jnp.where(slot < live_keys, distance, FAR)


def both_heads(pair):
    first = lax.broadcasted_iota(jnp.int32, pair.shape, 1) < HD
    zero = jnp.zeros_like(pair)
    return jnp.concatenate([jnp.where(first, pair, zero), jnp.where(first, zero, pair)], axis=0)


def one_pair(stacked):
    half = stacked.shape[0] // 2
    first = lax.broadcasted_iota(jnp.int32, (half, LANES), 1) < HD
    return jnp.where(first, stacked[:half], stacked[half:])


def by_size(plan, most_live, work):
    def step(image, carry):
        if plan.slots <= LANES:
            work(image, plan.slots)
        else:
            live = most_live(image)

            @pl.when(live <= LANES)
            def _():
                work(image, LANES)

            @pl.when(live > LANES)
            def _():
                work(image, plan.slots)

        return carry

    lax.fori_loop(0, plan.per, step, 0)


def rows_of(plan, image, first, size):
    return pl.ds(pl.multiple_of(image * plan.slots + first, 8), size)


def pair_lanes(base, pair):
    if isinstance(pair, int):
        return pl.ds(base + pair * LANES, LANES)
    return pl.ds(pl.multiple_of(base + pair * LANES, LANES), LANES)


def over_pairs(plan, work, size):
    unroll = PAIRS if size <= LANES else plan.unroll

    def step(at, carry):
        for part in range(unroll):
            work(at * unroll + part)
        return carry

    if unroll == PAIRS:
        step(0, 0)
    else:
        lax.fori_loop(0, PAIRS // unroll, step, 0)


def attend(plan, most_live, query, keys, values, spread, slopes, heard, weights):
    def work(image, size):
        rows = rows_of(plan, image, 0, size)
        if size < plan.slots:
            rest = rows_of(plan, image, size, plan.slots - size)
            heard[rest, :] = jnp.zeros((plan.slots - size, plan.width), F32)
        spread(image, size)
        gap_ref = spread.target

        def one(pair):
            q = both_heads(query[0][rows, pair_lanes(query[1], pair)]).astype(BF)
            k = keys[0][rows, pair_lanes(keys[1], pair)].astype(BF)
            v = values[0][rows, pair_lanes(values[1], pair)].astype(BF)
            first = lax.broadcasted_iota(jnp.int32, (1, 2 * size), 1) < size
            slope = jnp.where(first, slopes[2 * pair], slopes[2 * pair + 1])
            scores = dot_nt(k, q) - slope * gap_ref[image, :size, : 2 * size]
            scores = jnp.exp(scores - jnp.max(scores, axis=0, keepdims=True))
            totals = jnp.sum(scores, axis=0, keepdims=True)
            p = (scores * (1.0 / totals)).astype(BF)
            weights[image * PAIRS + pair, :size, : 2 * size] = p
            heard[rows, pair_lanes(0, pair)] = one_pair(dot_tn(p, v))

        over_pairs(plan, one, size)

    by_size(plan, most_live, work)


def attend_back(plan, most_live, query, keys, values, grad_heard, weights, grads):
    grad_q, grad_k, grad_v = grads

    def work(image, size):
        rows = rows_of(plan, image, 0, size)
        if size < plan.slots:
            rest = rows_of(plan, image, size, plan.slots - size)
            for ref, offset in grads:
                ref[rest, offset : offset + plan.width] = jnp.zeros((plan.slots - size, plan.width), F32)

        def one(pair):
            q = both_heads(query[0][rows, pair_lanes(query[1], pair)]).astype(BF)
            k = keys[0][rows, pair_lanes(keys[1], pair)].astype(BF)
            v = values[0][rows, pair_lanes(values[1], pair)].astype(BF)
            g = both_heads(grad_heard[rows, pair_lanes(0, pair)]).astype(BF)
            p = weights[image * PAIRS + pair, :size, : 2 * size]
            wide = p.astype(F32)
            product = dot_nt(v, g) * wide
            grad_s = (product - wide * jnp.sum(product, axis=0, keepdims=True)).astype(BF)
            grad_v[0][rows, pair_lanes(grad_v[1], pair)] = dot_nn(p, g)
            grad_k[0][rows, pair_lanes(grad_k[1], pair)] = dot_nn(grad_s, q)
            grad_q[0][rows, pair_lanes(grad_q[1], pair)] = one_pair(dot_tn(grad_s, k)) * SCORE_SCALE

        over_pairs(plan, one, size)

    by_size(plan, most_live, work)


def columns_of(positions):
    images = positions.shape[0]
    low = positions.astype(F32).astype(BF)
    row = lax.broadcasted_iota(jnp.int32, (images, LANES), 0)
    lane = lax.broadcasted_iota(jnp.int32, (images, LANES), 1)
    return dot_tn(low, (row == lane).astype(F32).astype(BF))


def twice(positions, size):
    slots = positions.shape[1]
    low = positions.astype(F32).astype(BF)
    row = lax.broadcasted_iota(jnp.int32, (slots, 2 * size), 0)
    lane = lax.broadcasted_iota(jnp.int32, (slots, 2 * size), 1)
    from_slot = jnp.where(lane < size, lane, lane - size)
    return dot_nn(low, (row == from_slot).astype(F32).astype(BF))


class Spread:
    def __init__(self, plan, r, target, k, key_positions, key_count):
        self.plan, self.r, self.target, self.k = plan, r, target, k
        self.key_positions, self.key_count = key_positions, key_count

    def __call__(self, image, size):
        at = self.k * self.plan.per + image
        query = twice(self.r["positions"][pl.ds(at, 1), :], size)
        keys = columns_of(self.r[self.key_positions][pl.ds(at, 1), :])
        self.target[image, :size, : 2 * size] = distances(
            keys[:size, :1], query, self.r[self.key_count][at]
        )


def most_live(plan, r, k, names):
    def live(image):
        found = r[names[0]][k * plan.per + image]
        for name in names[1:]:
            found = jnp.maximum(found, r[name][k * plan.per + image])
        return found

    return live


def fill_rows(target, images, slots, counts, first_image, source):
    for image in range(images):
        live = counts[first_image + image]
        for at in range(0, slots, 8):
            span = slice(image * slots + at, image * slots + at + 8)
            row = at + lax.broadcasted_iota(jnp.int32, (8, source.shape[1]), 0)
            target[span, :] = jnp.where(row < live, source[span, :], 0.0)


class Plan:
    def __init__(self, batches, slots, width, hidden, halving, unroll=1):
        self.batches, self.slots, self.width, self.hidden = batches, slots, width, hidden
        self.halving = halving
        self.unroll = unroll
        self.per = 2 if batches % 2 == 0 else 1
        self.steps = batches // self.per
        self.rows = self.per * slots
        self.total = batches * slots

    def unrolled(self, unroll):
        return Plan(self.batches, self.slots, self.width, self.hidden, self.halving, unroll)


def small_shape(plan):
    rows = 13 + plan.hidden // plan.width
    return (-(-rows // 8) * 8, plan.width)


WEIGHT_NAMES = ("wqkv", "wout", "wfc1", "wfc2", "wcqkv", "wcout")


def scratch_shapes(plan):
    r, d, f = plan.rows, plan.width, plan.hidden
    w = {
        "wqkv": ((d, 3 * d), BF),
        "wout": ((d, d), BF),
        "wfc1": ((d, f), BF),
        "wfc2": ((f, d), BF),
        "wcqkv": ((d, 3 * d), BF),
        "wcout": ((d, d), BF),
        "xb": ((r, d), BF),
        "x": ((r, d), F32),
        "n": ((r, d), BF),
        "qkv": ((r, 3 * d), F32),
        "p": ((plan.per * PAIRS, plan.slots, 2 * plan.slots), BF),
        "dist": ((plan.per, plan.slots, 2 * plan.slots), F32),
        "heard": ((r, d), F32),
        "o": ((r, d), BF),
        "h": ((r, d), F32),
        "n2": ((r, d), BF),
        "u": ((r, f), F32),
        "a": ((r, f), BF),
        "gp": ((r, f), BF),
        "y": ((r, d), F32),
        "yout": ((r, d), F32),
        "ysend": ((r, d), BF),
        "gin": ((r, d), BF),
        "g": ((r, d), F32),
        "gbr": ((r, d), BF),
        "du": ((r, f), BF),
        "dn": ((r, d), F32),
        "dh": ((r, d), F32),
        "gm": ((r, d), BF),
        "go": ((r, d), F32),
        "dqkv": ((r, 3 * d), F32),
        "dqkvb": ((r, 3 * d), BF),
        "dx": ((r, d), F32),
        "dxb": ((r, d), BF),
        "ln": ((8, d), F32),
        "cdist": ((plan.per, plan.slots, 2 * plan.slots), F32),
        "m": ((r, d), BF),
        "cq": ((r, d), F32),
        "ckvb": ((r, 2 * d), BF),
        "ckv": ((r, 2 * d), F32),
        "cp": ((plan.per * PAIRS, plan.slots, 2 * plan.slots), BF),
        "cheard": ((r, d), F32),
        "co": ((r, d), BF),
        "h2": ((r, d), F32),
        "gaf": ((r, d), BF),
        "cgo": ((r, d), F32),
        "dcqkv": ((r, 3 * d), F32),
        "dcq": ((r, d), BF),
        "dckv": ((r, 2 * d), BF),
        "dm": ((r, d), F32),
        "dmid": ((r, d), F32),
        "gl": ((plan.total, f), BF),
        "gr": ((plan.total, f), BF),
        "gsums": ((8, f), F32),
        "small": (small_shape(plan), F32),
        "gnat": ((2, 16, d // 16, d) if plan.halving else (2, d, d), BF),
        "gnat_tall": ((2, 4, d // 4, d), BF),
        "gout": ((2, 2, 8, d // 16, d), BF),
        "gout_tall": ((2, 2, 2, d // 4, d), BF),
        "rdr": ((plan.total, d), F32),
        "rb": ((plan.total, d), BF),
        "rkv": ((plan.total, 2 * d), BF),
    }
    return w


def chunk_shape(plan, height, breadth):
    if not plan.halving:
        return (height, breadth), BF
    if height == plan.width:
        return (8, height // 16, breadth), BF
    return (2, 2, 2, height // 16, breadth), BF


def chunk_state(name, height, breadth):
    def size(plan, amount):
        return plan.hidden if amount is None else amount * plan.width

    def main(plan):
        return chunk_shape(plan, size(plan, height), size(plan, breadth))

    def sums(plan):
        return (8, size(plan, breadth)), F32

    return {name: main, name + "_send": main, name + "_sums": sums}


STATE = {
    "n": lambda p: ((p.total, p.width), BF),
    "o": lambda p: ((p.total, p.width), BF),
    "n2": lambda p: ((p.total, p.width), BF),
    "a": lambda p: ((p.total, p.hidden), BF),
    "layer_out": lambda p: ((p.total, p.width), F32),
    "qkv": lambda p: ((p.total, 3 * p.width), F32),
    "p": lambda p: ((p.batches * PAIRS, p.slots, 2 * p.slots), BF),
    "h": lambda p: ((p.total, p.width), F32),
    "gp": lambda p: ((p.total, p.hidden), BF),
    "ckv": lambda p: ((p.total, 2 * p.width), BF),
    "gbr": lambda p: ((p.total, p.width), BF),
    "du": lambda p: ((p.total, p.hidden), BF),
    "gm": lambda p: ((p.total, p.width), BF),
    "dqkv": lambda p: ((p.total, 3 * p.width), BF),
    "input_grads": lambda p: ((p.total, p.width), F32),
    "m": lambda p: ((p.total, p.width), BF),
    "co": lambda p: ((p.total, p.width), BF),
    "gaf": lambda p: ((p.total, p.width), BF),
    "dcq": lambda p: ((p.total, p.width), BF),
    "dckv": lambda p: ((p.total, 2 * p.width), BF),
    "between": lambda p: ((p.rows, p.width), F32),
    "send": lambda p: ((p.rows, p.width), BF),
    "ln": lambda p: ((8, p.width), F32),
    "small": lambda p: (small_shape(p), F32),
    **chunk_state("cross", 1, 4),
    **chunk_state("fc2", None, 1),
    **chunk_state("fc1", 1, None),
    **chunk_state("attn", 1, 4),
}

FORWARD_0 = dict(
    reads=("streams",),
    writes=("n", "o", "n2", "a", "layer_out", "qkv", "p", "h", "gp", "send"),
    weights=("wqkv", "wout", "wfc1", "wfc2"),
    scratch=("xb", "x", "n", "qkv", "p", "dist", "heard", "o", "h", "n2", "u", "a", "gp", "y", "yout", "ysend"),
)
RADAR = dict(reads=("streams",), writes=("ckv",), weights=("wcqkv",), scratch=["rb", "rkv"])
MERGED = dict(
    reads=("received", "cotangent", "ckv"),
    writes=("n", "o", "n2", "a", "layer_out", "gbr", "du", "gm", "dqkv", "m", "co", "gaf", "dcq", "dckv", "send", "ln"),
    weights=WEIGHT_NAMES,
    scratch=("xb", "x", "n", "qkv", "p", "dist", "heard", "o", "h", "n2", "u", "a", "gp", "y", "yout", "gin", "g", "gbr", "du", "dn", "dh", "gm", "go", "dqkv", "dqkvb", "dxb", "ln", "cdist", "m", "cq", "ckvb", "ckv", "cp", "cheard", "co", "h2", "gaf", "cgo", "dcqkv", "dcq", "dckv", "dm", "dmid",),
)
BACKWARD_0 = dict(
    reads=("streams", "returned", "qkv", "p", "h", "gp"),
    writes=("gbr", "du", "gm", "dqkv", "input_grads", "ln"),
    weights=("wfc2", "wfc1", "wout", "wqkv"),
    scratch=("xb", "x", "qkv", "p", "h", "gp", "gin", "g", "gbr", "du", "dn", "dh", "gm", "go", "dqkv", "dqkvb", "dx", "ln"),
)
BACKWARD_MLP = dict(
    reads=("returned", "gp", "h"),
    writes=("du", "between", "ln"),
    weights=("wfc2", "wfc1"),
    scratch=("h", "gp", "gin", "g", "gbr", "du", "dn", "dh", "ln"),
)
BACKWARD_SELF = dict(
    reads=("between", "streams", "qkv", "p"),
    writes=("gm", "dqkv", "input_grads", "ln"),
    weights=("wout", "wqkv"),
    scratch=("xb", "x", "qkv", "p", "dn", "dh", "gm", "go", "dqkv", "dqkvb", "dx", "ln"),
)
RADAR_BACK = dict(
    reads=("dckv",), writes=("input_grads",), weights=("wcqkv",), scratch=("rkv", "rdr")
)
GRAD_SCRATCH = ("gl", "gr", "gnat", "gout", "gsums")
GRADS_CROSS = dict(
    reads=("m", "streams", "co", "dcq", "dckv", "gaf"),
    writes=("cross", "cross_send", "cross_sums"),
    weights=(),
    scratch=GRAD_SCRATCH,
)
GRADS_FC2 = dict(
    reads=("a", "gbr", "returned"),
    writes=("fc2", "fc2_send", "fc2_sums"),
    weights=(),
    scratch=("gl", "gr", "gnat", "gnat_tall", "gout_tall", "gsums", "gin", "dn", "g"),
)
GRADS_FC1 = dict(
    reads=("n2", "du"), writes=("fc1", "fc1_send", "fc1_sums"), weights=(), scratch=GRAD_SCRATCH
)
GRADS_ATTN = dict(
    reads=("n", "o", "dqkv", "gm", "fc1_sums", "fc2_sums", "cross_sums"),
    writes=("attn", "attn_send", "attn_sums", "small"),
    weights=(),
    scratch=GRAD_SCRATCH + ("small",),
)
GRADS_MORE = {
    name: tuple(dict.fromkeys(GRADS_FC2[name] + GRADS_FC1[name]))
    for name in GRADS_FC2
}
JOBS = {
    "forward": FORWARD_0,
    "radar": RADAR,
    "merged": MERGED,
    "backward": BACKWARD_0,
    "backward_mlp": BACKWARD_MLP,
    "backward_self": BACKWARD_SELF,
    "radar_back": RADAR_BACK,
    "grads_cross": GRADS_CROSS,
    "grads_fc2": GRADS_FC2,
    "grads_fc1": GRADS_FC1,
    "grads_attn": GRADS_ATTN,
    "grads_more": GRADS_MORE,
}
TILE = 768


def tiles(extent, tile=TILE):
    return [slice(at, min(at + tile, extent)) for at in range(0, extent, tile)]


def self_forward(plan, r, s, c, k, waits, save):
    d = plan.width
    rows = pl.ds(k * plan.rows, plan.rows)
    out = []
    gain, shift, bias = r["gains"], r["shifts"], r["attn_bias"]
    norm_forward(s["x"], gain[:, :d], shift[:, :d], s["n"])
    out.append(c.start(s["n"], r["n"].at[rows]))
    waits["wqkv"].wait()
    normed = s["n"][...]
    s["qkv"][:, :d] = (dot_nn(normed, s["wqkv"][:, :d]) + bias[:, :d]).astype(BF).astype(F32) * SCORE_SCALE
    s["qkv"][:, d : 2 * d] = dot_nn(normed, s["wqkv"][:, d : 2 * d])
    s["qkv"][:, 2 * d :] = dot_nn(normed, s["wqkv"][:, 2 * d :]) + bias[:, d : 2 * d]
    if save:
        out.append(c.start(s["qkv"], r["qkv"].at[rows]))
    attend(
        plan,
        most_live(plan, r, k, ("counts",)),
        (s["qkv"], 0),
        (s["qkv"], d),
        (s["qkv"], 2 * d),
        Spread(plan, r, s["dist"], k, "positions", "counts"),
        r["slopes"],
        s["heard"],
        s["p"],
    )
    if save:
        out.append(c.start(s["p"], r["p"].at[pl.ds(k * plan.per * PAIRS, plan.per * PAIRS)]))
    s["o"][...] = s["heard"][...].astype(BF)
    out.append(c.start(s["o"], r["o"].at[rows]))
    waits["wout"].wait()
    s["h"][...] = s["x"][...] + dot_nn(s["o"][...], s["wout"][...]) + bias[:, 2 * d :]
    if save:
        out.append(c.start(s["h"], r["h"].at[rows]))
    return out


def mlp_forward(plan, r, s, c, k, waits, after, save):
    d, f = plan.width, plan.hidden
    rows = pl.ds(k * plan.rows, plan.rows)
    out = []
    norm_forward(after, r["gains"][:, d:], r["shifts"][:, d:], s["n2"])
    out.append(c.start(s["n2"], r["n2"].at[rows]))
    waits["wfc1"].wait()
    bias = r["mlp_bias"]
    for tile in tiles(f):
        s["u"][:, tile] = dot_nn(s["n2"][...], s["wfc1"][:, tile]) + bias[:, tile]
        for span in spans(plan.rows):
            active, slope = gelu_both(s["u"][span, tile])
            s["a"][span, tile] = active.astype(BF)
            s["gp"][span, tile] = slope.astype(BF)
    out.append(c.start(s["a"], r["a"].at[rows]))
    if save:
        out.append(c.start(s["gp"], r["gp"].at[rows]))
    waits["wfc2"].wait()
    s["y"][...] = after[...] + dot_nn(s["a"][...], s["wfc2"][...]) + bias[:, f:]
    fill_rows(s["yout"], plan.per, plan.slots, r["counts"], k * plan.per, s["y"])
    out.append(c.start(s["yout"], r["layer_out"].at[rows]))
    return out


def mlp_backward(plan, r, s, c, k, waits, after, target):
    d, f = plan.width, plan.hidden
    rows = pl.ds(k * plan.rows, plan.rows)
    out = []
    s["dn"][...] = s["gin"][...].astype(F32)
    fill_rows(s["g"], plan.per, plan.slots, r["counts"], k * plan.per, s["dn"])
    s["gbr"][...] = s["g"][...].astype(BF)
    if "gbr" in r:
        out.append(c.start(s["gbr"], r["gbr"].at[rows]))
    if "wfc2" in waits:
        waits["wfc2"].wait()
    for tile in tiles(f):
        grad = dot_nt(s["gbr"][...], s["wfc2"][tile, :])
        s["du"][:, tile] = (grad * s["gp"][:, tile].astype(F32)).astype(BF)
    out.append(c.start(s["du"], r["du"].at[rows]))
    if "wfc1" in waits:
        waits["wfc1"].wait()
    s["dn"][...] = dot_nt(s["du"][...], s["wfc1"][...])
    sums = norm_backward(after, r["gains"][:, d:], s["dn"], s["g"], target)
    return out, sums


def self_backward(plan, r, s, c, k, waits, grad, target):
    d = plan.width
    rows = pl.ds(k * plan.rows, plan.rows)
    out = []
    s["gm"][...] = grad[...].astype(BF)
    out.append(c.start(s["gm"], r["gm"].at[rows]))
    if "wout" in waits:
        waits["wout"].wait()
    s["go"][...] = dot_nt(s["gm"][...], s["wout"][...])
    attend_back(
        plan,
        most_live(plan, r, k, ("counts",)),
        (s["qkv"], 0),
        (s["qkv"], d),
        (s["qkv"], 2 * d),
        s["go"],
        s["p"],
        [(s["dqkv"], part * d) for part in range(3)],
    )
    s["dqkvb"][...] = s["dqkv"][...].astype(BF)
    out.append(c.start(s["dqkvb"], r["dqkv"].at[rows]))
    if "wqkv" in waits:
        waits["wqkv"].wait()
    s["dn"][...] = dot_nt(s["dqkvb"][...], s["wqkv"][...])
    sums = norm_backward(s["x"], r["gains"][:, :d], s["dn"], grad, target)
    return out, sums


def write_sums(s, c, r, parts):
    s["ln"][...] = jnp.zeros_like(s["ln"])
    for at, part in enumerate(parts):
        s["ln"][at : at + 1, :] = part
    return c.start(s["ln"], r["ln"])


def start_weights(r, s, c, names):
    return {name: c.start(r[name], s[name]) for name in names}


def run_forward(plan, r, s, c, k):
    rows = pl.ds(k * plan.rows, plan.rows)
    arrive = c.start(r["streams"].at[rows], s["xb"])
    waits = start_weights(r, s, c, FORWARD_0["weights"])
    arrive.wait()
    s["x"][...] = s["xb"][...].astype(F32)
    out = self_forward(plan, r, s, c, k, waits, True)
    out += mlp_forward(plan, r, s, c, k, waits, s["h"], True)
    s["ysend"][...] = s["yout"][...].astype(BF)
    out.append(c.start(s["ysend"], r["send"]))
    for copy in out:
        copy.wait()


def run_radar(plan, r, s, c, k):
    d = plan.width
    arrive = c.start(r["streams"], s["rb"])
    weight = c.start(r["wcqkv"], s["wcqkv"])
    arrive.wait()
    weight.wait()
    s["rkv"][:, :d] = dot_nn(s["rb"][...], s["wcqkv"][:, d : 2 * d]).astype(BF)
    s["rkv"][:, d:] = (
        dot_nn(s["rb"][...], s["wcqkv"][:, 2 * d :]) + r["cross_bias"][:, d : 2 * d]
    ).astype(BF)
    c.start(s["rkv"], r["ckv"]).wait()


def run_merged(plan, r, s, c, k):
    plan = plan.unrolled(3)
    d = plan.width
    rows = pl.ds(k * plan.rows, plan.rows)
    arrive = c.start(r["received"], s["xb"])
    waits = start_weights(r, s, c, ("wqkv", "wout", "wcqkv", "wcout", "wfc1", "wfc2"))
    arrive_kv = c.start(r["ckv"].at[rows], s["ckvb"])
    arrive_grad = c.start(r["cotangent"].at[rows], s["gin"])
    arrive.wait()
    s["x"][...] = s["xb"][...].astype(F32)
    out = self_forward(plan, r, s, c, k, waits, False)
    bias = r["cross_bias"]
    norm_forward(s["h"], r["cross_gain"][...], bias[:, 3 * d :], s["m"])
    out.append(c.start(s["m"], r["m"].at[rows]))
    waits["wcqkv"].wait()
    s["cq"][...] = (dot_nn(s["m"][...], s["wcqkv"][:, :d]) + bias[:, :d]).astype(BF).astype(F32) * SCORE_SCALE
    arrive_kv.wait()
    s["ckv"][...] = s["ckvb"][...].astype(F32)
    live = most_live(plan, r, k, ("counts", "radar_counts"))
    attend(
        plan,
        live,
        (s["cq"], 0),
        (s["ckv"], 0),
        (s["ckv"], d),
        Spread(plan, r, s["cdist"], k, "radar_positions", "radar_counts"),
        r["slopes"],
        s["cheard"],
        s["cp"],
    )
    s["co"][...] = s["cheard"][...].astype(BF)
    out.append(c.start(s["co"], r["co"].at[rows]))
    waits["wcout"].wait()
    s["h2"][...] = s["h"][...] + dot_nn(s["co"][...], s["wcout"][...]) + bias[:, 2 * d : 3 * d]
    out += mlp_forward(plan, r, s, c, k, waits, s["h2"], False)
    arrive_grad.wait()
    more, sums_two = mlp_backward(plan, r, s, c, k, {}, s["h2"], s["dh"])
    out += more
    s["gaf"][...] = s["dh"][...].astype(BF)
    out.append(c.start(s["gaf"], r["gaf"].at[rows]))
    s["cgo"][...] = dot_nt(s["gaf"][...], s["wcout"][...])
    attend_back(
        plan,
        live,
        (s["cq"], 0),
        (s["ckv"], 0),
        (s["ckv"], d),
        s["cgo"],
        s["cp"],
        [(s["dcqkv"], part * d) for part in range(3)],
    )
    s["dcq"][...] = s["dcqkv"][:, :d].astype(BF)
    s["dckv"][...] = s["dcqkv"][:, d:].astype(BF)
    out.append(c.start(s["dcq"], r["dcq"].at[rows]))
    out.append(c.start(s["dckv"], r["dckv"].at[rows]))
    s["dm"][...] = dot_nt(s["dcq"][...], s["wcqkv"][:, :d])
    sums_cross = norm_backward(s["h"], r["cross_gain"][...], s["dm"], s["dh"], s["dmid"])
    more, sums_one = self_backward(plan, r, s, c, k, {}, s["dmid"], s["dh"])
    out += more
    s["dxb"][...] = s["dh"][...].astype(BF)
    out.append(c.start(s["dxb"], r["send"]))
    out.append(write_sums(s, c, r, sums_one + sums_two + sums_cross))
    for copy in out:
        copy.wait()


def load_mlp_back(plan, r, s, c, k):
    rows = pl.ds(k * plan.rows, plan.rows)
    arrive = [c.start(r["returned"], s["gin"])]
    waits = start_weights(r, s, c, ("wfc2",))
    arrive.append(c.start(r["gp"].at[rows], s["gp"]))
    waits.update(start_weights(r, s, c, ("wfc1",)))
    arrive.append(c.start(r["h"].at[rows], s["h"]))
    return arrive, waits


def load_self_back(plan, r, s, c, k):
    rows = pl.ds(k * plan.rows, plan.rows)
    waits = start_weights(r, s, c, ("wout",))
    arrive = [
        c.start(r["qkv"].at[rows], s["qkv"]),
        c.start(r["p"].at[pl.ds(k * plan.per * PAIRS, plan.per * PAIRS)], s["p"]),
    ]
    waits.update(start_weights(r, s, c, ("wqkv",)))
    arrive.append(c.start(r["streams"].at[rows], s["xb"]))
    return arrive, waits


def wait_all(copies):
    for copy in copies:
        copy.wait()


def run_backward(plan, r, s, c, k):
    rows = pl.ds(k * plan.rows, plan.rows)
    arrive, waits = load_mlp_back(plan, r, s, c, k)
    arrive_self, waits_self = load_self_back(plan, r, s, c, k)
    waits.update(waits_self)
    wait_all(arrive)
    out, sums_two = mlp_backward(plan, r, s, c, k, waits, s["h"], s["dh"])
    wait_all(arrive_self)
    s["x"][...] = s["xb"][...].astype(F32)
    more, sums_one = self_backward(plan, r, s, c, k, waits, s["dh"], s["dx"])
    out += more
    out.append(c.start(s["dx"], r["input_grads"].at[rows]))
    out.append(write_sums(s, c, r, sums_one + sums_two))
    wait_all(out)


def run_backward_mlp(plan, r, s, c, k):
    arrive, waits = load_mlp_back(plan, r, s, c, k)
    wait_all(arrive)
    out, sums_two = mlp_backward(plan, r, s, c, k, waits, s["h"], s["dh"])
    out.append(c.start(s["dh"], r["between"]))
    nothing = jnp.zeros_like(sums_two[0])
    out.append(write_sums(s, c, r, (nothing, nothing) + sums_two))
    wait_all(out)


def run_backward_self(plan, r, s, c, k):
    rows = pl.ds(k * plan.rows, plan.rows)
    arrive = [c.start(r["between"], s["dh"])]
    more, waits = load_self_back(plan, r, s, c, k)
    wait_all(arrive + more)
    s["x"][...] = s["xb"][...].astype(F32)
    out, sums_one = self_backward(plan, r, s, c, k, waits, s["dh"], s["dx"])
    out.append(c.start(s["dx"], r["input_grads"].at[rows]))
    out.append(write_sums(s, c, r, sums_one))
    wait_all(out)


def run_radar_back(plan, r, s, c, k):
    d = plan.width
    arrive = c.start(r["dckv"], s["rkv"])
    weight = c.start(r["wcqkv"], s["wcqkv"])
    arrive.wait()
    weight.wait()
    s["rdr"][...] = dot_nt(s["rkv"][...], s["wcqkv"][:, d:])
    c.start(s["rdr"], r["input_grads"]).wait()


def slot_of(relative):
    return ((relative >> 1) & 1) * 4 + ((relative >> 2) & 1) * 2 + ((relative >> 3) & 1)


def weight_grads(plan, r, s, c, lefts, rights, left_of, tall, name, fix=None):
    d, total = plan.width, plan.total

    def blocks(buffer, names):
        found = []
        for array in names:
            for tile in tiles(r[array].shape[1], d):
                at = len(found) * d
                found.append((r[array].at[:, tile], buffer.at[:, at : at + d]))
        return found

    left_blocks, right_blocks = blocks(s["gl"], lefts), blocks(s["gr"], rights)
    count = max(len(left_blocks), len(right_blocks))
    loads, seen = [], set()
    for t in range(count):
        wanted = [(0, 0 if tall else t), (1, left_of(t))]
        fresh = [key for key in wanted if key not in seen]
        seen.update(fresh)
        loads.append([c.start(*(right_blocks, left_blocks)[side][at]) for side, at in fresh])
    if fix is not None:
        wait_all(loads[0])
        loads[0] = []
        fix()
    mine = r["device"][0]
    block = d // 4 if tall else d // 16
    natural = s["gnat_tall" if tall and plan.halving else "gnat"]
    gout = s["gout_tall" if tall else "gout"] if plan.halving else None
    sems = c.reserve(4)

    def columns(at):
        return pl.ds(pl.multiple_of(at * d, LANES), d)

    def copies_out(t):
        slot = lax.rem(t, 2)
        found = []
        for sent in range(2 if plan.halving else 1):
            ref = r[name + ("_send" if sent else "")]
            if not plan.halving:
                target = ref.at[columns(t), :] if tall else ref.at[:, columns(t)]
                source = natural.at[slot]
            elif tall:
                away = t ^ (mine >> 2)
                target, source = ref.at[:, away & 1, away >> 1], gout.at[slot, sent]
            else:
                target, source = ref.at[:, :, columns(t)], gout.at[slot, sent]
            found.append(pltpu.make_async_copy(source, target, sems(slot * 2 + sent)))
        return found

    def wait_out(t):
        wait_all(copies_out(t))

    def hand_on(t):
        for one in copies_out(t):
            one.start()

    def arrange(slot):
        if tall:
            for relative in range(4):
                gout[slot, relative & 1, relative >> 1] = natural[slot, (mine & 3) ^ relative]
        else:
            for relative in range(16):
                gout[slot, relative & 1, slot_of(relative)] = natural[slot, mine ^ relative]

    behind = 1 if plan.halving else 0

    def step(t, carry):
        for at, found in enumerate(loads):
            if found:
                pl.when(t == at)(lambda found=found: wait_all(found))
        pl.when(t >= 2 + behind)(lambda: wait_out(t - 2 - behind))
        slot = lax.rem(t, 2)
        grad = s["gr"][:, columns(0 if tall else t)]
        low = dot_tn(s["gl"][:, columns(left_of(t))], grad).astype(BF)
        if plan.halving:
            for part in range(d // block):
                natural[slot, part] = low[part * block : (part + 1) * block]
            arrange(1 - slot)
        else:
            natural[slot] = low
        sums = jnp.sum(grad.astype(F32).reshape(total // 8, 8, d), axis=0)
        s["gsums"][:, columns(0 if tall else t)] = sums
        pl.when(t >= behind)(lambda: hand_on(t - behind))
        return carry

    lax.fori_loop(0, count, step, 0)
    if plan.halving:
        wait_out(count - 3)
        arrange((count - 1) % 2)
        hand_on(count - 1)
    breadth = len(right_blocks) * d
    last = c.start(s["gsums"].at[:, :breadth], r[name + "_sums"])
    wait_out(count - 2)
    wait_out(count - 1)
    last.wait()


def run_grads_cross(plan, r, s, c, k):
    weight_grads(
        plan, r, s, c, ("m", "streams", "co"), ("dcq", "dckv", "gaf"),
        lambda t: (t + 1) // 2, False, "cross",
    )


def run_grads_fc2(plan, r, s, c, k):
    last = plan.steps - 1
    arrive = c.start(r["returned"], s["gin"])

    def fix():
        arrive.wait()

        @pl.when(r["section"][0] == 0)
        def _():
            s["dn"][...] = s["gin"][...].astype(F32)
            fill_rows(s["g"], plan.per, plan.slots, r["counts"], last * plan.per, s["dn"])
            s["gr"][last * plan.rows :, : plan.width] = s["g"][...].astype(BF)

    weight_grads(plan, r, s, c, ("a",), ("gbr",), lambda t: t, True, "fc2", fix)


def run_grads_fc1(plan, r, s, c, k):
    weight_grads(plan, r, s, c, ("n2",), ("du",), lambda t: 0 * t, False, "fc1")


def run_grads_more(plan, r, s, c, k):
    run_grads_fc2(plan, r, s, c, k)
    run_grads_fc1(plan, r, s, c, k)


def run_grads_attn(plan, r, s, c, k):
    weight_grads(plan, r, s, c, ("n", "o"), ("dqkv", "gm"), lambda t: t // 3, False, "attn")
    d = plan.width
    first = sum(r[name][...] for name in r if name.startswith("ln_first"))
    second = sum(r[name][...] for name in r if name.startswith("ln_second"))
    norms = jnp.where(r["section"][0] == 0, first, second)
    ratio = plan.hidden // d

    def column(ref, at):
        return jnp.sum(ref[:, at * d : (at + 1) * d], axis=0, keepdims=True)

    rows = [column(s["gsums"], 0), column(s["gsums"], 2), column(s["gsums"], 3)]
    rows += [column(r["fc1_sums"], at) for at in range(ratio)] + [column(r["fc2_sums"], 0)]
    rows += [norms[0:1], norms[2:3], norms[1:2], norms[3:4], norms[4:5]]
    rows += [column(r["cross_sums"], at) for at in (0, 2, 3)] + [norms[5:6]]
    s["small"][...] = jnp.zeros_like(s["small"])
    for at, row in enumerate(rows):
        s["small"][at : at + 1, :] = row
    c.start(s["small"], r["small"]).wait()


RUN = {
    "forward": run_forward,
    "radar": run_radar,
    "merged": run_merged,
    "backward": run_backward,
    "backward_mlp": run_backward_mlp,
    "backward_self": run_backward_self,
    "radar_back": run_radar_back,
    "grads_cross": run_grads_cross,
    "grads_fc2": run_grads_fc2,
    "grads_fc1": run_grads_fc1,
    "grads_attn": run_grads_attn,
    "grads_more": run_grads_more,
}


def phase(plan, fixed, state, weights, first, second, after=()):
    jobs = [job for job in (first, second) if job is not None]
    shared = len(jobs) == 2 and jobs[0][0] == jobs[1][0]
    kinds = [JOBS[job[0]] for job in jobs]
    taken = {}
    for job in jobs:
        taken.update(job[2])
    writes = []
    for kind in kinds:
        writes += [name for name in kind["writes"] if name not in writes]
    reads = []
    for kind in kinds:
        for name in kind["reads"]:
            if name in state and name not in reads and name not in writes:
                reads.append(name)
            elif name in ("streams", "cotangent"):
                taken[name] = fixed[name]
    used = [name for name in WEIGHT_NAMES if any(name in kind["weights"] for kind in kinds)]
    fresh = [name for name in writes if name not in state or name in ("send", "ln")]
    kept = [name for name in writes if name not in fresh]
    small = [name for name in fixed if name not in ("streams", "cotangent")]
    if all(job[0].startswith("grads") for job in jobs):
        small = ["section", "device", "counts"]
    elif not any(job[0] in ("radar", "merged") for job in jobs):
        small = [name for name in small if not name.startswith("cross")]
    every = scratch_shapes(plan)
    need = list(used)
    for kind in kinds:
        need += [name for name in kind["scratch"] if name not in need]

    operands, specs, names = [], [], []
    for name in small:
        operands.append(fixed[name])
        specs.append(SM if name in ("section", "device", "counts", "radar_counts", "slopes") else VM)
        names.append(name)
    for name in used:
        operands.append(weights[name])
        specs.append(ANY)
        names.append(name)
    for name, array in list(taken.items()) + [(name, state[name]) for name in reads]:
        operands.append(array)
        specs.append(VM if name.startswith("ln_") or name.endswith("_sums") else ANY)
        names.append(name)
    operands += after
    specs += [ANY] * len(after)
    names += [None] * len(after)
    alias = {}
    for at, name in enumerate(kept):
        alias[len(operands)] = at
        operands.append(state[name])
        specs.append(ANY)
        names.append(None)
    outs = kept + fresh
    shapes = [jax.ShapeDtypeStruct(*STATE[name](plan)) for name in outs]

    def kernel(*refs):
        r, s = {}, {}
        for name, ref in zip(names, refs):
            if name is not None:
                r[name] = ref
        refs = refs[len(names) :]
        for name, ref in zip(outs, refs):
            r[name] = ref
        refs = refs[len(outs) :]
        for name, ref in zip(need, refs):
            s[name] = ref
        sems = refs[len(need)]
        if shared:
            RUN[first[0]](plan, r, s, Copies(sems), first[1])
            return
        for which, job in ((0, first), (1, second)):
            if job is not None:

                @pl.when(r["section"][0] == which)
                def _():
                    RUN[job[0]](plan, r, s, Copies(sems), job[1])

    results = pl.pallas_call(
        kernel,
        out_shape=shapes,
        in_specs=specs,
        out_specs=[ANY] * len(outs),
        scratch_shapes=[pltpu.VMEM(*every[name]) for name in need] + [pltpu.SemaphoreType.DMA((32,))],
        input_output_aliases=alias,
        compiler_params=pltpu.CompilerParams(vmem_limit_bytes=VMEM_LIMIT),
        cost_estimate=CHEAP,
        name="_".join(job[0] + str(job[1]) for job in jobs),
    )(*operands)
    new = dict(zip(outs, results))
    for name in outs:
        if name not in ("send", "ln"):
            state[name] = new[name]
    return new.get("send"), new.get("ln")


def body(
    streams,
    cotangent,
    counts,
    positions,
    radar_counts,
    radar_positions,
    qkv_weight,
    out_weight,
    fc1_weight,
    fc2_weight,
    attn_bias,
    mlp_bias,
    norm_gains,
    norm_shifts,
    cross_qkv_weight,
    cross_out_weight,
    cross_gain,
    cross_bias,
):
    devices = lax.axis_size("batch")
    section_id = lax.axis_index("section")
    me = lax.axis_index("batch")
    width = cotangent.shape[1]
    hidden = fc1_weight.shape[2]
    halving = devices == 16
    plan = Plan(counts.shape[0], positions.shape[1], width, hidden, halving)
    device = me.astype(jnp.int32).reshape(1)
    section = section_id.astype(jnp.int32).reshape(1)
    head_slopes = [2.0 ** (-8.0 * (head + 1.0) / H) for head in range(H)]
    fixed = {
        "section": section,
        "device": device,
        "counts": counts,
        "radar_counts": radar_counts,
        "slopes": jnp.array(head_slopes, F32),
        "positions": positions,
        "radar_positions": radar_positions,
        "attn_bias": attn_bias,
        "mlp_bias": mlp_bias,
        "gains": norm_gains,
        "shifts": norm_shifts,
        "cross_gain": cross_gain.reshape(1, width),
        "cross_bias": cross_bias.reshape(1, 4 * width),
        "streams": streams[0],
        "cotangent": cotangent,
    }
    weights = dict(
        zip(
            WEIGHT_NAMES,
            (
                qkv_weight[0],
                out_weight[0],
                fc1_weight[0],
                fc2_weight[0],
                cross_qkv_weight,
                cross_out_weight,
            ),
        )
    )
    state = {}
    steps = plan.steps
    arrived = []
    for k in range(steps):
        second = ("radar", 0, {}) if k == min(1, steps - 1) else None
        send, _ = phase(plan, fixed, state, weights, ("forward", k, {}), second)
        arrived.append(lax.ppermute(send, "section", [(0, 1)]))
    returned, first_sums, second_sums = [], [], []
    for k in range(steps):
        send, sums = phase(
            plan, fixed, state, weights, None, ("merged", k, {"received": arrived[k]})
        )
        second_sums.append(sums)
        returned.append(lax.ppermute(send, "section", [(1, 0)]))
        if 0 < k < steps - 1:
            _, sums = phase(
                plan, fixed, state, weights, ("backward", k - 1, {"returned": returned[k - 1]}), None
            )
            first_sums.append(sums)

    route = {bit: [(at, at ^ bit) for at in range(devices)] for bit in (1, 2, 4, 8)} if halving else {}

    def trade(block, bit):
        return lax.ppermute(block, "batch", route[bit])

    def trade_second(block, bit):
        pairs = [(devices + left, devices + right) for left, right in route[bit]]
        return lax.ppermute(block, ("section", "batch"), pairs)

    def scatter(part):
        return lax.psum_scatter(part, "batch", scatter_dimension=0, tiled=True).astype(F32)

    def run(first, second, after=()):
        _, sums = phase(plan, fixed, state, weights, first, second, after=list(after))
        if first is not None and first[0].startswith("backward"):
            first_sums.append(sums)

    def both(job, taken, after=()):
        run((job, 0, taken), (job, 0, taken), after)

    def add_up(parts, low, high):
        return sum(part[low:high].astype(F32) for part in parts)

    def begin(name, exchange, pieces=1):
        kept, sent = state[name], state[name + "_send"]
        kept, sent = (x.reshape(8, -1, x.shape[-1]) for x in (kept, sent))
        come = [exchange(piece, 1) for piece in jnp.split(sent, pieces)]
        return [kept, jnp.concatenate(come) if pieces > 1 else come[0]]

    def step(parts, exchange, bit):
        half = parts[-1].shape[0] // 2
        return parts + [exchange(add_up(parts, half, 2 * half).astype(BF), bit)]

    def total(parts):
        return add_up(parts, 0, 1)[0]

    def taken_sums():
        found = {"ln_first" + str(at): array for at, array in enumerate(first_sums)}
        return found | {"ln_second" + str(at): array for at, array in enumerate(second_sums)}

    def once(*arrays):
        return lax.optimization_barrier(arrays)

    last = steps - 1
    queue = [("backward", k, {"returned": returned[k]}) for k in range(max(last - 1, 0), last)] or [None]
    for job in queue[:-1]:
        run(job, None)
    run(queue[-1], ("grads_cross", 0, {}))
    if halving:
        state["cross_send"], returned[last] = once(state["cross_send"], returned[last])
        cross = step(begin("cross", trade_second), trade_second, 2)
        taken = {"returned": returned[last]}
        run(("grads_fc2", 0, taken), ("grads_more", 0, taken), [cross[1]])
        state["fc2"], state["fc2_send"], cross[-1] = once(
            state["fc2"], state["fc2_send"], cross[-1]
        )
        fc2 = begin("fc2", trade)
        ahead = add_up(fc2, 4, 8).astype(BF)
        cross[-1], ahead = once(cross[-1], ahead)
        fc2.append(trade(ahead, 2))
        cross = step(cross, trade_second, 4)
        run(("backward_mlp", last, taken), None, [cross[-1]])
        run(("grads_fc1", 0, {}), None)
        cross = step(cross, trade_second, 8)
        state["fc1"], state["fc1_send"], fc2[-1] = once(
            state["fc1"], state["fc1_send"], fc2[-1]
        )
        fc1 = begin("fc1", trade)
        fc2 = step(fc2, trade, 4)
        run(("backward_self", last, {}), None, [fc1[-1]])
        fc1 = step(fc1, trade, 2)
        both("grads_attn", taken_sums())
        state["attn"], state["attn_send"], fc1[-1], fc2[-1], cross[-1] = once(
            state["attn"], state["attn_send"], fc1[-1], fc2[-1], cross[-1]
        )
        cross_share = total(cross)
        fc2 = step(fc2, trade, 8)
        attn = begin("attn", trade)
        attn[-1], fc2[-1] = once(attn[-1], fc2[-1])
        grad_fc2 = total(fc2)
        ahead = add_up(attn, 4, 8).astype(BF)
        ahead, fc1[-1] = once(ahead, fc1[-1])
        attn.append(trade(ahead, 2))
        fc1 = step(fc1, trade, 4)
        small, _ = once(state["small"], ahead)
        small = small + trade(small, 1)
        small = small + trade(small, 2)
        run(None, ("radar_back", 0, {}), [small])
        fc1 = step(fc1, trade, 8)
        attn[-1], fc1[-1], state["input_grads"] = once(attn[-1], fc1[-1], state["input_grads"])
        ahead = add_up(attn, 2, 4).astype(BF)
        ahead, fc1[-1], small, cross_share = once(ahead, fc1[-1], small, cross_share)
        attn.append(trade(ahead, 4))
        grad_fc1 = total(fc1)
        small = small + trade(small, 4)
        small = small + trade(small, 8)
        ahead = add_up(attn, 1, 2).astype(BF)
        ahead, small, cross_share = once(ahead, small, cross_share)
        attn.append(trade(ahead, 8))
        grad_attn = total(attn)
    else:
        both("grads_fc2", {"returned": returned[last]})
        run(("backward_mlp", last, {"returned": returned[last]}), None)
        both("grads_fc1", {})
        run(("backward_self", last, {}), None)
        both("grads_attn", taken_sums())
        small = lax.psum(state["small"], "batch")
        run(None, ("radar_back", 0, {}))
        cross_share, grad_fc2, grad_fc1, grad_attn = (
            scatter(state[name]) for name in ("cross", "fc2", "fc1", "attn")
        )
    split = qkv_weight.shape[2]

    is_first = section_id == 0

    def to_both(block):
        return jnp.where(is_first, lax.ppermute(block, "section", [(1, 0)]), block).astype(F32)

    cross_all = to_both(cross_share.astype(BF))
    ratio = hidden // width
    edges = [0, 3, 4 + ratio, 6 + ratio, 8 + ratio, 9 + ratio, 13 + ratio]
    cross_small = to_both(small[edges[4] : edges[6]])
    parts = []
    for low, high in zip(edges, edges[1:]):
        rows = small[low:high] if high <= edges[4] else cross_small[low - edges[4] : high - edges[4]]
        size = (high - low) * width // devices
        parts.append(lax.dynamic_slice(rows.reshape(-1), (me * size,), (size,)))
    return (
        state["layer_out"][None],
        state["input_grads"][None],
        grad_attn[None, :, :split],
        grad_attn[None, :, split:],
        grad_fc1[None],
        grad_fc2[None],
        parts[0][None],
        parts[1][None],
        parts[2][None],
        parts[3][None],
        cross_all[:, :split],
        cross_all[:, split:],
        parts[4],
        parts[5],
    )


def solution(mesh):
    in_specs = (
        P("section", "batch", None),
        P("batch", None),
        P("batch"),
        P("batch", None),
        P("batch"),
        P("batch", None),
        P("section", None, None),
        P("section", None, None),
        P("section", None, None),
        P("section", None, None),
        P("section", None),
        P("section", None),
        P("section", None),
        P("section", None),
        P(),
        P(),
        P(),
        P(),
    )
    out_specs = (
        P("section", "batch", None),
        P("section", "batch", None),
        P("section", "batch", None),
        P("section", "batch", None),
        P("section", "batch", None),
        P("section", "batch", None),
        P("section", "batch"),
        P("section", "batch"),
        P("section", "batch"),
        P("section", "batch"),
        P("batch", None),
        P("batch", None),
        P("batch"),
        P("batch"),
    )
    return jax.shard_map(body, mesh=mesh, in_specs=in_specs, out_specs=out_specs, check_vma=False)
```

```python
import enum
import typing

import jax
import jax.numpy as jnp
from jax import lax
from jax.experimental import pallas as pl
from jax.experimental.pallas import tpu as pltpu
from jax.sharding import PartitionSpec as P

SECTION, BATCH = "section", "batch"
H = 12
HD = 64
PAIRS = H // 2
LANES = 2 * HD
GRID = 15
SCORE_SCALE = 0.125
NORM_EPS = 1e-06
FAR = 1e33
CHUNK = 16
BF = jnp.bfloat16
F32 = jnp.float32
VMEM_LIMIT = 60 << 20
CHEAP = pl.CostEstimate(flops=1, bytes_accessed=1, transcendentals=0)
ANY = pl.BlockSpec(memory_space=pl.ANY)
VM = pl.BlockSpec(memory_space=pltpu.VMEM)
SM = pl.BlockSpec(memory_space=pltpu.SMEM)


class K(enum.Enum):
    a = enum.auto()
    attn = enum.auto()
    attn_bias = enum.auto()
    attn_send = enum.auto()
    attn_sums = enum.auto()
    backward = enum.auto()
    backward_mlp = enum.auto()
    backward_self = enum.auto()
    between = enum.auto()
    cdist = enum.auto()
    cgo = enum.auto()
    cheard = enum.auto()
    ckv = enum.auto()
    ckvb = enum.auto()
    co = enum.auto()
    cotangent = enum.auto()
    counts = enum.auto()
    cp = enum.auto()
    cq = enum.auto()
    cross = enum.auto()
    cross_bias = enum.auto()
    cross_gain = enum.auto()
    cross_send = enum.auto()
    cross_sums = enum.auto()
    dckv = enum.auto()
    dcq = enum.auto()
    dcqkv = enum.auto()
    device = enum.auto()
    dh = enum.auto()
    dist = enum.auto()
    dm = enum.auto()
    dmid = enum.auto()
    dn = enum.auto()
    dqkv = enum.auto()
    dqkvb = enum.auto()
    du = enum.auto()
    dx = enum.auto()
    dxb = enum.auto()
    fc1 = enum.auto()
    fc1_send = enum.auto()
    fc1_sums = enum.auto()
    fc2 = enum.auto()
    fc2_send = enum.auto()
    fc2_sums = enum.auto()
    forward = enum.auto()
    g = enum.auto()
    gaf = enum.auto()
    gains = enum.auto()
    gbr = enum.auto()
    gin = enum.auto()
    gl = enum.auto()
    gm = enum.auto()
    gnat = enum.auto()
    gnat_tall = enum.auto()
    go = enum.auto()
    gout = enum.auto()
    gout_tall = enum.auto()
    gp = enum.auto()
    gr = enum.auto()
    grads_attn = enum.auto()
    grads_cross = enum.auto()
    grads_fc1 = enum.auto()
    grads_fc2 = enum.auto()
    grads_more = enum.auto()
    gsums = enum.auto()
    h = enum.auto()
    h2 = enum.auto()
    heard = enum.auto()
    input_grads = enum.auto()
    layer_out = enum.auto()
    ln = enum.auto()
    m = enum.auto()
    merged = enum.auto()
    mlp_bias = enum.auto()
    n = enum.auto()
    n2 = enum.auto()
    o = enum.auto()
    p = enum.auto()
    positions = enum.auto()
    qkv = enum.auto()
    radar = enum.auto()
    radar_back = enum.auto()
    radar_counts = enum.auto()
    radar_positions = enum.auto()
    rb = enum.auto()
    rdr = enum.auto()
    received = enum.auto()
    returned = enum.auto()
    rkv = enum.auto()
    section = enum.auto()
    send = enum.auto()
    shifts = enum.auto()
    slopes = enum.auto()
    small = enum.auto()
    streams = enum.auto()
    u = enum.auto()
    wcout = enum.auto()
    wcqkv = enum.auto()
    wfc1 = enum.auto()
    wfc2 = enum.auto()
    wout = enum.auto()
    wqkv = enum.auto()
    x = enum.auto()
    xb = enum.auto()
    y = enum.auto()
    yout = enum.auto()
    ysend = enum.auto()


SENT = {K.cross: K.cross_send, K.fc2: K.fc2_send, K.fc1: K.fc1_send, K.attn: K.attn_send}
SUMS = {K.cross: K.cross_sums, K.fc2: K.fc2_sums, K.fc1: K.fc1_sums, K.attn: K.attn_sums}
FIRST = [(K.ln, 0, at) for at in range(64)]
SECOND = [(K.ln, 1, at) for at in range(64)]
IN_VMEM = FIRST + SECOND + list(SUMS.values())
GRAD_JOBS = (K.grads_cross, K.grads_fc2, K.grads_fc1, K.grads_attn, K.grads_more)
BACK_JOBS = (K.backward, K.backward_mlp, K.backward_self)


class Job(typing.NamedTuple):
    reads: tuple
    writes: tuple
    weights: tuple
    scratch: tuple


def dot_nn(left, right):
    return jnp.dot(left, right, preferred_element_type=F32)


def dot_tn(left, right):
    return lax.dot_general(left, right, (((0,), (0,)), ((), ())), preferred_element_type=F32)


def dot_nt(left, right):
    return lax.dot_general(left, right, (((1,), (1,)), ((), ())), preferred_element_type=F32)


class Copies:
    def __init__(self, sems):
        self.sems = sems
        self.used = 0

    def start(self, source, target):
        copy = pltpu.make_async_copy(source, target, self.sems.at[self.used])
        self.used += 1
        copy.start()
        return copy

    def reserve(self, count):
        first = self.used
        self.used += count
        return lambda at: self.sems.at[first + at]


def spans(rows):
    return [slice(at, at + CHUNK) for at in range(0, rows, CHUNK)]


def norm_parts(values):
    average = jnp.mean(values, axis=-1, keepdims=True)
    centred = values - average
    spread = jnp.mean(centred * centred, axis=-1, keepdims=True)
    scale = lax.rsqrt(spread + NORM_EPS)
    return centred * scale, scale


def norm_forward(source, gain, shift, target):
    for span in spans(source.shape[0]):
        unit, _ = norm_parts(source[span, :])
        target[span, :] = (unit * gain + shift).astype(BF)


def norm_backward(source, gain, upstream, residual, target):
    gain_sum = jnp.zeros((8, source.shape[1]), F32)
    shift_sum = jnp.zeros((8, source.shape[1]), F32)
    for span in spans(source.shape[0]):
        unit, scale = norm_parts(source[span, :])
        grad = upstream[span, :]
        product = grad * unit
        gain_sum = gain_sum + product[:8] + product[8:]
        shift_sum = shift_sum + grad[:8] + grad[8:]
        inner = grad * gain
        mean_one = jnp.mean(inner, axis=-1, keepdims=True)
        mean_two = jnp.mean(inner * unit, axis=-1, keepdims=True)
        target[span, :] = residual[span, :] + scale * (inner - mean_one - unit * mean_two)
    return (
        jnp.sum(gain_sum, axis=0, keepdims=True),
        jnp.sum(shift_sum, axis=0, keepdims=True),
    )


def gelu_both(values):
    cdf = 0.5 + 0.5 * lax.erf(values * 0.7071067811865476)
    density = 0.3989422804014327 * jnp.exp(-0.5 * values * values)
    return values * cdf, cdf + values * density


def place(positions):
    values = positions
    row = jnp.floor((values + 0.5) * (1.0 / GRID))
    return row, values - GRID * row


def distances(key_col, query_row, live_keys):
    row_q, col_q = place(query_row)
    row_k, col_k = place(key_col)
    gap_row = row_q - row_k
    gap_col = col_q - col_k
    distance = jnp.sqrt(gap_row * gap_row + gap_col * gap_col)
    slot = lax.broadcasted_iota(jnp.int32, distance.shape, 0)
    return jnp.where(slot < live_keys, distance, FAR)


def both_heads(pair):
    first = lax.broadcasted_iota(jnp.int32, pair.shape, 1) < HD
    zero = jnp.zeros_like(pair)
    return jnp.concatenate([jnp.where(first, pair, zero), jnp.where(first, zero, pair)], axis=0)


def one_pair(stacked):
    half = stacked.shape[0] // 2
    first = lax.broadcasted_iota(jnp.int32, (half, LANES), 1) < HD
    return jnp.where(first, stacked[:half], stacked[half:])


def by_size(plan, most_live, work):
    def step(image, carry):
        if plan.slots <= LANES:
            work(image, plan.slots)
        else:
            live = most_live(image)

            @pl.when(live <= LANES)
            def _():
                work(image, LANES)

            @pl.when(live > LANES)
            def _():
                work(image, plan.slots)

        return carry

    lax.fori_loop(0, plan.per, step, 0)


def rows_of(plan, image, first, size):
    return pl.ds(pl.multiple_of(image * plan.slots + first, 8), size)


def pair_lanes(base, pair):
    if isinstance(pair, int):
        return pl.ds(base + pair * LANES, LANES)
    return pl.ds(pl.multiple_of(base + pair * LANES, LANES), LANES)


def over_pairs(plan, work, size):
    unroll = PAIRS if size <= LANES else plan.unroll

    def step(at, carry):
        for part in range(unroll):
            work(at * unroll + part)
        return carry

    if unroll == PAIRS:
        step(0, 0)
    else:
        lax.fori_loop(0, PAIRS // unroll, step, 0)


def attend(plan, most_live, query, keys, values, spread, slopes, heard, weights):
    def work(image, size):
        rows = rows_of(plan, image, 0, size)
        if size < plan.slots:
            rest = rows_of(plan, image, size, plan.slots - size)
            heard[rest, :] = jnp.zeros((plan.slots - size, plan.width), F32)
        spread(image, size)
        gap_ref = spread.target

        def one(pair):
            q = both_heads(query[0][rows, pair_lanes(query[1], pair)]).astype(BF)
            k = keys[0][rows, pair_lanes(keys[1], pair)].astype(BF)
            v = values[0][rows, pair_lanes(values[1], pair)].astype(BF)
            first = lax.broadcasted_iota(jnp.int32, (1, 2 * size), 1) < size
            slope = jnp.where(first, slopes[2 * pair], slopes[2 * pair + 1])
            scores = dot_nt(k, q) - slope * gap_ref[image, :size, : 2 * size]
            scores = jnp.exp(scores - jnp.max(scores, axis=0, keepdims=True))
            totals = jnp.sum(scores, axis=0, keepdims=True)
            p = (scores * (1.0 / totals)).astype(BF)
            weights[image * PAIRS + pair, :size, : 2 * size] = p
            heard[rows, pair_lanes(0, pair)] = one_pair(dot_tn(p, v))

        over_pairs(plan, one, size)

    by_size(plan, most_live, work)


def attend_back(plan, most_live, query, keys, values, grad_heard, weights, grads):
    grad_q, grad_k, grad_v = grads

    def work(image, size):
        rows = rows_of(plan, image, 0, size)
        if size < plan.slots:
            rest = rows_of(plan, image, size, plan.slots - size)
            for ref, offset in grads:
                ref[rest, offset : offset + plan.width] = jnp.zeros((plan.slots - size, plan.width), F32)

        def one(pair):
            q = both_heads(query[0][rows, pair_lanes(query[1], pair)]).astype(BF)
            k = keys[0][rows, pair_lanes(keys[1], pair)].astype(BF)
            v = values[0][rows, pair_lanes(values[1], pair)].astype(BF)
            g = both_heads(grad_heard[rows, pair_lanes(0, pair)]).astype(BF)
            p = weights[image * PAIRS + pair, :size, : 2 * size]
            wide = p.astype(F32)
            product = dot_nt(v, g) * wide
            grad_s = (product - wide * jnp.sum(product, axis=0, keepdims=True)).astype(BF)
            grad_v[0][rows, pair_lanes(grad_v[1], pair)] = dot_nn(p, g)
            grad_k[0][rows, pair_lanes(grad_k[1], pair)] = dot_nn(grad_s, q)
            grad_q[0][rows, pair_lanes(grad_q[1], pair)] = one_pair(dot_tn(grad_s, k)) * SCORE_SCALE

        over_pairs(plan, one, size)

    by_size(plan, most_live, work)


def columns_of(positions):
    images = positions.shape[0]
    low = positions.astype(F32).astype(BF)
    row = lax.broadcasted_iota(jnp.int32, (images, LANES), 0)
    lane = lax.broadcasted_iota(jnp.int32, (images, LANES), 1)
    return dot_tn(low, (row == lane).astype(F32).astype(BF))


def twice(positions, size):
    slots = positions.shape[1]
    low = positions.astype(F32).astype(BF)
    row = lax.broadcasted_iota(jnp.int32, (slots, 2 * size), 0)
    lane = lax.broadcasted_iota(jnp.int32, (slots, 2 * size), 1)
    from_slot = jnp.where(lane < size, lane, lane - size)
    return dot_nn(low, (row == from_slot).astype(F32).astype(BF))


class Spread:
    def __init__(self, plan, r, target, k, key_positions, key_count):
        self.plan, self.r, self.target, self.k = plan, r, target, k
        self.key_positions, self.key_count = key_positions, key_count

    def __call__(self, image, size):
        at = self.k * self.plan.per + image
        query = twice(self.r[K.positions][pl.ds(at, 1), :], size)
        keys = columns_of(self.r[self.key_positions][pl.ds(at, 1), :])
        self.target[image, :size, : 2 * size] = distances(
            keys[:size, :1], query, self.r[self.key_count][at]
        )


def most_live(plan, r, k, names):
    def live(image):
        found = r[names[0]][k * plan.per + image]
        for name in names[1:]:
            found = jnp.maximum(found, r[name][k * plan.per + image])
        return found

    return live


def fill_rows(target, images, slots, counts, first_image, source):
    for image in range(images):
        live = counts[first_image + image]
        for at in range(0, slots, 8):
            span = slice(image * slots + at, image * slots + at + 8)
            row = at + lax.broadcasted_iota(jnp.int32, (8, source.shape[1]), 0)
            target[span, :] = jnp.where(row < live, source[span, :], 0.0)


class Plan:
    def __init__(self, batches, slots, width, hidden, halving, unroll=1):
        self.batches, self.slots, self.width, self.hidden = batches, slots, width, hidden
        self.halving = halving
        self.unroll = unroll
        self.per = 2 if batches % 2 == 0 else 1
        self.steps = batches // self.per
        self.rows = self.per * slots
        self.total = batches * slots

    def unrolled(self, unroll):
        return Plan(self.batches, self.slots, self.width, self.hidden, self.halving, unroll)


def small_shape(plan):
    rows = 13 + plan.hidden // plan.width
    return (-(-rows // 8) * 8, plan.width)


WEIGHT_NAMES = (K.wqkv, K.wout, K.wfc1, K.wfc2, K.wcqkv, K.wcout)


def scratch_shapes(plan):
    r, d, f = plan.rows, plan.width, plan.hidden
    w = {
        K.wqkv: ((d, 3 * d), BF),
        K.wout: ((d, d), BF),
        K.wfc1: ((d, f), BF),
        K.wfc2: ((f, d), BF),
        K.wcqkv: ((d, 3 * d), BF),
        K.wcout: ((d, d), BF),
        K.xb: ((r, d), BF),
        K.x: ((r, d), F32),
        K.n: ((r, d), BF),
        K.qkv: ((r, 3 * d), F32),
        K.p: ((plan.per * PAIRS, plan.slots, 2 * plan.slots), BF),
        K.dist: ((plan.per, plan.slots, 2 * plan.slots), F32),
        K.heard: ((r, d), F32),
        K.o: ((r, d), BF),
        K.h: ((r, d), F32),
        K.n2: ((r, d), BF),
        K.u: ((r, f), F32),
        K.a: ((r, f), BF),
        K.gp: ((r, f), BF),
        K.y: ((r, d), F32),
        K.yout: ((r, d), F32),
        K.ysend: ((r, d), BF),
        K.gin: ((r, d), BF),
        K.g: ((r, d), F32),
        K.gbr: ((r, d), BF),
        K.du: ((r, f), BF),
        K.dn: ((r, d), F32),
        K.dh: ((r, d), F32),
        K.gm: ((r, d), BF),
        K.go: ((r, d), F32),
        K.dqkv: ((r, 3 * d), F32),
        K.dqkvb: ((r, 3 * d), BF),
        K.dx: ((r, d), F32),
        K.dxb: ((r, d), BF),
        K.ln: ((8, d), F32),
        K.cdist: ((plan.per, plan.slots, 2 * plan.slots), F32),
        K.m: ((r, d), BF),
        K.cq: ((r, d), F32),
        K.ckvb: ((r, 2 * d), BF),
        K.ckv: ((r, 2 * d), F32),
        K.cp: ((plan.per * PAIRS, plan.slots, 2 * plan.slots), BF),
        K.cheard: ((r, d), F32),
        K.co: ((r, d), BF),
        K.h2: ((r, d), F32),
        K.gaf: ((r, d), BF),
        K.cgo: ((r, d), F32),
        K.dcqkv: ((r, 3 * d), F32),
        K.dcq: ((r, d), BF),
        K.dckv: ((r, 2 * d), BF),
        K.dm: ((r, d), F32),
        K.dmid: ((r, d), F32),
        K.gl: ((plan.total, f), BF),
        K.gr: ((plan.total, f), BF),
        K.gsums: ((8, f), F32),
        K.small: (small_shape(plan), F32),
        K.gnat: ((2, 16, d // 16, d) if plan.halving else (2, d, d), BF),
        K.gnat_tall: ((2, 4, d // 4, d), BF),
        K.gout: ((2, 2, 8, d // 16, d), BF),
        K.gout_tall: ((2, 2, 2, d // 4, d), BF),
        K.rdr: ((plan.total, d), F32),
        K.rb: ((plan.total, d), BF),
        K.rkv: ((plan.total, 2 * d), BF),
    }
    return w


def chunk_shape(plan, height, breadth):
    if not plan.halving:
        return (height, breadth), BF
    if height == plan.width:
        return (8, height // 16, breadth), BF
    return (2, 2, 2, height // 16, breadth), BF


def chunk_state(name, height, breadth):
    def size(plan, amount):
        return plan.hidden if amount is None else amount * plan.width

    def main(plan):
        return chunk_shape(plan, size(plan, height), size(plan, breadth))

    def sums(plan):
        return (8, size(plan, breadth)), F32

    return {name: main, SENT[name]: main, SUMS[name]: sums}


STATE = {
    K.n: lambda p: ((p.total, p.width), BF),
    K.o: lambda p: ((p.total, p.width), BF),
    K.n2: lambda p: ((p.total, p.width), BF),
    K.a: lambda p: ((p.total, p.hidden), BF),
    K.layer_out: lambda p: ((p.total, p.width), F32),
    K.qkv: lambda p: ((p.total, 3 * p.width), F32),
    K.p: lambda p: ((p.batches * PAIRS, p.slots, 2 * p.slots), BF),
    K.h: lambda p: ((p.total, p.width), F32),
    K.gp: lambda p: ((p.total, p.hidden), BF),
    K.ckv: lambda p: ((p.total, 2 * p.width), BF),
    K.gbr: lambda p: ((p.total, p.width), BF),
    K.du: lambda p: ((p.total, p.hidden), BF),
    K.gm: lambda p: ((p.total, p.width), BF),
    K.dqkv: lambda p: ((p.total, 3 * p.width), BF),
    K.input_grads: lambda p: ((p.total, p.width), F32),
    K.m: lambda p: ((p.total, p.width), BF),
    K.co: lambda p: ((p.total, p.width), BF),
    K.gaf: lambda p: ((p.total, p.width), BF),
    K.dcq: lambda p: ((p.total, p.width), BF),
    K.dckv: lambda p: ((p.total, 2 * p.width), BF),
    K.between: lambda p: ((p.rows, p.width), F32),
    K.send: lambda p: ((p.rows, p.width), BF),
    K.ln: lambda p: ((8, p.width), F32),
    K.small: lambda p: (small_shape(p), F32),
    **chunk_state(K.cross, 1, 4),
    **chunk_state(K.fc2, None, 1),
    **chunk_state(K.fc1, 1, None),
    **chunk_state(K.attn, 1, 4),
}

FORWARD_0 = Job(
    reads=(K.streams,),
    writes=(K.n, K.o, K.n2, K.a, K.layer_out, K.qkv, K.p, K.h, K.gp, K.send),
    weights=(K.wqkv, K.wout, K.wfc1, K.wfc2),
    scratch=(K.xb, K.x, K.n, K.qkv, K.p, K.dist, K.heard, K.o, K.h, K.n2, K.u, K.a, K.gp, K.y, K.yout, K.ysend),
)
RADAR = Job(reads=(K.streams,), writes=(K.ckv,), weights=(K.wcqkv,), scratch=[K.rb, K.rkv])
MERGED = Job(
    reads=(K.received, K.cotangent, K.ckv),
    writes=(K.n, K.o, K.n2, K.a, K.layer_out, K.gbr, K.du, K.gm, K.dqkv, K.m, K.co, K.gaf, K.dcq, K.dckv, K.send, K.ln),
    weights=WEIGHT_NAMES,
    scratch=(K.xb, K.x, K.n, K.qkv, K.p, K.dist, K.heard, K.o, K.h, K.n2, K.u, K.a, K.gp, K.y, K.yout, K.gin, K.g, K.gbr, K.du, K.dn, K.dh, K.gm, K.go, K.dqkv, K.dqkvb, K.dxb, K.ln, K.cdist, K.m, K.cq, K.ckvb, K.ckv, K.cp, K.cheard, K.co, K.h2, K.gaf, K.cgo, K.dcqkv, K.dcq, K.dckv, K.dm, K.dmid,),
)
BACKWARD_0 = Job(
    reads=(K.streams, K.returned, K.qkv, K.p, K.h, K.gp),
    writes=(K.gbr, K.du, K.gm, K.dqkv, K.input_grads, K.ln),
    weights=(K.wfc2, K.wfc1, K.wout, K.wqkv),
    scratch=(K.xb, K.x, K.qkv, K.p, K.h, K.gp, K.gin, K.g, K.gbr, K.du, K.dn, K.dh, K.gm, K.go, K.dqkv, K.dqkvb, K.dx, K.ln),
)
BACKWARD_MLP = Job(
    reads=(K.returned, K.gp, K.h),
    writes=(K.du, K.between, K.ln),
    weights=(K.wfc2, K.wfc1),
    scratch=(K.h, K.gp, K.gin, K.g, K.gbr, K.du, K.dn, K.dh, K.ln),
)
BACKWARD_SELF = Job(
    reads=(K.between, K.streams, K.qkv, K.p),
    writes=(K.gm, K.dqkv, K.input_grads, K.ln),
    weights=(K.wout, K.wqkv),
    scratch=(K.xb, K.x, K.qkv, K.p, K.dn, K.dh, K.gm, K.go, K.dqkv, K.dqkvb, K.dx, K.ln),
)
RADAR_BACK = Job(
    reads=(K.dckv,), writes=(K.input_grads,), weights=(K.wcqkv,), scratch=(K.rkv, K.rdr)
)
GRAD_SCRATCH = (K.gl, K.gr, K.gnat, K.gout, K.gsums)
GRADS_CROSS = Job(
    reads=(K.m, K.streams, K.co, K.dcq, K.dckv, K.gaf),
    writes=(K.cross, K.cross_send, K.cross_sums),
    weights=(),
    scratch=GRAD_SCRATCH,
)
GRADS_FC2 = Job(
    reads=(K.a, K.gbr, K.returned),
    writes=(K.fc2, K.fc2_send, K.fc2_sums),
    weights=(),
    scratch=(K.gl, K.gr, K.gnat, K.gnat_tall, K.gout_tall, K.gsums, K.gin, K.dn, K.g),
)
GRADS_FC1 = Job(
    reads=(K.n2, K.du), writes=(K.fc1, K.fc1_send, K.fc1_sums), weights=(), scratch=GRAD_SCRATCH
)
GRADS_ATTN = Job(
    reads=(K.n, K.o, K.dqkv, K.gm, K.fc1_sums, K.fc2_sums, K.cross_sums),
    writes=(K.attn, K.attn_send, K.attn_sums, K.small),
    weights=(),
    scratch=GRAD_SCRATCH + (K.small,),
)
GRADS_MORE = Job(*(tuple(dict.fromkeys(one + two)) for one, two in zip(GRADS_FC2, GRADS_FC1)))
JOBS = {
    K.forward: FORWARD_0,
    K.radar: RADAR,
    K.merged: MERGED,
    K.backward: BACKWARD_0,
    K.backward_mlp: BACKWARD_MLP,
    K.backward_self: BACKWARD_SELF,
    K.radar_back: RADAR_BACK,
    K.grads_cross: GRADS_CROSS,
    K.grads_fc2: GRADS_FC2,
    K.grads_fc1: GRADS_FC1,
    K.grads_attn: GRADS_ATTN,
    K.grads_more: GRADS_MORE,
}
TILE = 768


def tiles(extent, tile=TILE):
    return [slice(at, min(at + tile, extent)) for at in range(0, extent, tile)]


def self_forward(plan, r, s, c, k, waits, save):
    d = plan.width
    rows = pl.ds(k * plan.rows, plan.rows)
    out = []
    gain, shift, bias = r[K.gains], r[K.shifts], r[K.attn_bias]
    norm_forward(s[K.x], gain[:, :d], shift[:, :d], s[K.n])
    out.append(c.start(s[K.n], r[K.n].at[rows]))
    waits[K.wqkv].wait()
    normed = s[K.n][...]
    s[K.qkv][:, :d] = (dot_nn(normed, s[K.wqkv][:, :d]) + bias[:, :d]).astype(BF).astype(F32) * SCORE_SCALE
    s[K.qkv][:, d : 2 * d] = dot_nn(normed, s[K.wqkv][:, d : 2 * d])
    s[K.qkv][:, 2 * d :] = dot_nn(normed, s[K.wqkv][:, 2 * d :]) + bias[:, d : 2 * d]
    if save:
        out.append(c.start(s[K.qkv], r[K.qkv].at[rows]))
    attend(
        plan,
        most_live(plan, r, k, (K.counts,)),
        (s[K.qkv], 0),
        (s[K.qkv], d),
        (s[K.qkv], 2 * d),
        Spread(plan, r, s[K.dist], k, K.positions, K.counts),
        r[K.slopes],
        s[K.heard],
        s[K.p],
    )
    if save:
        out.append(c.start(s[K.p], r[K.p].at[pl.ds(k * plan.per * PAIRS, plan.per * PAIRS)]))
    s[K.o][...] = s[K.heard][...].astype(BF)
    out.append(c.start(s[K.o], r[K.o].at[rows]))
    waits[K.wout].wait()
    s[K.h][...] = s[K.x][...] + dot_nn(s[K.o][...], s[K.wout][...]) + bias[:, 2 * d :]
    if save:
        out.append(c.start(s[K.h], r[K.h].at[rows]))
    return out


def mlp_forward(plan, r, s, c, k, waits, after, save):
    d, f = plan.width, plan.hidden
    rows = pl.ds(k * plan.rows, plan.rows)
    out = []
    norm_forward(after, r[K.gains][:, d:], r[K.shifts][:, d:], s[K.n2])
    out.append(c.start(s[K.n2], r[K.n2].at[rows]))
    waits[K.wfc1].wait()
    bias = r[K.mlp_bias]
    for tile in tiles(f):
        s[K.u][:, tile] = dot_nn(s[K.n2][...], s[K.wfc1][:, tile]) + bias[:, tile]
        for span in spans(plan.rows):
            active, slope = gelu_both(s[K.u][span, tile])
            s[K.a][span, tile] = active.astype(BF)
            s[K.gp][span, tile] = slope.astype(BF)
    out.append(c.start(s[K.a], r[K.a].at[rows]))
    if save:
        out.append(c.start(s[K.gp], r[K.gp].at[rows]))
    waits[K.wfc2].wait()
    s[K.y][...] = after[...] + dot_nn(s[K.a][...], s[K.wfc2][...]) + bias[:, f:]
    fill_rows(s[K.yout], plan.per, plan.slots, r[K.counts], k * plan.per, s[K.y])
    out.append(c.start(s[K.yout], r[K.layer_out].at[rows]))
    return out


def mlp_backward(plan, r, s, c, k, waits, after, target):
    d, f = plan.width, plan.hidden
    rows = pl.ds(k * plan.rows, plan.rows)
    out = []
    s[K.dn][...] = s[K.gin][...].astype(F32)
    fill_rows(s[K.g], plan.per, plan.slots, r[K.counts], k * plan.per, s[K.dn])
    s[K.gbr][...] = s[K.g][...].astype(BF)
    if K.gbr in r:
        out.append(c.start(s[K.gbr], r[K.gbr].at[rows]))
    if K.wfc2 in waits:
        waits[K.wfc2].wait()
    for tile in tiles(f):
        grad = dot_nt(s[K.gbr][...], s[K.wfc2][tile, :])
        s[K.du][:, tile] = (grad * s[K.gp][:, tile].astype(F32)).astype(BF)
    out.append(c.start(s[K.du], r[K.du].at[rows]))
    if K.wfc1 in waits:
        waits[K.wfc1].wait()
    s[K.dn][...] = dot_nt(s[K.du][...], s[K.wfc1][...])
    sums = norm_backward(after, r[K.gains][:, d:], s[K.dn], s[K.g], target)
    return out, sums


def self_backward(plan, r, s, c, k, waits, grad, target):
    d = plan.width
    rows = pl.ds(k * plan.rows, plan.rows)
    out = []
    s[K.gm][...] = grad[...].astype(BF)
    out.append(c.start(s[K.gm], r[K.gm].at[rows]))
    if K.wout in waits:
        waits[K.wout].wait()
    s[K.go][...] = dot_nt(s[K.gm][...], s[K.wout][...])
    attend_back(
        plan,
        most_live(plan, r, k, (K.counts,)),
        (s[K.qkv], 0),
        (s[K.qkv], d),
        (s[K.qkv], 2 * d),
        s[K.go],
        s[K.p],
        [(s[K.dqkv], part * d) for part in range(3)],
    )
    s[K.dqkvb][...] = s[K.dqkv][...].astype(BF)
    out.append(c.start(s[K.dqkvb], r[K.dqkv].at[rows]))
    if K.wqkv in waits:
        waits[K.wqkv].wait()
    s[K.dn][...] = dot_nt(s[K.dqkvb][...], s[K.wqkv][...])
    sums = norm_backward(s[K.x], r[K.gains][:, :d], s[K.dn], grad, target)
    return out, sums


def write_sums(s, c, r, parts):
    s[K.ln][...] = jnp.zeros_like(s[K.ln])
    for at, part in enumerate(parts):
        s[K.ln][at : at + 1, :] = part
    return c.start(s[K.ln], r[K.ln])


def start_weights(r, s, c, names):
    return {name: c.start(r[name], s[name]) for name in names}


def run_forward(plan, r, s, c, k):
    rows = pl.ds(k * plan.rows, plan.rows)
    arrive = c.start(r[K.streams].at[rows], s[K.xb])
    waits = start_weights(r, s, c, FORWARD_0.weights)
    arrive.wait()
    s[K.x][...] = s[K.xb][...].astype(F32)
    out = self_forward(plan, r, s, c, k, waits, True)
    out += mlp_forward(plan, r, s, c, k, waits, s[K.h], True)
    s[K.ysend][...] = s[K.yout][...].astype(BF)
    out.append(c.start(s[K.ysend], r[K.send]))
    for copy in out:
        copy.wait()


def run_radar(plan, r, s, c, k):
    d = plan.width
    arrive = c.start(r[K.streams], s[K.rb])
    weight = c.start(r[K.wcqkv], s[K.wcqkv])
    arrive.wait()
    weight.wait()
    s[K.rkv][:, :d] = dot_nn(s[K.rb][...], s[K.wcqkv][:, d : 2 * d]).astype(BF)
    s[K.rkv][:, d:] = (
        dot_nn(s[K.rb][...], s[K.wcqkv][:, 2 * d :]) + r[K.cross_bias][:, d : 2 * d]
    ).astype(BF)
    c.start(s[K.rkv], r[K.ckv]).wait()


def run_merged(plan, r, s, c, k):
    plan = plan.unrolled(3)
    d = plan.width
    rows = pl.ds(k * plan.rows, plan.rows)
    arrive = c.start(r[K.received], s[K.xb])
    waits = start_weights(r, s, c, (K.wqkv, K.wout, K.wcqkv, K.wcout, K.wfc1, K.wfc2))
    arrive_kv = c.start(r[K.ckv].at[rows], s[K.ckvb])
    arrive_grad = c.start(r[K.cotangent].at[rows], s[K.gin])
    arrive.wait()
    s[K.x][...] = s[K.xb][...].astype(F32)
    out = self_forward(plan, r, s, c, k, waits, False)
    bias = r[K.cross_bias]
    norm_forward(s[K.h], r[K.cross_gain][...], bias[:, 3 * d :], s[K.m])
    out.append(c.start(s[K.m], r[K.m].at[rows]))
    waits[K.wcqkv].wait()
    s[K.cq][...] = (dot_nn(s[K.m][...], s[K.wcqkv][:, :d]) + bias[:, :d]).astype(BF).astype(F32) * SCORE_SCALE
    arrive_kv.wait()
    s[K.ckv][...] = s[K.ckvb][...].astype(F32)
    live = most_live(plan, r, k, (K.counts, K.radar_counts))
    attend(
        plan,
        live,
        (s[K.cq], 0),
        (s[K.ckv], 0),
        (s[K.ckv], d),
        Spread(plan, r, s[K.cdist], k, K.radar_positions, K.radar_counts),
        r[K.slopes],
        s[K.cheard],
        s[K.cp],
    )
    s[K.co][...] = s[K.cheard][...].astype(BF)
    out.append(c.start(s[K.co], r[K.co].at[rows]))
    waits[K.wcout].wait()
    s[K.h2][...] = s[K.h][...] + dot_nn(s[K.co][...], s[K.wcout][...]) + bias[:, 2 * d : 3 * d]
    out += mlp_forward(plan, r, s, c, k, waits, s[K.h2], False)
    arrive_grad.wait()
    more, sums_two = mlp_backward(plan, r, s, c, k, {}, s[K.h2], s[K.dh])
    out += more
    s[K.gaf][...] = s[K.dh][...].astype(BF)
    out.append(c.start(s[K.gaf], r[K.gaf].at[rows]))
    s[K.cgo][...] = dot_nt(s[K.gaf][...], s[K.wcout][...])
    attend_back(
        plan,
        live,
        (s[K.cq], 0),
        (s[K.ckv], 0),
        (s[K.ckv], d),
        s[K.cgo],
        s[K.cp],
        [(s[K.dcqkv], part * d) for part in range(3)],
    )
    s[K.dcq][...] = s[K.dcqkv][:, :d].astype(BF)
    s[K.dckv][...] = s[K.dcqkv][:, d:].astype(BF)
    out.append(c.start(s[K.dcq], r[K.dcq].at[rows]))
    out.append(c.start(s[K.dckv], r[K.dckv].at[rows]))
    s[K.dm][...] = dot_nt(s[K.dcq][...], s[K.wcqkv][:, :d])
    sums_cross = norm_backward(s[K.h], r[K.cross_gain][...], s[K.dm], s[K.dh], s[K.dmid])
    more, sums_one = self_backward(plan, r, s, c, k, {}, s[K.dmid], s[K.dh])
    out += more
    s[K.dxb][...] = s[K.dh][...].astype(BF)
    out.append(c.start(s[K.dxb], r[K.send]))
    out.append(write_sums(s, c, r, sums_one + sums_two + sums_cross))
    for copy in out:
        copy.wait()


def load_mlp_back(plan, r, s, c, k):
    rows = pl.ds(k * plan.rows, plan.rows)
    arrive = [c.start(r[K.returned], s[K.gin])]
    waits = start_weights(r, s, c, (K.wfc2,))
    arrive.append(c.start(r[K.gp].at[rows], s[K.gp]))
    waits.update(start_weights(r, s, c, (K.wfc1,)))
    arrive.append(c.start(r[K.h].at[rows], s[K.h]))
    return arrive, waits


def load_self_back(plan, r, s, c, k):
    rows = pl.ds(k * plan.rows, plan.rows)
    waits = start_weights(r, s, c, (K.wout,))
    arrive = [
        c.start(r[K.qkv].at[rows], s[K.qkv]),
        c.start(r[K.p].at[pl.ds(k * plan.per * PAIRS, plan.per * PAIRS)], s[K.p]),
    ]
    waits.update(start_weights(r, s, c, (K.wqkv,)))
    arrive.append(c.start(r[K.streams].at[rows], s[K.xb]))
    return arrive, waits


def wait_all(copies):
    for copy in copies:
        copy.wait()


def run_backward(plan, r, s, c, k):
    rows = pl.ds(k * plan.rows, plan.rows)
    arrive, waits = load_mlp_back(plan, r, s, c, k)
    arrive_self, waits_self = load_self_back(plan, r, s, c, k)
    waits.update(waits_self)
    wait_all(arrive)
    out, sums_two = mlp_backward(plan, r, s, c, k, waits, s[K.h], s[K.dh])
    wait_all(arrive_self)
    s[K.x][...] = s[K.xb][...].astype(F32)
    more, sums_one = self_backward(plan, r, s, c, k, waits, s[K.dh], s[K.dx])
    out += more
    out.append(c.start(s[K.dx], r[K.input_grads].at[rows]))
    out.append(write_sums(s, c, r, sums_one + sums_two))
    wait_all(out)


def run_backward_mlp(plan, r, s, c, k):
    arrive, waits = load_mlp_back(plan, r, s, c, k)
    wait_all(arrive)
    out, sums_two = mlp_backward(plan, r, s, c, k, waits, s[K.h], s[K.dh])
    out.append(c.start(s[K.dh], r[K.between]))
    nothing = jnp.zeros_like(sums_two[0])
    out.append(write_sums(s, c, r, (nothing, nothing) + sums_two))
    wait_all(out)


def run_backward_self(plan, r, s, c, k):
    rows = pl.ds(k * plan.rows, plan.rows)
    arrive = [c.start(r[K.between], s[K.dh])]
    more, waits = load_self_back(plan, r, s, c, k)
    wait_all(arrive + more)
    s[K.x][...] = s[K.xb][...].astype(F32)
    out, sums_one = self_backward(plan, r, s, c, k, waits, s[K.dh], s[K.dx])
    out.append(c.start(s[K.dx], r[K.input_grads].at[rows]))
    out.append(write_sums(s, c, r, sums_one))
    wait_all(out)


def run_radar_back(plan, r, s, c, k):
    d = plan.width
    arrive = c.start(r[K.dckv], s[K.rkv])
    weight = c.start(r[K.wcqkv], s[K.wcqkv])
    arrive.wait()
    weight.wait()
    s[K.rdr][...] = dot_nt(s[K.rkv][...], s[K.wcqkv][:, d:])
    c.start(s[K.rdr], r[K.input_grads]).wait()


def slot_of(relative):
    return ((relative >> 1) & 1) * 4 + ((relative >> 2) & 1) * 2 + ((relative >> 3) & 1)


def weight_grads(plan, r, s, c, lefts, rights, left_of, tall, name, fix=None):
    d, total = plan.width, plan.total

    def blocks(buffer, names):
        found = []
        for array in names:
            for tile in tiles(r[array].shape[1], d):
                at = len(found) * d
                found.append((r[array].at[:, tile], buffer.at[:, at : at + d]))
        return found

    left_blocks, right_blocks = blocks(s[K.gl], lefts), blocks(s[K.gr], rights)
    count = max(len(left_blocks), len(right_blocks))
    loads, seen = [], set()
    for t in range(count):
        wanted = [(0, 0 if tall else t), (1, left_of(t))]
        fresh = [key for key in wanted if key not in seen]
        seen.update(fresh)
        loads.append([c.start(*(right_blocks, left_blocks)[side][at]) for side, at in fresh])
    if fix is not None:
        wait_all(loads[0])
        loads[0] = []
        fix()
    mine = r[K.device][0]
    block = d // 4 if tall else d // 16
    natural = s[K.gnat_tall if tall and plan.halving else K.gnat]
    gout = s[K.gout_tall if tall else K.gout] if plan.halving else None
    sems = c.reserve(4)

    def columns(at):
        return pl.ds(pl.multiple_of(at * d, LANES), d)

    def copies_out(t):
        slot = lax.rem(t, 2)
        found = []
        for sent in range(2 if plan.halving else 1):
            ref = r[SENT[name] if sent else name]
            if not plan.halving:
                target = ref.at[columns(t), :] if tall else ref.at[:, columns(t)]
                source = natural.at[slot]
            elif tall:
                away = t ^ (mine >> 2)
                target, source = ref.at[:, away & 1, away >> 1], gout.at[slot, sent]
            else:
                target, source = ref.at[:, :, columns(t)], gout.at[slot, sent]
            found.append(pltpu.make_async_copy(source, target, sems(slot * 2 + sent)))
        return found

    def wait_out(t):
        wait_all(copies_out(t))

    def hand_on(t):
        for one in copies_out(t):
            one.start()

    def arrange(slot):
        if tall:
            for relative in range(4):
                gout[slot, relative & 1, relative >> 1] = natural[slot, (mine & 3) ^ relative]
        else:
            for relative in range(16):
                gout[slot, relative & 1, slot_of(relative)] = natural[slot, mine ^ relative]

    behind = 1 if plan.halving else 0

    def step(t, carry):
        for at, found in enumerate(loads):
            if found:
                pl.when(t == at)(lambda found=found: wait_all(found))
        pl.when(t >= 2 + behind)(lambda: wait_out(t - 2 - behind))
        slot = lax.rem(t, 2)
        grad = s[K.gr][:, columns(0 if tall else t)]
        low = dot_tn(s[K.gl][:, columns(left_of(t))], grad).astype(BF)
        if plan.halving:
            for part in range(d // block):
                natural[slot, part] = low[part * block : (part + 1) * block]
            arrange(1 - slot)
        else:
            natural[slot] = low
        sums = jnp.sum(grad.astype(F32).reshape(total // 8, 8, d), axis=0)
        s[K.gsums][:, columns(0 if tall else t)] = sums
        pl.when(t >= behind)(lambda: hand_on(t - behind))
        return carry

    lax.fori_loop(0, count, step, 0)
    if plan.halving:
        wait_out(count - 3)
        arrange((count - 1) % 2)
        hand_on(count - 1)
    breadth = len(right_blocks) * d
    last = c.start(s[K.gsums].at[:, :breadth], r[SUMS[name]])
    wait_out(count - 2)
    wait_out(count - 1)
    last.wait()


def run_grads_cross(plan, r, s, c, k):
    weight_grads(
        plan, r, s, c, (K.m, K.streams, K.co), (K.dcq, K.dckv, K.gaf),
        lambda t: (t + 1) // 2, False, K.cross,
    )


def run_grads_fc2(plan, r, s, c, k):
    last = plan.steps - 1
    arrive = c.start(r[K.returned], s[K.gin])

    def fix():
        arrive.wait()

        @pl.when(r[K.section][0] == 0)
        def _():
            s[K.dn][...] = s[K.gin][...].astype(F32)
            fill_rows(s[K.g], plan.per, plan.slots, r[K.counts], last * plan.per, s[K.dn])
            s[K.gr][last * plan.rows :, : plan.width] = s[K.g][...].astype(BF)

    weight_grads(plan, r, s, c, (K.a,), (K.gbr,), lambda t: t, True, K.fc2, fix)


def run_grads_fc1(plan, r, s, c, k):
    weight_grads(plan, r, s, c, (K.n2,), (K.du,), lambda t: 0 * t, False, K.fc1)


def run_grads_more(plan, r, s, c, k):
    run_grads_fc2(plan, r, s, c, k)
    run_grads_fc1(plan, r, s, c, k)


def run_grads_attn(plan, r, s, c, k):
    weight_grads(plan, r, s, c, (K.n, K.o), (K.dqkv, K.gm), lambda t: t // 3, False, K.attn)
    d = plan.width
    first = sum(r[name][...] for name in r if name in FIRST)
    second = sum(r[name][...] for name in r if name in SECOND)
    norms = jnp.where(r[K.section][0] == 0, first, second)
    ratio = plan.hidden // d

    def column(ref, at):
        return jnp.sum(ref[:, at * d : (at + 1) * d], axis=0, keepdims=True)

    rows = [column(s[K.gsums], 0), column(s[K.gsums], 2), column(s[K.gsums], 3)]
    rows += [column(r[K.fc1_sums], at) for at in range(ratio)] + [column(r[K.fc2_sums], 0)]
    rows += [norms[0:1], norms[2:3], norms[1:2], norms[3:4], norms[4:5]]
    rows += [column(r[K.cross_sums], at) for at in (0, 2, 3)] + [norms[5:6]]
    s[K.small][...] = jnp.zeros_like(s[K.small])
    for at, row in enumerate(rows):
        s[K.small][at : at + 1, :] = row
    c.start(s[K.small], r[K.small]).wait()


RUN = {
    K.forward: run_forward,
    K.radar: run_radar,
    K.merged: run_merged,
    K.backward: run_backward,
    K.backward_mlp: run_backward_mlp,
    K.backward_self: run_backward_self,
    K.radar_back: run_radar_back,
    K.grads_cross: run_grads_cross,
    K.grads_fc2: run_grads_fc2,
    K.grads_fc1: run_grads_fc1,
    K.grads_attn: run_grads_attn,
    K.grads_more: run_grads_more,
}


def phase(plan, fixed, state, weights, first, second, after=()):
    jobs = [job for job in (first, second) if job is not None]
    shared = len(jobs) == 2 and jobs[0][0] == jobs[1][0]
    kinds = [JOBS[job[0]] for job in jobs]
    taken = {}
    for job in jobs:
        taken.update(job[2])
    writes = []
    for kind in kinds:
        writes += [name for name in kind.writes if name not in writes]
    reads = []
    for kind in kinds:
        for name in kind.reads:
            if name in state and name not in reads and name not in writes:
                reads.append(name)
            elif name in (K.streams, K.cotangent):
                taken[name] = fixed[name]
    used = [name for name in WEIGHT_NAMES if any(name in kind.weights for kind in kinds)]
    fresh = [name for name in writes if name not in state or name in (K.send, K.ln)]
    kept = [name for name in writes if name not in fresh]
    small = [name for name in fixed if name not in (K.streams, K.cotangent)]
    if all(job[0] in GRAD_JOBS for job in jobs):
        small = [K.section, K.device, K.counts]
    elif not any(job[0] in (K.radar, K.merged) for job in jobs):
        small = [name for name in small if name not in (K.cross_gain, K.cross_bias)]
    every = scratch_shapes(plan)
    need = list(used)
    for kind in kinds:
        need += [name for name in kind.scratch if name not in need]

    operands, specs, names = [], [], []
    for name in small:
        operands.append(fixed[name])
        specs.append(SM if name in (K.section, K.device, K.counts, K.radar_counts, K.slopes) else VM)
        names.append(name)
    for name in used:
        operands.append(weights[name])
        specs.append(ANY)
        names.append(name)
    for name, array in list(taken.items()) + [(name, state[name]) for name in reads]:
        operands.append(array)
        specs.append(VM if name in IN_VMEM else ANY)
        names.append(name)
    operands += after
    specs += [ANY] * len(after)
    names += [None] * len(after)
    alias = {}
    for at, name in enumerate(kept):
        alias[len(operands)] = at
        operands.append(state[name])
        specs.append(ANY)
        names.append(None)
    outs = kept + fresh
    shapes = [jax.ShapeDtypeStruct(*STATE[name](plan)) for name in outs]

    def kernel(*refs):
        r, s = {}, {}
        for name, ref in zip(names, refs):
            if name is not None:
                r[name] = ref
        refs = refs[len(names) :]
        for name, ref in zip(outs, refs):
            r[name] = ref
        refs = refs[len(outs) :]
        for name, ref in zip(need, refs):
            s[name] = ref
        sems = refs[len(need)]
        if shared:
            RUN[first[0]](plan, r, s, Copies(sems), first[1])
            return
        for which, job in ((0, first), (1, second)):
            if job is not None:

                @pl.when(r[K.section][0] == which)
                def _():
                    RUN[job[0]](plan, r, s, Copies(sems), job[1])

    results = pl.pallas_call(
        kernel,
        out_shape=shapes,
        in_specs=specs,
        out_specs=[ANY] * len(outs),
        scratch_shapes=[pltpu.VMEM(*every[name]) for name in need] + [pltpu.SemaphoreType.DMA((32,))],
        input_output_aliases=alias,
        compiler_params=pltpu.CompilerParams(vmem_limit_bytes=VMEM_LIMIT),
        cost_estimate=CHEAP,
        name="_".join(job[0].name + str(job[1]) for job in jobs),
    )(*operands)
    new = dict(zip(outs, results))
    for name in outs:
        if name not in (K.send, K.ln):
            state[name] = new[name]
    return new.get(K.send), new.get(K.ln)


def body(
    streams,
    cotangent,
    counts,
    positions,
    radar_counts,
    radar_positions,
    qkv_weight,
    out_weight,
    fc1_weight,
    fc2_weight,
    attn_bias,
    mlp_bias,
    norm_gains,
    norm_shifts,
    cross_qkv_weight,
    cross_out_weight,
    cross_gain,
    cross_bias,
):
    devices = lax.axis_size(BATCH)
    section_id = lax.axis_index(SECTION)
    me = lax.axis_index(BATCH)
    width = cotangent.shape[1]
    hidden = fc1_weight.shape[2]
    halving = devices == 16
    plan = Plan(counts.shape[0], positions.shape[1], width, hidden, halving)
    device = me.astype(jnp.int32).reshape(1)
    section = section_id.astype(jnp.int32).reshape(1)
    head_slopes = [2.0 ** (-8.0 * (head + 1.0) / H) for head in range(H)]
    fixed = {
        K.section: section,
        K.device: device,
        K.counts: counts,
        K.radar_counts: radar_counts,
        K.slopes: jnp.array(head_slopes, F32),
        K.positions: positions,
        K.radar_positions: radar_positions,
        K.attn_bias: attn_bias,
        K.mlp_bias: mlp_bias,
        K.gains: norm_gains,
        K.shifts: norm_shifts,
        K.cross_gain: cross_gain.reshape(1, width),
        K.cross_bias: cross_bias.reshape(1, 4 * width),
        K.streams: streams[0],
        K.cotangent: cotangent,
    }
    weights = dict(
        zip(
            WEIGHT_NAMES,
            (
                qkv_weight[0],
                out_weight[0],
                fc1_weight[0],
                fc2_weight[0],
                cross_qkv_weight,
                cross_out_weight,
            ),
        )
    )
    state = {}
    steps = plan.steps
    arrived = []
    for k in range(steps):
        second = (K.radar, 0, {}) if k == min(1, steps - 1) else None
        send, _ = phase(plan, fixed, state, weights, (K.forward, k, {}), second)
        arrived.append(lax.ppermute(send, SECTION, [(0, 1)]))
    returned, first_sums, second_sums = [], [], []
    for k in range(steps):
        send, sums = phase(
            plan, fixed, state, weights, None, (K.merged, k, {K.received: arrived[k]})
        )
        second_sums.append(sums)
        returned.append(lax.ppermute(send, SECTION, [(1, 0)]))
        if 0 < k < steps - 1:
            _, sums = phase(
                plan, fixed, state, weights, (K.backward, k - 1, {K.returned: returned[k - 1]}), None
            )
            first_sums.append(sums)

    route = {bit: [(at, at ^ bit) for at in range(devices)] for bit in (1, 2, 4, 8, 12)} if halving else {}

    def trade(block, bit):
        return lax.ppermute(block, BATCH, route[bit])

    def trade_second(block, bit):
        pairs = [(devices + left, devices + right) for left, right in route[bit]]
        return lax.ppermute(block, (SECTION, BATCH), pairs)

    def scatter(part):
        return lax.psum_scatter(part, BATCH, scatter_dimension=0, tiled=True).astype(F32)

    def run(first, second, after=()):
        _, sums = phase(plan, fixed, state, weights, first, second, after=list(after))
        if first is not None and first[0] in BACK_JOBS:
            first_sums.append(sums)

    def both(job, taken, after=()):
        run((job, 0, taken), (job, 0, taken), after)

    def add_up(parts, low, high):
        return sum(part[low:high].astype(F32) for part in parts)

    def begin(name, exchange, pieces=1):
        kept, sent = state[name], state[SENT[name]]
        kept, sent = (x.reshape(8, -1, x.shape[-1]) for x in (kept, sent))
        come = [exchange(piece, 1) for piece in jnp.split(sent, pieces)]
        return [kept, jnp.concatenate(come) if pieces > 1 else come[0]]

    def step(parts, exchange, bit):
        half = parts[-1].shape[0] // 2
        return parts + [exchange(add_up(parts, half, 2 * half).astype(BF), bit)]

    def spread(parts, exchange):
        found = [exchange(add_up(parts, at, at + 1).astype(BF), bit) for at, bit in ((1, 8), (2, 4), (3, 12))]
        return [part[:1] for part in parts] + found

    def total(parts):
        return add_up(parts, 0, 1)[0]

    def taken_sums():
        return dict(zip(FIRST, first_sums)) | dict(zip(SECOND, second_sums))

    def once(*arrays):
        return lax.optimization_barrier(arrays)

    last = steps - 1
    queue = [(K.backward, k, {K.returned: returned[k]}) for k in range(max(last - 1, 0), last)] or [None]
    for job in queue[:-1]:
        run(job, None)
    run(queue[-1], (K.grads_cross, 0, {}))
    if halving:
        state[K.cross_send], returned[last] = once(state[K.cross_send], returned[last])
        cross = step(begin(K.cross, trade_second), trade_second, 2)
        taken = {K.returned: returned[last]}
        run((K.grads_fc2, 0, taken), (K.grads_more, 0, taken), [cross[1]])
        state[K.fc2], state[K.fc2_send], cross[-1] = once(
            state[K.fc2], state[K.fc2_send], cross[-1]
        )
        fc2 = begin(K.fc2, trade)
        ahead = add_up(fc2, 4, 8).astype(BF)
        cross[-1], ahead = once(cross[-1], ahead)
        fc2.append(trade(ahead, 2))
        cross = spread(cross, trade_second)
        run((K.backward_mlp, last, taken), None, [fc2[1]])
        run((K.grads_fc1, 0, {}), None)
        state[K.fc1], state[K.fc1_send], fc2[-1], *cross[-3:] = once(
            state[K.fc1], state[K.fc1_send], fc2[-1], *cross[-3:]
        )
        fc1 = begin(K.fc1, trade)
        fc2 = spread(fc2, trade)
        run((K.backward_self, last, {}), None, [fc1[-1]])
        fc1 = step(fc1, trade, 2)
        both(K.grads_attn, taken_sums())
        state[K.attn], state[K.attn_send], fc1[-1], *fc2[-3:] = once(
            state[K.attn], state[K.attn_send], fc1[-1], *fc2[-3:]
        )
        attn = begin(K.attn, trade)
        ahead = add_up(attn, 4, 8).astype(BF)
        ahead, fc1[-1], small = once(ahead, fc1[-1], state[K.small])
        attn.append(trade(ahead, 2))
        fc1 = spread(fc1, trade)
        small = small + trade(small, 1)
        next_small = trade(small, 2)
        run(None, (K.radar_back, 0, {}), [small])
        attn[-1], next_small, state[K.input_grads], *fc1[-3:] = once(
            attn[-1], next_small, state[K.input_grads], *fc1[-3:]
        )
        small = small + next_small
        small = small + sum(trade(small, bit) for bit in (4, 8, 12))
        attn = spread(attn, trade)
        cross_share, grad_fc2, grad_fc1, grad_attn = (total(x) for x in (cross, fc2, fc1, attn))
    else:
        both(K.grads_fc2, {K.returned: returned[last]})
        run((K.backward_mlp, last, {K.returned: returned[last]}), None)
        both(K.grads_fc1, {})
        run((K.backward_self, last, {}), None)
        both(K.grads_attn, taken_sums())
        small = lax.psum(state[K.small], BATCH)
        run(None, (K.radar_back, 0, {}))
        cross_share, grad_fc2, grad_fc1, grad_attn = (
            scatter(state[name]) for name in (K.cross, K.fc2, K.fc1, K.attn)
        )
    split = qkv_weight.shape[2]

    is_first = section_id == 0

    def to_both(block):
        return jnp.where(is_first, lax.ppermute(block, SECTION, [(1, 0)]), block).astype(F32)

    cross_all = to_both(cross_share.astype(BF))
    ratio = hidden // width
    edges = [0, 3, 4 + ratio, 6 + ratio, 8 + ratio, 9 + ratio, 13 + ratio]
    cross_small = to_both(small[edges[4] : edges[6]])
    parts = []
    for low, high in zip(edges, edges[1:]):
        rows = small[low:high] if high <= edges[4] else cross_small[low - edges[4] : high - edges[4]]
        size = (high - low) * width // devices
        parts.append(lax.dynamic_slice(rows.reshape(-1), (me * size,), (size,)))
    return (
        state[K.layer_out][None],
        state[K.input_grads][None],
        grad_attn[None, :, :split],
        grad_attn[None, :, split:],
        grad_fc1[None],
        grad_fc2[None],
        parts[0][None],
        parts[1][None],
        parts[2][None],
        parts[3][None],
        cross_all[:, :split],
        cross_all[:, split:],
        parts[4],
        parts[5],
    )


def solution(mesh):
    in_specs = (
        P(SECTION, BATCH, None),
        P(BATCH, None),
        P(BATCH),
        P(BATCH, None),
        P(BATCH),
        P(BATCH, None),
        P(SECTION, None, None),
        P(SECTION, None, None),
        P(SECTION, None, None),
        P(SECTION, None, None),
        P(SECTION, None),
        P(SECTION, None),
        P(SECTION, None),
        P(SECTION, None),
        P(),
        P(),
        P(),
        P(),
    )
    out_specs = (
        P(SECTION, BATCH, None),
        P(SECTION, BATCH, None),
        P(SECTION, BATCH, None),
        P(SECTION, BATCH, None),
        P(SECTION, BATCH, None),
        P(SECTION, BATCH, None),
        P(SECTION, BATCH),
        P(SECTION, BATCH),
        P(SECTION, BATCH),
        P(SECTION, BATCH),
        P(BATCH, None),
        P(BATCH, None),
        P(BATCH),
        P(BATCH),
    )
    return jax.shard_map(body, mesh=mesh, in_specs=in_specs, out_specs=out_specs, check_vma=False)
```

```python
import enum
import typing

import jax
import jax.numpy as jnp
from jax import lax
from jax.experimental import pallas as pl
from jax.experimental.pallas import tpu as pltpu
from jax.sharding import PartitionSpec as P

SECTION, BATCH = "section", "batch"
H = 12
HD = 64
PAIRS = H // 2
LANES = 2 * HD
GRID = 15
SCORE_SCALE = 0.125
NORM_EPS = 1e-06
FAR = 1e33
CHUNK = 16
BF = jnp.bfloat16
F32 = jnp.float32
VMEM_LIMIT = 60 << 20
CHEAP = pl.CostEstimate(flops=1, bytes_accessed=1, transcendentals=0)
ANY = pl.BlockSpec(memory_space=pl.ANY)
VM = pl.BlockSpec(memory_space=pltpu.VMEM)
SM = pl.BlockSpec(memory_space=pltpu.SMEM)


class K(enum.Enum):
    a = enum.auto()
    attn = enum.auto()
    attn_bias = enum.auto()
    attn_send = enum.auto()
    attn_sums = enum.auto()
    backward = enum.auto()
    backward_mlp = enum.auto()
    backward_self = enum.auto()
    between = enum.auto()
    cdist = enum.auto()
    cgo = enum.auto()
    cheard = enum.auto()
    ckv = enum.auto()
    ckvb = enum.auto()
    co = enum.auto()
    cotangent = enum.auto()
    counts = enum.auto()
    cp = enum.auto()
    cq = enum.auto()
    cross = enum.auto()
    cross_bias = enum.auto()
    cross_gain = enum.auto()
    cross_send = enum.auto()
    cross_sums = enum.auto()
    dckv = enum.auto()
    dcq = enum.auto()
    dcqkv = enum.auto()
    device = enum.auto()
    dh = enum.auto()
    dist = enum.auto()
    dm = enum.auto()
    dmid = enum.auto()
    dn = enum.auto()
    dqkv = enum.auto()
    dqkvb = enum.auto()
    du = enum.auto()
    dx = enum.auto()
    dxb = enum.auto()
    fc1 = enum.auto()
    fc1_send = enum.auto()
    fc1_sums = enum.auto()
    fc2 = enum.auto()
    fc2_send = enum.auto()
    fc2_sums = enum.auto()
    forward = enum.auto()
    g = enum.auto()
    gaf = enum.auto()
    gains = enum.auto()
    gbr = enum.auto()
    gin = enum.auto()
    gl = enum.auto()
    gm = enum.auto()
    gnat = enum.auto()
    gnat_tall = enum.auto()
    go = enum.auto()
    gout = enum.auto()
    gout_tall = enum.auto()
    gp = enum.auto()
    gr = enum.auto()
    grads_attn = enum.auto()
    grads_cross = enum.auto()
    grads_fc1 = enum.auto()
    grads_fc2 = enum.auto()
    grads_early = enum.auto()
    grads_late = enum.auto()
    gsums = enum.auto()
    h = enum.auto()
    h2 = enum.auto()
    heard = enum.auto()
    input_grads = enum.auto()
    layer_out = enum.auto()
    ln = enum.auto()
    m = enum.auto()
    merged = enum.auto()
    mlp_bias = enum.auto()
    n = enum.auto()
    n2 = enum.auto()
    o = enum.auto()
    p = enum.auto()
    positions = enum.auto()
    qkv = enum.auto()
    radar = enum.auto()
    radar_back = enum.auto()
    radar_counts = enum.auto()
    radar_positions = enum.auto()
    rb = enum.auto()
    rdr = enum.auto()
    received = enum.auto()
    returned = enum.auto()
    rkv = enum.auto()
    section = enum.auto()
    send = enum.auto()
    shifts = enum.auto()
    slopes = enum.auto()
    small = enum.auto()
    streams = enum.auto()
    u = enum.auto()
    wcout = enum.auto()
    wcqkv = enum.auto()
    wfc1 = enum.auto()
    wfc2 = enum.auto()
    wout = enum.auto()
    wqkv = enum.auto()
    x = enum.auto()
    xb = enum.auto()
    y = enum.auto()
    yout = enum.auto()
    ysend = enum.auto()


SENT = {K.cross: K.cross_send, K.fc2: K.fc2_send, K.fc1: K.fc1_send, K.attn: K.attn_send}
SUMS = {K.cross: K.cross_sums, K.fc2: K.fc2_sums, K.fc1: K.fc1_sums, K.attn: K.attn_sums}
FIRST = [(K.ln, 0, at) for at in range(64)]
SECOND = [(K.ln, 1, at) for at in range(64)]
IN_VMEM = FIRST + SECOND + list(SUMS.values())
GRAD_JOBS = (K.grads_cross, K.grads_fc2, K.grads_fc1, K.grads_attn, K.grads_early, K.grads_late)
BACK_JOBS = (K.backward, K.backward_mlp, K.backward_self)


class Job(typing.NamedTuple):
    reads: tuple
    writes: tuple
    weights: tuple
    scratch: tuple


def dot_nn(left, right):
    return jnp.dot(left, right, preferred_element_type=F32)


def dot_tn(left, right):
    return lax.dot_general(left, right, (((0,), (0,)), ((), ())), preferred_element_type=F32)


def dot_nt(left, right):
    return lax.dot_general(left, right, (((1,), (1,)), ((), ())), preferred_element_type=F32)


class Copies:
    def __init__(self, sems):
        self.sems = sems
        self.used = 0

    def start(self, source, target):
        copy = pltpu.make_async_copy(source, target, self.sems.at[self.used])
        self.used += 1
        copy.start()
        return copy

    def reserve(self, count):
        first = self.used
        self.used += count
        return lambda at: self.sems.at[first + at]


def spans(rows):
    return [slice(at, at + CHUNK) for at in range(0, rows, CHUNK)]


def norm_parts(values):
    average = jnp.mean(values, axis=-1, keepdims=True)
    centred = values - average
    spread = jnp.mean(centred * centred, axis=-1, keepdims=True)
    scale = lax.rsqrt(spread + NORM_EPS)
    return centred * scale, scale


def norm_forward(source, gain, shift, target):
    for span in spans(source.shape[0]):
        unit, _ = norm_parts(source[span, :])
        target[span, :] = (unit * gain + shift).astype(BF)


def norm_backward(source, gain, upstream, residual, target):
    gain_sum = jnp.zeros((8, source.shape[1]), F32)
    shift_sum = jnp.zeros((8, source.shape[1]), F32)
    for span in spans(source.shape[0]):
        unit, scale = norm_parts(source[span, :])
        grad = upstream[span, :]
        product = grad * unit
        gain_sum = gain_sum + product[:8] + product[8:]
        shift_sum = shift_sum + grad[:8] + grad[8:]
        inner = grad * gain
        mean_one = jnp.mean(inner, axis=-1, keepdims=True)
        mean_two = jnp.mean(inner * unit, axis=-1, keepdims=True)
        target[span, :] = residual[span, :] + scale * (inner - mean_one - unit * mean_two)
    return (
        jnp.sum(gain_sum, axis=0, keepdims=True),
        jnp.sum(shift_sum, axis=0, keepdims=True),
    )


def gelu_both(values):
    cdf = 0.5 + 0.5 * lax.erf(values * 0.7071067811865476)
    density = 0.3989422804014327 * jnp.exp(-0.5 * values * values)
    return values * cdf, cdf + values * density


def place(positions):
    values = positions
    row = jnp.floor((values + 0.5) * (1.0 / GRID))
    return row, values - GRID * row


def distances(key_col, query_row, live_keys):
    row_q, col_q = place(query_row)
    row_k, col_k = place(key_col)
    gap_row = row_q - row_k
    gap_col = col_q - col_k
    distance = jnp.sqrt(gap_row * gap_row + gap_col * gap_col)
    slot = lax.broadcasted_iota(jnp.int32, distance.shape, 0)
    return jnp.where(slot < live_keys, distance, FAR)


def both_heads(pair):
    first = lax.broadcasted_iota(jnp.int32, pair.shape, 1) < HD
    zero = jnp.zeros_like(pair)
    return jnp.concatenate([jnp.where(first, pair, zero), jnp.where(first, zero, pair)], axis=0)


def one_pair(stacked):
    half = stacked.shape[0] // 2
    first = lax.broadcasted_iota(jnp.int32, (half, LANES), 1) < HD
    return jnp.where(first, stacked[:half], stacked[half:])


def by_size(plan, most_live, work):
    def step(image, carry):
        if plan.slots <= LANES:
            work(image, plan.slots)
        else:
            live = most_live(image)

            @pl.when(live <= LANES)
            def _():
                work(image, LANES)

            @pl.when(live > LANES)
            def _():
                work(image, plan.slots)

        return carry

    lax.fori_loop(0, plan.per, step, 0)


def rows_of(plan, image, first, size):
    return pl.ds(pl.multiple_of(image * plan.slots + first, 8), size)


def pair_lanes(base, pair):
    if isinstance(pair, int):
        return pl.ds(base + pair * LANES, LANES)
    return pl.ds(pl.multiple_of(base + pair * LANES, LANES), LANES)


def over_pairs(plan, work, size):
    unroll = PAIRS if size <= LANES else plan.unroll

    def step(at, carry):
        for part in range(unroll):
            work(at * unroll + part)
        return carry

    if unroll == PAIRS:
        step(0, 0)
    else:
        lax.fori_loop(0, PAIRS // unroll, step, 0)


def attend(plan, most_live, query, keys, values, spread, slopes, heard, weights):
    def work(image, size):
        rows = rows_of(plan, image, 0, size)
        if size < plan.slots:
            rest = rows_of(plan, image, size, plan.slots - size)
            heard[rest, :] = jnp.zeros((plan.slots - size, plan.width), F32)
        spread(image, size)
        gap_ref = spread.target

        def one(pair):
            q = both_heads(query[0][rows, pair_lanes(query[1], pair)]).astype(BF)
            k = keys[0][rows, pair_lanes(keys[1], pair)].astype(BF)
            v = values[0][rows, pair_lanes(values[1], pair)].astype(BF)
            first = lax.broadcasted_iota(jnp.int32, (1, 2 * size), 1) < size
            slope = jnp.where(first, slopes[2 * pair], slopes[2 * pair + 1])
            scores = dot_nt(k, q) - slope * gap_ref[image, :size, : 2 * size]
            scores = jnp.exp(scores - jnp.max(scores, axis=0, keepdims=True))
            totals = jnp.sum(scores, axis=0, keepdims=True)
            p = (scores * (1.0 / totals)).astype(BF)
            weights[image * PAIRS + pair, :size, : 2 * size] = p
            heard[rows, pair_lanes(0, pair)] = one_pair(dot_tn(p, v))

        over_pairs(plan, one, size)

    by_size(plan, most_live, work)


def attend_back(plan, most_live, query, keys, values, grad_heard, weights, grads):
    grad_q, grad_k, grad_v = grads

    def work(image, size):
        rows = rows_of(plan, image, 0, size)
        if size < plan.slots:
            rest = rows_of(plan, image, size, plan.slots - size)
            for ref, offset in grads:
                ref[rest, offset : offset + plan.width] = jnp.zeros((plan.slots - size, plan.width), F32)

        def one(pair):
            q = both_heads(query[0][rows, pair_lanes(query[1], pair)]).astype(BF)
            k = keys[0][rows, pair_lanes(keys[1], pair)].astype(BF)
            v = values[0][rows, pair_lanes(values[1], pair)].astype(BF)
            g = both_heads(grad_heard[rows, pair_lanes(0, pair)]).astype(BF)
            p = weights[image * PAIRS + pair, :size, : 2 * size]
            wide = p.astype(F32)
            product = dot_nt(v, g) * wide
            grad_s = (product - wide * jnp.sum(product, axis=0, keepdims=True)).astype(BF)
            grad_v[0][rows, pair_lanes(grad_v[1], pair)] = dot_nn(p, g)
            grad_k[0][rows, pair_lanes(grad_k[1], pair)] = dot_nn(grad_s, q)
            grad_q[0][rows, pair_lanes(grad_q[1], pair)] = one_pair(dot_tn(grad_s, k)) * SCORE_SCALE

        over_pairs(plan, one, size)

    by_size(plan, most_live, work)


def columns_of(positions):
    images = positions.shape[0]
    low = positions.astype(F32).astype(BF)
    row = lax.broadcasted_iota(jnp.int32, (images, LANES), 0)
    lane = lax.broadcasted_iota(jnp.int32, (images, LANES), 1)
    return dot_tn(low, (row == lane).astype(F32).astype(BF))


def twice(positions, size):
    slots = positions.shape[1]
    low = positions.astype(F32).astype(BF)
    row = lax.broadcasted_iota(jnp.int32, (slots, 2 * size), 0)
    lane = lax.broadcasted_iota(jnp.int32, (slots, 2 * size), 1)
    from_slot = jnp.where(lane < size, lane, lane - size)
    return dot_nn(low, (row == from_slot).astype(F32).astype(BF))


class Spread:
    def __init__(self, plan, r, target, k, key_positions, key_count):
        self.plan, self.r, self.target, self.k = plan, r, target, k
        self.key_positions, self.key_count = key_positions, key_count

    def __call__(self, image, size):
        at = self.k * self.plan.per + image
        query = twice(self.r[K.positions][pl.ds(at, 1), :], size)
        keys = columns_of(self.r[self.key_positions][pl.ds(at, 1), :])
        self.target[image, :size, : 2 * size] = distances(
            keys[:size, :1], query, self.r[self.key_count][at]
        )


def most_live(plan, r, k, names):
    def live(image):
        found = r[names[0]][k * plan.per + image]
        for name in names[1:]:
            found = jnp.maximum(found, r[name][k * plan.per + image])
        return found

    return live


def fill_rows(target, images, slots, counts, first_image, source):
    for image in range(images):
        live = counts[first_image + image]
        for at in range(0, slots, 8):
            span = slice(image * slots + at, image * slots + at + 8)
            row = at + lax.broadcasted_iota(jnp.int32, (8, source.shape[1]), 0)
            target[span, :] = jnp.where(row < live, source[span, :], 0.0)


class Plan:
    def __init__(self, batches, slots, width, hidden, halving, unroll=1):
        self.batches, self.slots, self.width, self.hidden = batches, slots, width, hidden
        self.halving = halving
        self.unroll = unroll
        self.per = 2 if batches % 2 == 0 else 1
        self.steps = batches // self.per
        self.rows = self.per * slots
        self.total = batches * slots

    def unrolled(self, unroll):
        return Plan(self.batches, self.slots, self.width, self.hidden, self.halving, unroll)


def small_shape(plan):
    rows = 13 + plan.hidden // plan.width
    return (-(-rows // 8) * 8, plan.width)


WEIGHT_NAMES = (K.wqkv, K.wout, K.wfc1, K.wfc2, K.wcqkv, K.wcout)


def scratch_shapes(plan):
    r, d, f = plan.rows, plan.width, plan.hidden
    w = {
        K.wqkv: ((d, 3 * d), BF),
        K.wout: ((d, d), BF),
        K.wfc1: ((d, f), BF),
        K.wfc2: ((f, d), BF),
        K.wcqkv: ((d, 3 * d), BF),
        K.wcout: ((d, d), BF),
        K.xb: ((r, d), BF),
        K.x: ((r, d), F32),
        K.n: ((r, d), BF),
        K.qkv: ((r, 3 * d), F32),
        K.p: ((plan.per * PAIRS, plan.slots, 2 * plan.slots), BF),
        K.dist: ((plan.per, plan.slots, 2 * plan.slots), F32),
        K.heard: ((r, d), F32),
        K.o: ((r, d), BF),
        K.h: ((r, d), F32),
        K.n2: ((r, d), BF),
        K.u: ((r, f), F32),
        K.a: ((r, f), BF),
        K.gp: ((r, f), BF),
        K.y: ((r, d), F32),
        K.yout: ((r, d), F32),
        K.ysend: ((r, d), BF),
        K.gin: ((r, d), BF),
        K.g: ((r, d), F32),
        K.gbr: ((r, d), BF),
        K.du: ((r, f), BF),
        K.dn: ((r, d), F32),
        K.dh: ((r, d), F32),
        K.gm: ((r, d), BF),
        K.go: ((r, d), F32),
        K.dqkv: ((r, 3 * d), F32),
        K.dqkvb: ((r, 3 * d), BF),
        K.dx: ((r, d), F32),
        K.dxb: ((r, d), BF),
        K.ln: ((8, d), F32),
        K.cdist: ((plan.per, plan.slots, 2 * plan.slots), F32),
        K.m: ((r, d), BF),
        K.cq: ((r, d), F32),
        K.ckvb: ((r, 2 * d), BF),
        K.ckv: ((r, 2 * d), F32),
        K.cp: ((plan.per * PAIRS, plan.slots, 2 * plan.slots), BF),
        K.cheard: ((r, d), F32),
        K.co: ((r, d), BF),
        K.h2: ((r, d), F32),
        K.gaf: ((r, d), BF),
        K.cgo: ((r, d), F32),
        K.dcqkv: ((r, 3 * d), F32),
        K.dcq: ((r, d), BF),
        K.dckv: ((r, 2 * d), BF),
        K.dm: ((r, d), F32),
        K.dmid: ((r, d), F32),
        K.gl: ((plan.total, f), BF),
        K.gr: ((plan.total, f + d), BF),
        K.gsums: ((8, f + d), F32),
        K.small: (small_shape(plan), F32),
        K.gnat: ((2, 16, d // 16, d) if plan.halving else (2, d, d), BF),
        K.gnat_tall: ((2, 4, d // 4, d), BF),
        K.gout: ((2, 2, 8, d // 16, d), BF),
        K.gout_tall: ((2, 2, 2, d // 4, d), BF),
        K.rdr: ((plan.total, d), F32),
        K.rb: ((plan.total, d), BF),
        K.rkv: ((plan.total, 2 * d), BF),
    }
    return w


def chunk_shape(plan, height, breadth):
    if not plan.halving:
        return (height, breadth), BF
    if height == plan.width:
        return (8, height // 16, breadth), BF
    return (2, 2, 2, height // 16, breadth), BF


def chunk_state(name, height, breadth):
    def size(plan, amount):
        return plan.hidden if amount is None else amount * plan.width

    def main(plan):
        return chunk_shape(plan, size(plan, height), size(plan, breadth))

    def sums(plan):
        return (8, size(plan, breadth)), F32

    return {name: main, SENT[name]: main, SUMS[name]: sums}


STATE = {
    K.n: lambda p: ((p.total, p.width), BF),
    K.o: lambda p: ((p.total, p.width), BF),
    K.n2: lambda p: ((p.total, p.width), BF),
    K.a: lambda p: ((p.total, p.hidden), BF),
    K.layer_out: lambda p: ((p.total, p.width), F32),
    K.qkv: lambda p: ((p.total, 3 * p.width), F32),
    K.p: lambda p: ((p.batches * PAIRS, p.slots, 2 * p.slots), BF),
    K.h: lambda p: ((p.total, p.width), F32),
    K.gp: lambda p: ((p.total, p.hidden), BF),
    K.ckv: lambda p: ((p.total, 2 * p.width), BF),
    K.gbr: lambda p: ((p.total, p.width), BF),
    K.du: lambda p: ((p.total, p.hidden), BF),
    K.gm: lambda p: ((p.total, p.width), BF),
    K.dqkv: lambda p: ((p.total, 3 * p.width), BF),
    K.input_grads: lambda p: ((p.total, p.width), F32),
    K.m: lambda p: ((p.total, p.width), BF),
    K.co: lambda p: ((p.total, p.width), BF),
    K.gaf: lambda p: ((p.total, p.width), BF),
    K.dcq: lambda p: ((p.total, p.width), BF),
    K.dckv: lambda p: ((p.total, 2 * p.width), BF),
    K.between: lambda p: ((p.rows, p.width), F32),
    K.send: lambda p: ((p.rows, p.width), BF),
    K.ln: lambda p: ((8, p.width), F32),
    K.small: lambda p: (small_shape(p), F32),
    **chunk_state(K.cross, 1, 4),
    **chunk_state(K.fc2, None, 1),
    **chunk_state(K.fc1, 1, 5),
    **chunk_state(K.attn, 1, 3),
}

FORWARD_0 = Job(
    reads=(K.streams,),
    writes=(K.n, K.o, K.n2, K.a, K.layer_out, K.qkv, K.p, K.h, K.gp, K.send),
    weights=(K.wqkv, K.wout, K.wfc1, K.wfc2),
    scratch=(K.xb, K.x, K.n, K.qkv, K.p, K.dist, K.heard, K.o, K.h, K.n2, K.u, K.a, K.gp, K.y, K.yout, K.ysend),
)
RADAR = Job(reads=(K.streams,), writes=(K.ckv,), weights=(K.wcqkv,), scratch=[K.rb, K.rkv])
MERGED = Job(
    reads=(K.received, K.cotangent, K.ckv),
    writes=(K.n, K.o, K.n2, K.a, K.layer_out, K.gbr, K.du, K.gm, K.dqkv, K.m, K.co, K.gaf, K.dcq, K.dckv, K.send, K.ln),
    weights=WEIGHT_NAMES,
    scratch=(K.xb, K.x, K.n, K.qkv, K.p, K.dist, K.heard, K.o, K.h, K.n2, K.u, K.a, K.gp, K.y, K.yout, K.gin, K.g, K.gbr, K.du, K.dn, K.dh, K.gm, K.go, K.dqkv, K.dqkvb, K.dxb, K.ln, K.cdist, K.m, K.cq, K.ckvb, K.ckv, K.cp, K.cheard, K.co, K.h2, K.gaf, K.cgo, K.dcqkv, K.dcq, K.dckv, K.dm, K.dmid,),
)
BACKWARD_0 = Job(
    reads=(K.streams, K.returned, K.qkv, K.p, K.h, K.gp),
    writes=(K.gbr, K.du, K.gm, K.dqkv, K.input_grads, K.ln),
    weights=(K.wfc2, K.wfc1, K.wout, K.wqkv),
    scratch=(K.xb, K.x, K.qkv, K.p, K.h, K.gp, K.gin, K.g, K.gbr, K.du, K.dn, K.dh, K.gm, K.go, K.dqkv, K.dqkvb, K.dx, K.ln),
)
BACKWARD_MLP = Job(
    reads=(K.returned, K.gp, K.h),
    writes=(K.du, K.gm, K.between, K.ln),
    weights=(K.wfc2, K.wfc1),
    scratch=(K.h, K.gp, K.gin, K.g, K.gbr, K.du, K.dn, K.dh, K.gm, K.ln),
)
BACKWARD_SELF = Job(
    reads=(K.between, K.streams, K.qkv, K.p),
    writes=(K.dqkv, K.input_grads, K.ln),
    weights=(K.wout, K.wqkv),
    scratch=(K.xb, K.x, K.qkv, K.p, K.dn, K.dh, K.gm, K.go, K.dqkv, K.dqkvb, K.dx, K.ln),
)
RADAR_BACK = Job(
    reads=(K.dckv,), writes=(K.input_grads,), weights=(K.wcqkv,), scratch=(K.rkv, K.rdr)
)
GRAD_SCRATCH = (K.gl, K.gr, K.gnat, K.gout, K.gsums)
GRADS_CROSS = Job(
    reads=(K.m, K.streams, K.co, K.dcq, K.dckv, K.gaf),
    writes=(K.cross, K.cross_send, K.cross_sums),
    weights=(),
    scratch=GRAD_SCRATCH,
)
GRADS_FC2 = Job(
    reads=(K.a, K.gbr, K.returned),
    writes=(K.fc2, K.fc2_send, K.fc2_sums),
    weights=(),
    scratch=(K.gl, K.gr, K.gnat, K.gnat_tall, K.gout_tall, K.gsums, K.gin, K.dn, K.g),
)
GRADS_FC1 = Job(
    reads=(K.n2, K.o, K.du, K.gm),
    writes=(K.fc1, K.fc1_send, K.fc1_sums),
    weights=(),
    scratch=GRAD_SCRATCH,
)
GRADS_ATTN = Job(
    reads=(K.n, K.dqkv, K.fc1_sums, K.fc2_sums, K.cross_sums),
    writes=(K.attn, K.attn_send, K.attn_sums, K.small),
    weights=(),
    scratch=GRAD_SCRATCH + (K.small,),
)
GRADS_EARLY = Job(
    reads=(K.a, K.gbr),
    writes=(K.fc2, K.fc2_send, K.fc2_sums),
    weights=(),
    scratch=(K.gl, K.gr, K.gnat, K.gnat_tall, K.gout_tall, K.gsums),
)
GRADS_LATE = Job(*(tuple(dict.fromkeys(one + two)) for one, two in zip(GRADS_CROSS, GRADS_FC1)))
JOBS = {
    K.forward: FORWARD_0,
    K.radar: RADAR,
    K.merged: MERGED,
    K.backward: BACKWARD_0,
    K.backward_mlp: BACKWARD_MLP,
    K.backward_self: BACKWARD_SELF,
    K.radar_back: RADAR_BACK,
    K.grads_cross: GRADS_CROSS,
    K.grads_fc2: GRADS_FC2,
    K.grads_fc1: GRADS_FC1,
    K.grads_attn: GRADS_ATTN,
    K.grads_early: GRADS_EARLY,
    K.grads_late: GRADS_LATE,
}
TILE = 768


def tiles(extent, tile=TILE):
    return [slice(at, min(at + tile, extent)) for at in range(0, extent, tile)]


def self_forward(plan, r, s, c, k, waits, save):
    d = plan.width
    rows = pl.ds(k * plan.rows, plan.rows)
    out = []
    gain, shift, bias = r[K.gains], r[K.shifts], r[K.attn_bias]
    norm_forward(s[K.x], gain[:, :d], shift[:, :d], s[K.n])
    out.append(c.start(s[K.n], r[K.n].at[rows]))
    waits[K.wqkv].wait()
    normed = s[K.n][...]
    s[K.qkv][:, :d] = (dot_nn(normed, s[K.wqkv][:, :d]) + bias[:, :d]).astype(BF).astype(F32) * SCORE_SCALE
    s[K.qkv][:, d : 2 * d] = dot_nn(normed, s[K.wqkv][:, d : 2 * d])
    s[K.qkv][:, 2 * d :] = dot_nn(normed, s[K.wqkv][:, 2 * d :]) + bias[:, d : 2 * d]
    if save:
        out.append(c.start(s[K.qkv], r[K.qkv].at[rows]))
    attend(
        plan,
        most_live(plan, r, k, (K.counts,)),
        (s[K.qkv], 0),
        (s[K.qkv], d),
        (s[K.qkv], 2 * d),
        Spread(plan, r, s[K.dist], k, K.positions, K.counts),
        r[K.slopes],
        s[K.heard],
        s[K.p],
    )
    if save:
        out.append(c.start(s[K.p], r[K.p].at[pl.ds(k * plan.per * PAIRS, plan.per * PAIRS)]))
    s[K.o][...] = s[K.heard][...].astype(BF)
    out.append(c.start(s[K.o], r[K.o].at[rows]))
    waits[K.wout].wait()
    s[K.h][...] = s[K.x][...] + dot_nn(s[K.o][...], s[K.wout][...]) + bias[:, 2 * d :]
    if save:
        out.append(c.start(s[K.h], r[K.h].at[rows]))
    return out


def mlp_forward(plan, r, s, c, k, waits, after, save):
    d, f = plan.width, plan.hidden
    rows = pl.ds(k * plan.rows, plan.rows)
    out = []
    norm_forward(after, r[K.gains][:, d:], r[K.shifts][:, d:], s[K.n2])
    out.append(c.start(s[K.n2], r[K.n2].at[rows]))
    waits[K.wfc1].wait()
    bias = r[K.mlp_bias]
    for tile in tiles(f):
        s[K.u][:, tile] = dot_nn(s[K.n2][...], s[K.wfc1][:, tile]) + bias[:, tile]
        for span in spans(plan.rows):
            active, slope = gelu_both(s[K.u][span, tile])
            s[K.a][span, tile] = active.astype(BF)
            s[K.gp][span, tile] = slope.astype(BF)
    out.append(c.start(s[K.a], r[K.a].at[rows]))
    if save:
        out.append(c.start(s[K.gp], r[K.gp].at[rows]))
    waits[K.wfc2].wait()
    s[K.y][...] = after[...] + dot_nn(s[K.a][...], s[K.wfc2][...]) + bias[:, f:]
    fill_rows(s[K.yout], plan.per, plan.slots, r[K.counts], k * plan.per, s[K.y])
    out.append(c.start(s[K.yout], r[K.layer_out].at[rows]))
    return out


def mlp_backward(plan, r, s, c, k, waits, after, target):
    d, f = plan.width, plan.hidden
    rows = pl.ds(k * plan.rows, plan.rows)
    out = []
    s[K.dn][...] = s[K.gin][...].astype(F32)
    fill_rows(s[K.g], plan.per, plan.slots, r[K.counts], k * plan.per, s[K.dn])
    s[K.gbr][...] = s[K.g][...].astype(BF)
    if K.gbr in r:
        out.append(c.start(s[K.gbr], r[K.gbr].at[rows]))
    if K.wfc2 in waits:
        waits[K.wfc2].wait()
    for tile in tiles(f):
        grad = dot_nt(s[K.gbr][...], s[K.wfc2][tile, :])
        s[K.du][:, tile] = (grad * s[K.gp][:, tile].astype(F32)).astype(BF)
    out.append(c.start(s[K.du], r[K.du].at[rows]))
    if K.wfc1 in waits:
        waits[K.wfc1].wait()
    s[K.dn][...] = dot_nt(s[K.du][...], s[K.wfc1][...])
    sums = norm_backward(after, r[K.gains][:, d:], s[K.dn], s[K.g], target)
    return out, sums


def self_backward(plan, r, s, c, k, waits, grad, target):
    d = plan.width
    rows = pl.ds(k * plan.rows, plan.rows)
    out = []
    s[K.gm][...] = grad[...].astype(BF)
    if K.gm in r:
        out.append(c.start(s[K.gm], r[K.gm].at[rows]))
    if K.wout in waits:
        waits[K.wout].wait()
    s[K.go][...] = dot_nt(s[K.gm][...], s[K.wout][...])
    attend_back(
        plan,
        most_live(plan, r, k, (K.counts,)),
        (s[K.qkv], 0),
        (s[K.qkv], d),
        (s[K.qkv], 2 * d),
        s[K.go],
        s[K.p],
        [(s[K.dqkv], part * d) for part in range(3)],
    )
    s[K.dqkvb][...] = s[K.dqkv][...].astype(BF)
    out.append(c.start(s[K.dqkvb], r[K.dqkv].at[rows]))
    if K.wqkv in waits:
        waits[K.wqkv].wait()
    s[K.dn][...] = dot_nt(s[K.dqkvb][...], s[K.wqkv][...])
    sums = norm_backward(s[K.x], r[K.gains][:, :d], s[K.dn], grad, target)
    return out, sums


def write_sums(s, c, r, parts):
    s[K.ln][...] = jnp.zeros_like(s[K.ln])
    for at, part in enumerate(parts):
        s[K.ln][at : at + 1, :] = part
    return c.start(s[K.ln], r[K.ln])


def start_weights(r, s, c, names):
    return {name: c.start(r[name], s[name]) for name in names}


def run_forward(plan, r, s, c, k):
    rows = pl.ds(k * plan.rows, plan.rows)
    arrive = c.start(r[K.streams].at[rows], s[K.xb])
    waits = start_weights(r, s, c, FORWARD_0.weights)
    arrive.wait()
    s[K.x][...] = s[K.xb][...].astype(F32)
    out = self_forward(plan, r, s, c, k, waits, True)
    out += mlp_forward(plan, r, s, c, k, waits, s[K.h], True)
    s[K.ysend][...] = s[K.yout][...].astype(BF)
    out.append(c.start(s[K.ysend], r[K.send]))
    for copy in out:
        copy.wait()


def run_radar(plan, r, s, c, k):
    d = plan.width
    arrive = c.start(r[K.streams], s[K.rb])
    weight = c.start(r[K.wcqkv], s[K.wcqkv])
    arrive.wait()
    weight.wait()
    s[K.rkv][:, :d] = dot_nn(s[K.rb][...], s[K.wcqkv][:, d : 2 * d]).astype(BF)
    s[K.rkv][:, d:] = (
        dot_nn(s[K.rb][...], s[K.wcqkv][:, 2 * d :]) + r[K.cross_bias][:, d : 2 * d]
    ).astype(BF)
    c.start(s[K.rkv], r[K.ckv]).wait()


def run_merged(plan, r, s, c, k):
    plan = plan.unrolled(3)
    d = plan.width
    rows = pl.ds(k * plan.rows, plan.rows)
    arrive = c.start(r[K.received], s[K.xb])
    waits = start_weights(r, s, c, (K.wqkv, K.wout, K.wcqkv, K.wcout, K.wfc1, K.wfc2))
    arrive_kv = c.start(r[K.ckv].at[rows], s[K.ckvb])
    arrive_grad = c.start(r[K.cotangent].at[rows], s[K.gin])
    arrive.wait()
    s[K.x][...] = s[K.xb][...].astype(F32)
    out = self_forward(plan, r, s, c, k, waits, False)
    bias = r[K.cross_bias]
    norm_forward(s[K.h], r[K.cross_gain][...], bias[:, 3 * d :], s[K.m])
    out.append(c.start(s[K.m], r[K.m].at[rows]))
    waits[K.wcqkv].wait()
    s[K.cq][...] = (dot_nn(s[K.m][...], s[K.wcqkv][:, :d]) + bias[:, :d]).astype(BF).astype(F32) * SCORE_SCALE
    arrive_kv.wait()
    s[K.ckv][...] = s[K.ckvb][...].astype(F32)
    live = most_live(plan, r, k, (K.counts, K.radar_counts))
    attend(
        plan,
        live,
        (s[K.cq], 0),
        (s[K.ckv], 0),
        (s[K.ckv], d),
        Spread(plan, r, s[K.cdist], k, K.radar_positions, K.radar_counts),
        r[K.slopes],
        s[K.cheard],
        s[K.cp],
    )
    s[K.co][...] = s[K.cheard][...].astype(BF)
    out.append(c.start(s[K.co], r[K.co].at[rows]))
    waits[K.wcout].wait()
    s[K.h2][...] = s[K.h][...] + dot_nn(s[K.co][...], s[K.wcout][...]) + bias[:, 2 * d : 3 * d]
    out += mlp_forward(plan, r, s, c, k, waits, s[K.h2], False)
    arrive_grad.wait()
    more, sums_two = mlp_backward(plan, r, s, c, k, {}, s[K.h2], s[K.dh])
    out += more
    s[K.gaf][...] = s[K.dh][...].astype(BF)
    out.append(c.start(s[K.gaf], r[K.gaf].at[rows]))
    s[K.cgo][...] = dot_nt(s[K.gaf][...], s[K.wcout][...])
    attend_back(
        plan,
        live,
        (s[K.cq], 0),
        (s[K.ckv], 0),
        (s[K.ckv], d),
        s[K.cgo],
        s[K.cp],
        [(s[K.dcqkv], part * d) for part in range(3)],
    )
    s[K.dcq][...] = s[K.dcqkv][:, :d].astype(BF)
    s[K.dckv][...] = s[K.dcqkv][:, d:].astype(BF)
    out.append(c.start(s[K.dcq], r[K.dcq].at[rows]))
    out.append(c.start(s[K.dckv], r[K.dckv].at[rows]))
    s[K.dm][...] = dot_nt(s[K.dcq][...], s[K.wcqkv][:, :d])
    sums_cross = norm_backward(s[K.h], r[K.cross_gain][...], s[K.dm], s[K.dh], s[K.dmid])
    more, sums_one = self_backward(plan, r, s, c, k, {}, s[K.dmid], s[K.dh])
    out += more
    s[K.dxb][...] = s[K.dh][...].astype(BF)
    out.append(c.start(s[K.dxb], r[K.send]))
    out.append(write_sums(s, c, r, sums_one + sums_two + sums_cross))
    for copy in out:
        copy.wait()


def load_mlp_back(plan, r, s, c, k):
    rows = pl.ds(k * plan.rows, plan.rows)
    arrive = [c.start(r[K.returned], s[K.gin])]
    waits = start_weights(r, s, c, (K.wfc2,))
    arrive.append(c.start(r[K.gp].at[rows], s[K.gp]))
    waits.update(start_weights(r, s, c, (K.wfc1,)))
    arrive.append(c.start(r[K.h].at[rows], s[K.h]))
    return arrive, waits


def load_self_back(plan, r, s, c, k):
    rows = pl.ds(k * plan.rows, plan.rows)
    waits = start_weights(r, s, c, (K.wout,))
    arrive = [
        c.start(r[K.qkv].at[rows], s[K.qkv]),
        c.start(r[K.p].at[pl.ds(k * plan.per * PAIRS, plan.per * PAIRS)], s[K.p]),
    ]
    waits.update(start_weights(r, s, c, (K.wqkv,)))
    arrive.append(c.start(r[K.streams].at[rows], s[K.xb]))
    return arrive, waits


def wait_all(copies):
    for copy in copies:
        copy.wait()


def run_backward(plan, r, s, c, k):
    rows = pl.ds(k * plan.rows, plan.rows)
    arrive, waits = load_mlp_back(plan, r, s, c, k)
    arrive_self, waits_self = load_self_back(plan, r, s, c, k)
    waits.update(waits_self)
    wait_all(arrive)
    out, sums_two = mlp_backward(plan, r, s, c, k, waits, s[K.h], s[K.dh])
    wait_all(arrive_self)
    s[K.x][...] = s[K.xb][...].astype(F32)
    more, sums_one = self_backward(plan, r, s, c, k, waits, s[K.dh], s[K.dx])
    out += more
    out.append(c.start(s[K.dx], r[K.input_grads].at[rows]))
    out.append(write_sums(s, c, r, sums_one + sums_two))
    wait_all(out)


def run_backward_mlp(plan, r, s, c, k):
    arrive, waits = load_mlp_back(plan, r, s, c, k)
    wait_all(arrive)
    out, sums_two = mlp_backward(plan, r, s, c, k, waits, s[K.h], s[K.dh])
    out.append(c.start(s[K.dh], r[K.between]))
    s[K.gm][...] = s[K.dh][...].astype(BF)
    out.append(c.start(s[K.gm], r[K.gm].at[pl.ds(k * plan.rows, plan.rows)]))
    nothing = jnp.zeros_like(sums_two[0])
    out.append(write_sums(s, c, r, (nothing, nothing) + sums_two))
    wait_all(out)


def run_backward_self(plan, r, s, c, k):
    rows = pl.ds(k * plan.rows, plan.rows)
    arrive = [c.start(r[K.between], s[K.dh])]
    more, waits = load_self_back(plan, r, s, c, k)
    wait_all(arrive + more)
    s[K.x][...] = s[K.xb][...].astype(F32)
    out, sums_one = self_backward(plan, r, s, c, k, waits, s[K.dh], s[K.dx])
    out.append(c.start(s[K.dx], r[K.input_grads].at[rows]))
    out.append(write_sums(s, c, r, sums_one))
    wait_all(out)


def run_radar_back(plan, r, s, c, k):
    d = plan.width
    arrive = c.start(r[K.dckv], s[K.rkv])
    weight = c.start(r[K.wcqkv], s[K.wcqkv])
    arrive.wait()
    weight.wait()
    s[K.rdr][...] = dot_nt(s[K.rkv][...], s[K.wcqkv][:, d:])
    c.start(s[K.rdr], r[K.input_grads]).wait()


def slot_of(relative):
    return ((relative >> 1) & 1) * 4 + ((relative >> 2) & 1) * 2 + ((relative >> 3) & 1)


def weight_grads(plan, r, s, c, lefts, rights, left_of, tall, name, fix=None):
    d, total = plan.width, plan.total

    def blocks(buffer, names):
        found = []
        for array in names:
            for tile in tiles(r[array].shape[1], d):
                at = len(found) * d
                found.append((r[array].at[:, tile], buffer.at[:, at : at + d]))
        return found

    left_blocks, right_blocks = blocks(s[K.gl], lefts), blocks(s[K.gr], rights)
    count = max(len(left_blocks), len(right_blocks))
    loads, seen = [], set()
    for t in range(count):
        wanted = [(0, 0 if tall else t), (1, left_of(t))]
        fresh = [key for key in wanted if key not in seen]
        seen.update(fresh)
        loads.append([c.start(*(right_blocks, left_blocks)[side][at]) for side, at in fresh])
    if fix is not None:
        wait_all(loads[0])
        loads[0] = []
        fix()
    mine = r[K.device][0]
    block = d // 4 if tall else d // 16
    natural = s[K.gnat_tall if tall and plan.halving else K.gnat]
    gout = s[K.gout_tall if tall else K.gout] if plan.halving else None
    sems = c.reserve(4)

    def columns(at):
        return pl.ds(pl.multiple_of(at * d, LANES), d)

    def copies_out(t):
        slot = lax.rem(t, 2)
        found = []
        for sent in range(2 if plan.halving else 1):
            ref = r[SENT[name] if sent else name]
            if not plan.halving:
                target = ref.at[columns(t), :] if tall else ref.at[:, columns(t)]
                source = natural.at[slot]
            elif tall:
                away = t ^ (mine >> 2)
                target, source = ref.at[:, away & 1, away >> 1], gout.at[slot, sent]
            else:
                target, source = ref.at[:, :, columns(t)], gout.at[slot, sent]
            found.append(pltpu.make_async_copy(source, target, sems(slot * 2 + sent)))
        return found

    def wait_out(t):
        wait_all(copies_out(t))

    def hand_on(t):
        for one in copies_out(t):
            one.start()

    def arrange(slot):
        if tall:
            for relative in range(4):
                gout[slot, relative & 1, relative >> 1] = natural[slot, (mine & 3) ^ relative]
        else:
            for relative in range(16):
                gout[slot, relative & 1, slot_of(relative)] = natural[slot, mine ^ relative]

    behind = 1 if plan.halving else 0

    def step(t, carry):
        for at, found in enumerate(loads):
            if found:
                pl.when(t == at)(lambda found=found: wait_all(found))
        pl.when(t >= 2 + behind)(lambda: wait_out(t - 2 - behind))
        slot = lax.rem(t, 2)
        grad = s[K.gr][:, columns(0 if tall else t)]
        low = dot_tn(s[K.gl][:, columns(left_of(t))], grad).astype(BF)
        if plan.halving:
            for part in range(d // block):
                natural[slot, part] = low[part * block : (part + 1) * block]
            arrange(1 - slot)
        else:
            natural[slot] = low
        sums = jnp.sum(grad.astype(F32).reshape(total // 8, 8, d), axis=0)
        s[K.gsums][:, columns(0 if tall else t)] = sums
        pl.when(t >= behind)(lambda: hand_on(t - behind))
        return carry

    lax.fori_loop(0, count, step, 0)
    if plan.halving:
        wait_out(count - 3)
        arrange((count - 1) % 2)
        hand_on(count - 1)
    breadth = len(right_blocks) * d
    last = c.start(s[K.gsums].at[:, :breadth], r[SUMS[name]])
    wait_out(count - 2)
    wait_out(count - 1)
    last.wait()


def run_grads_cross(plan, r, s, c, k):
    weight_grads(
        plan, r, s, c, (K.m, K.streams, K.co), (K.dcq, K.dckv, K.gaf),
        lambda t: (t + 1) // 2, False, K.cross,
    )


def run_grads_fc2(plan, r, s, c, k):
    last = plan.steps - 1
    arrive = c.start(r[K.returned], s[K.gin])

    def fix():
        arrive.wait()

        @pl.when(r[K.section][0] == 0)
        def _():
            s[K.dn][...] = s[K.gin][...].astype(F32)
            fill_rows(s[K.g], plan.per, plan.slots, r[K.counts], last * plan.per, s[K.dn])
            s[K.gr][last * plan.rows :, : plan.width] = s[K.g][...].astype(BF)

    weight_grads(plan, r, s, c, (K.a,), (K.gbr,), lambda t: t, True, K.fc2, fix)


def run_grads_fc1(plan, r, s, c, k):
    last = plan.hidden // plan.width
    weight_grads(plan, r, s, c, (K.n2, K.o), (K.du, K.gm), lambda t: t // last, False, K.fc1)


def run_grads_early(plan, r, s, c, k):
    weight_grads(plan, r, s, c, (K.a,), (K.gbr,), lambda t: t, True, K.fc2)


def run_grads_late(plan, r, s, c, k):
    run_grads_cross(plan, r, s, c, k)
    run_grads_fc1(plan, r, s, c, k)


def run_grads_attn(plan, r, s, c, k):
    weight_grads(plan, r, s, c, (K.n,), (K.dqkv,), lambda t: 0 * t, False, K.attn)
    d = plan.width
    first = sum(r[name][...] for name in r if name in FIRST)
    second = sum(r[name][...] for name in r if name in SECOND)
    norms = jnp.where(r[K.section][0] == 0, first, second)
    ratio = plan.hidden // d

    def column(ref, at):
        return jnp.sum(ref[:, at * d : (at + 1) * d], axis=0, keepdims=True)

    rows = [column(s[K.gsums], 0), column(s[K.gsums], 2), column(r[K.fc1_sums], ratio)]
    rows += [column(r[K.fc1_sums], at) for at in range(ratio)] + [column(r[K.fc2_sums], 0)]
    rows += [norms[0:1], norms[2:3], norms[1:2], norms[3:4], norms[4:5]]
    rows += [column(r[K.cross_sums], at) for at in (0, 2, 3)] + [norms[5:6]]
    s[K.small][...] = jnp.zeros_like(s[K.small])
    for at, row in enumerate(rows):
        s[K.small][at : at + 1, :] = row
    c.start(s[K.small], r[K.small]).wait()


RUN = {
    K.forward: run_forward,
    K.radar: run_radar,
    K.merged: run_merged,
    K.backward: run_backward,
    K.backward_mlp: run_backward_mlp,
    K.backward_self: run_backward_self,
    K.radar_back: run_radar_back,
    K.grads_cross: run_grads_cross,
    K.grads_fc2: run_grads_fc2,
    K.grads_fc1: run_grads_fc1,
    K.grads_attn: run_grads_attn,
    K.grads_early: run_grads_early,
    K.grads_late: run_grads_late,
}


def phase(plan, fixed, state, weights, first, second, after=()):
    jobs = [job for job in (first, second) if job is not None]
    shared = len(jobs) == 2 and jobs[0][0] == jobs[1][0]
    kinds = [JOBS[job[0]] for job in jobs]
    taken = {}
    for job in jobs:
        taken.update(job[2])
    writes = []
    for kind in kinds:
        writes += [name for name in kind.writes if name not in writes]
    reads = []
    for kind in kinds:
        for name in kind.reads:
            if name in state and name not in reads and name not in writes:
                reads.append(name)
            elif name in (K.streams, K.cotangent):
                taken[name] = fixed[name]
    used = [name for name in WEIGHT_NAMES if any(name in kind.weights for kind in kinds)]
    fresh = [name for name in writes if name not in state or name in (K.send, K.ln)]
    kept = [name for name in writes if name not in fresh]
    small = [name for name in fixed if name not in (K.streams, K.cotangent)]
    if all(job[0] in GRAD_JOBS for job in jobs):
        small = [K.section, K.device, K.counts]
    elif not any(job[0] in (K.radar, K.merged) for job in jobs):
        small = [name for name in small if name not in (K.cross_gain, K.cross_bias)]
    every = scratch_shapes(plan)
    need = list(used)
    for kind in kinds:
        need += [name for name in kind.scratch if name not in need]

    operands, specs, names = [], [], []
    for name in small:
        operands.append(fixed[name])
        specs.append(SM if name in (K.section, K.device, K.counts, K.radar_counts, K.slopes) else VM)
        names.append(name)
    for name in used:
        operands.append(weights[name])
        specs.append(ANY)
        names.append(name)
    for name, array in list(taken.items()) + [(name, state[name]) for name in reads]:
        operands.append(array)
        specs.append(VM if name in IN_VMEM else ANY)
        names.append(name)
    operands += after
    specs += [ANY] * len(after)
    names += [None] * len(after)
    alias = {}
    for at, name in enumerate(kept):
        alias[len(operands)] = at
        operands.append(state[name])
        specs.append(ANY)
        names.append(None)
    outs = kept + fresh
    shapes = [jax.ShapeDtypeStruct(*STATE[name](plan)) for name in outs]

    def kernel(*refs):
        r, s = {}, {}
        for name, ref in zip(names, refs):
            if name is not None:
                r[name] = ref
        refs = refs[len(names) :]
        for name, ref in zip(outs, refs):
            r[name] = ref
        refs = refs[len(outs) :]
        for name, ref in zip(need, refs):
            s[name] = ref
        sems = refs[len(need)]
        if shared:
            RUN[first[0]](plan, r, s, Copies(sems), first[1])
            return
        for which, job in ((0, first), (1, second)):
            if job is not None:

                @pl.when(r[K.section][0] == which)
                def _():
                    RUN[job[0]](plan, r, s, Copies(sems), job[1])

    results = pl.pallas_call(
        kernel,
        out_shape=shapes,
        in_specs=specs,
        out_specs=[ANY] * len(outs),
        scratch_shapes=[pltpu.VMEM(*every[name]) for name in need] + [pltpu.SemaphoreType.DMA((32,))],
        input_output_aliases=alias,
        compiler_params=pltpu.CompilerParams(vmem_limit_bytes=VMEM_LIMIT),
        cost_estimate=CHEAP,
        name="_".join(job[0].name + str(job[1]) for job in jobs),
    )(*operands)
    new = dict(zip(outs, results))
    for name in outs:
        if name not in (K.send, K.ln):
            state[name] = new[name]
    return new.get(K.send), new.get(K.ln)


def body(
    streams,
    cotangent,
    counts,
    positions,
    radar_counts,
    radar_positions,
    qkv_weight,
    out_weight,
    fc1_weight,
    fc2_weight,
    attn_bias,
    mlp_bias,
    norm_gains,
    norm_shifts,
    cross_qkv_weight,
    cross_out_weight,
    cross_gain,
    cross_bias,
):
    devices = lax.axis_size(BATCH)
    section_id = lax.axis_index(SECTION)
    me = lax.axis_index(BATCH)
    width = cotangent.shape[1]
    hidden = fc1_weight.shape[2]
    halving = devices == 16
    plan = Plan(counts.shape[0], positions.shape[1], width, hidden, halving)
    device = me.astype(jnp.int32).reshape(1)
    section = section_id.astype(jnp.int32).reshape(1)
    head_slopes = [2.0 ** (-8.0 * (head + 1.0) / H) for head in range(H)]
    fixed = {
        K.section: section,
        K.device: device,
        K.counts: counts,
        K.radar_counts: radar_counts,
        K.slopes: jnp.array(head_slopes, F32),
        K.positions: positions,
        K.radar_positions: radar_positions,
        K.attn_bias: attn_bias,
        K.mlp_bias: mlp_bias,
        K.gains: norm_gains,
        K.shifts: norm_shifts,
        K.cross_gain: cross_gain.reshape(1, width),
        K.cross_bias: cross_bias.reshape(1, 4 * width),
        K.streams: streams[0],
        K.cotangent: cotangent,
    }
    weights = dict(
        zip(
            WEIGHT_NAMES,
            (
                qkv_weight[0],
                out_weight[0],
                fc1_weight[0],
                fc2_weight[0],
                cross_qkv_weight,
                cross_out_weight,
            ),
        )
    )
    state = {}
    steps = plan.steps
    arrived = []
    for k in range(steps):
        second = (K.radar, 0, {}) if k == min(1, steps - 1) else None
        send, _ = phase(plan, fixed, state, weights, (K.forward, k, {}), second)
        arrived.append(lax.ppermute(send, SECTION, [(0, 1)]))
    returned, first_sums, second_sums = [], [], []
    for k in range(steps):
        send, sums = phase(
            plan, fixed, state, weights, None, (K.merged, k, {K.received: arrived[k]})
        )
        second_sums.append(sums)
        returned.append(lax.ppermute(send, SECTION, [(1, 0)]))
        if 0 < k < steps - 1:
            _, sums = phase(
                plan, fixed, state, weights, (K.backward, k - 1, {K.returned: returned[k - 1]}), None
            )
            first_sums.append(sums)

    route = {bit: [(at, at ^ bit) for at in range(devices)] for bit in (1, 2, 4, 8, 12)} if halving else {}

    def trade(block, bit):
        return lax.ppermute(block, BATCH, route[bit])

    def trade_second(block, bit):
        pairs = [(devices + left, devices + right) for left, right in route[bit]]
        return lax.ppermute(block, (SECTION, BATCH), pairs)

    is_first = section_id == 0

    def to_both(block):
        return jnp.where(is_first, lax.ppermute(block, SECTION, [(1, 0)]), block).astype(F32)

    def scatter(part):
        return lax.psum_scatter(part, BATCH, scatter_dimension=0, tiled=True).astype(F32)

    def run(first, second, after=()):
        _, sums = phase(plan, fixed, state, weights, first, second, after=list(after))
        if first is not None and first[0] in BACK_JOBS:
            first_sums.append(sums)

    def both(job, taken, after=()):
        run((job, 0, taken), (job, 0, taken), after)

    def add_up(parts, low, high):
        return sum(part[low:high].astype(F32) for part in parts)

    def begin(name, exchange, pieces=1):
        kept, sent = state[name], state[SENT[name]]
        kept, sent = (x.reshape(8, -1, x.shape[-1]) for x in (kept, sent))
        come = [exchange(piece, 1) for piece in jnp.split(sent, pieces)]
        return [kept, jnp.concatenate(come) if pieces > 1 else come[0]]

    def step(parts, exchange, bit):
        half = parts[-1].shape[0] // 2
        return parts + [exchange(add_up(parts, half, 2 * half).astype(BF), bit)]

    def along_z(parts):
        return [add_up(parts, at, at + 1).astype(BF) for at in (1, 2, 3)]

    def come_along_z(parts, sends, exchange):
        come = [exchange(part, bit) for part, bit in zip(sends, (8, 4, 12))]
        return [part[:1] for part in parts] + come

    def spread(parts, exchange):
        return come_along_z(parts, along_z(parts), exchange)

    def total(parts):
        return add_up(parts, 0, 1)[0]

    def taken_sums():
        return dict(zip(FIRST, first_sums)) | dict(zip(SECOND, second_sums))

    def once(*arrays):
        return lax.optimization_barrier(arrays)

    last = steps - 1
    queue = [(K.backward, k, {K.returned: returned[k]}) for k in range(max(last - 1, 0), last)] or [None]
    for job in queue[:-1]:
        run(job, None)
    run(queue[-1], (K.grads_early, 0, {}))
    if halving:
        taken = {K.returned: returned[last]}
        run((K.grads_fc2, 0, taken), None)
        fc2 = step(begin(K.fc2, trade), trade, 2)
        run((K.backward_mlp, last, taken), (K.grads_late, 0, {}), [fc2[1]])
        cross = begin(K.cross, trade_second)
        half = cross[0].shape[-1] // 2
        pair_sum = add_up(cross, 0, 8).astype(BF)
        mine, theirs = pair_sum[..., :half], pair_sum[..., half:]
        theirs = lax.ppermute(theirs, SECTION, [(1, 0)])
        run((K.grads_fc1, 0, {}), None)
        state[K.fc1], state[K.fc1_send], fc2[-1] = once(
            state[K.fc1], state[K.fc1_send], fc2[-1]
        )
        fc1 = begin(K.fc1, trade)
        fc2 = spread(fc2, trade)
        run((K.backward_self, last, {}), None, [fc1[-1]])
        fc1 = step(fc1, trade, 2)
        both(K.grads_attn, taken_sums())
        state[K.attn], state[K.attn_send], fc1[-1], theirs, *fc2[-3:] = once(
            state[K.attn], state[K.attn_send], fc1[-1], theirs, *fc2[-3:]
        )
        cross = step([jnp.where(is_first, theirs, mine)], trade, 2)
        attn = begin(K.attn, trade)
        ahead = add_up(attn, 4, 8).astype(BF)
        sends = along_z(fc1)
        ahead, small, *sends = once(ahead, state[K.small], *sends)
        attn.append(trade(ahead, 2))
        fc1 = come_along_z(fc1, sends, trade)
        small = small + trade(small, 1)
        next_small = trade(small, 2)
        run(None, (K.radar_back, 0, {}), [small])
        cross = spread(cross, trade)
        attn[-1], next_small, state[K.input_grads], *rest = once(
            attn[-1], next_small, state[K.input_grads], *fc1[-3:], *cross[-3:]
        )
        fc1[-3:], cross[-3:] = rest[:3], rest[3:]
        small = small + next_small
        attn = spread(attn, trade)
        small = small + sum(trade(small, bit) for bit in (4, 8, 12))
        mine, grad_fc2, grad_fc1, grad_attn = (total(x) for x in (cross, fc2, fc1, attn))
        mine = mine.astype(BF)
        theirs = lax.ppermute(mine, SECTION, [(0, 1), (1, 0)])
        ends = (jnp.where(is_first, theirs, mine), jnp.where(is_first, mine, theirs))
        cross_all = jnp.concatenate(ends, axis=1).astype(F32)
    else:
        taken = {K.returned: returned[last]}
        run((K.grads_fc2, 0, taken), None)
        run((K.backward_mlp, last, taken), (K.grads_late, 0, {}))
        run((K.grads_fc1, 0, {}), None)
        run((K.backward_self, last, {}), None)
        both(K.grads_attn, taken_sums())
        small = lax.psum(state[K.small], BATCH)
        run(None, (K.radar_back, 0, {}))
        cross_share, grad_fc2, grad_fc1, grad_attn = (
            scatter(state[name]) for name in (K.cross, K.fc2, K.fc1, K.attn)
        )
        cross_all = to_both(cross_share.astype(BF))
    split = qkv_weight.shape[2]

    ratio = hidden // width
    edges = [0, 3, 4 + ratio, 6 + ratio, 8 + ratio, 9 + ratio, 13 + ratio]
    cross_small = to_both(small[edges[4] : edges[6]])
    parts = []
    for low, high in zip(edges, edges[1:]):
        rows = small[low:high] if high <= edges[4] else cross_small[low - edges[4] : high - edges[4]]
        size = (high - low) * width // devices
        parts.append(lax.dynamic_slice(rows.reshape(-1), (me * size,), (size,)))
    return (
        state[K.layer_out][None],
        state[K.input_grads][None],
        grad_attn[None],
        grad_fc1[None, :, hidden:],
        grad_fc1[None, :, :hidden],
        grad_fc2[None],
        parts[0][None],
        parts[1][None],
        parts[2][None],
        parts[3][None],
        cross_all[:, :split],
        cross_all[:, split:],
        parts[4],
        parts[5],
    )


def solution(mesh):
    in_specs = (
        P(SECTION, BATCH, None),
        P(BATCH, None),
        P(BATCH),
        P(BATCH, None),
        P(BATCH),
        P(BATCH, None),
        P(SECTION, None, None),
        P(SECTION, None, None),
        P(SECTION, None, None),
        P(SECTION, None, None),
        P(SECTION, None),
        P(SECTION, None),
        P(SECTION, None),
        P(SECTION, None),
        P(),
        P(),
        P(),
        P(),
    )
    out_specs = (
        P(SECTION, BATCH, None),
        P(SECTION, BATCH, None),
        P(SECTION, BATCH, None),
        P(SECTION, BATCH, None),
        P(SECTION, BATCH, None),
        P(SECTION, BATCH, None),
        P(SECTION, BATCH),
        P(SECTION, BATCH),
        P(SECTION, BATCH),
        P(SECTION, BATCH),
        P(BATCH, None),
        P(BATCH, None),
        P(BATCH),
        P(BATCH),
    )
    return jax.shard_map(body, mesh=mesh, in_specs=in_specs, out_specs=out_specs, check_vma=False)
```

```python
import enum
import typing

import jax
import jax.numpy as jnp
from jax import lax
from jax.experimental import pallas as pl
from jax.experimental.pallas import tpu as pltpu
from jax.sharding import PartitionSpec as P

SECTION, BATCH = "section", "batch"
H = 12
HD = 64
PAIRS = H // 2
LANES = 2 * HD
GRID = 15
SCORE_SCALE = 0.125
NORM_EPS = 1e-06
FAR = 1e33
CHUNK = 16
BF = jnp.bfloat16
F32 = jnp.float32
VMEM_LIMIT = 60 << 20
CHEAP = pl.CostEstimate(flops=1, bytes_accessed=1, transcendentals=0)
ANY = pl.BlockSpec(memory_space=pl.ANY)
VM = pl.BlockSpec(memory_space=pltpu.VMEM)
SM = pl.BlockSpec(memory_space=pltpu.SMEM)


class K(enum.Enum):
    a = enum.auto()
    attn = enum.auto()
    attn_bias = enum.auto()
    attn_send = enum.auto()
    attn_sums = enum.auto()
    backward = enum.auto()
    backward_mlp = enum.auto()
    backward_self = enum.auto()
    between = enum.auto()
    cdist = enum.auto()
    cgo = enum.auto()
    cheard = enum.auto()
    ckv = enum.auto()
    ckvb = enum.auto()
    co = enum.auto()
    cotangent = enum.auto()
    counts = enum.auto()
    cp = enum.auto()
    cq = enum.auto()
    cross = enum.auto()
    cross_bias = enum.auto()
    cross_gain = enum.auto()
    cross_send = enum.auto()
    cross_sums = enum.auto()
    dckv = enum.auto()
    dcq = enum.auto()
    dcqkv = enum.auto()
    device = enum.auto()
    dh = enum.auto()
    dist = enum.auto()
    dm = enum.auto()
    dmid = enum.auto()
    dn = enum.auto()
    dqkv = enum.auto()
    dqkvb = enum.auto()
    du = enum.auto()
    dx = enum.auto()
    dxb = enum.auto()
    fc1 = enum.auto()
    fc1_send = enum.auto()
    fc1_sums = enum.auto()
    fc2 = enum.auto()
    fc2_send = enum.auto()
    fc2_sums = enum.auto()
    forward = enum.auto()
    g = enum.auto()
    gaf = enum.auto()
    gains = enum.auto()
    gbr = enum.auto()
    gin = enum.auto()
    gl = enum.auto()
    gm = enum.auto()
    gnat = enum.auto()
    gnat_tall = enum.auto()
    go = enum.auto()
    gout = enum.auto()
    gout_tall = enum.auto()
    gp = enum.auto()
    gr = enum.auto()
    grads_attn = enum.auto()
    grads_cross = enum.auto()
    grads_fc1 = enum.auto()
    grads_fc2 = enum.auto()
    grads_early = enum.auto()
    grads_late = enum.auto()
    gsums = enum.auto()
    h = enum.auto()
    h2 = enum.auto()
    heard = enum.auto()
    input_grads = enum.auto()
    layer_out = enum.auto()
    ln = enum.auto()
    m = enum.auto()
    merged = enum.auto()
    mlp_bias = enum.auto()
    n = enum.auto()
    n2 = enum.auto()
    o = enum.auto()
    p = enum.auto()
    positions = enum.auto()
    qkv = enum.auto()
    radar = enum.auto()
    radar_back = enum.auto()
    radar_counts = enum.auto()
    radar_positions = enum.auto()
    rb = enum.auto()
    rdr = enum.auto()
    received = enum.auto()
    returned = enum.auto()
    rkv = enum.auto()
    section = enum.auto()
    send = enum.auto()
    shifts = enum.auto()
    slopes = enum.auto()
    small = enum.auto()
    streams = enum.auto()
    u = enum.auto()
    wcout = enum.auto()
    wcqkv = enum.auto()
    wfc1 = enum.auto()
    wfc2 = enum.auto()
    wout = enum.auto()
    wqkv = enum.auto()
    x = enum.auto()
    xb = enum.auto()
    y = enum.auto()
    yout = enum.auto()
    ysend = enum.auto()


SENT = {K.cross: K.cross_send, K.fc2: K.fc2_send, K.fc1: K.fc1_send, K.attn: K.attn_send}
SUMS = {K.cross: K.cross_sums, K.fc2: K.fc2_sums, K.fc1: K.fc1_sums, K.attn: K.attn_sums}
FIRST = [(K.ln, 0, at) for at in range(64)]
SECOND = [(K.ln, 1, at) for at in range(64)]
IN_VMEM = FIRST + SECOND + list(SUMS.values())
GRAD_JOBS = (K.grads_cross, K.grads_fc2, K.grads_fc1, K.grads_attn, K.grads_early, K.grads_late)
BACK_JOBS = (K.backward, K.backward_mlp, K.backward_self)


class Job(typing.NamedTuple):
    reads: tuple
    writes: tuple
    weights: tuple
    scratch: tuple


def dot_nn(left, right):
    return jnp.dot(left, right, preferred_element_type=F32)


def dot_tn(left, right):
    return lax.dot_general(left, right, (((0,), (0,)), ((), ())), preferred_element_type=F32)


def dot_nt(left, right):
    return lax.dot_general(left, right, (((1,), (1,)), ((), ())), preferred_element_type=F32)


class Copies:
    def __init__(self, sems):
        self.sems = sems
        self.used = 0

    def start(self, source, target):
        copy = pltpu.make_async_copy(source, target, self.sems.at[self.used])
        self.used += 1
        copy.start()
        return copy

    def reserve(self, count):
        first = self.used
        self.used += count
        return lambda at: self.sems.at[first + at]


def spans(rows):
    return [slice(at, at + CHUNK) for at in range(0, rows, CHUNK)]


def norm_parts(values):
    average = jnp.mean(values, axis=-1, keepdims=True)
    centred = values - average
    spread = jnp.mean(centred * centred, axis=-1, keepdims=True)
    scale = lax.rsqrt(spread + NORM_EPS)
    return centred * scale, scale


def norm_forward(source, gain, shift, target):
    for span in spans(source.shape[0]):
        unit, _ = norm_parts(source[span, :])
        target[span, :] = (unit * gain + shift).astype(BF)


def norm_backward(source, gain, upstream, residual, target):
    gain_sum = jnp.zeros((8, source.shape[1]), F32)
    shift_sum = jnp.zeros((8, source.shape[1]), F32)
    for span in spans(source.shape[0]):
        unit, scale = norm_parts(source[span, :])
        grad = upstream[span, :]
        product = grad * unit
        gain_sum = gain_sum + product[:8] + product[8:]
        shift_sum = shift_sum + grad[:8] + grad[8:]
        inner = grad * gain
        mean_one = jnp.mean(inner, axis=-1, keepdims=True)
        mean_two = jnp.mean(inner * unit, axis=-1, keepdims=True)
        target[span, :] = residual[span, :] + scale * (inner - mean_one - unit * mean_two)
    return (
        jnp.sum(gain_sum, axis=0, keepdims=True),
        jnp.sum(shift_sum, axis=0, keepdims=True),
    )


def gelu_both(values):
    cdf = 0.5 + 0.5 * lax.erf(values * 0.7071067811865476)
    density = 0.3989422804014327 * jnp.exp(-0.5 * values * values)
    return values * cdf, cdf + values * density


def place(positions):
    values = positions
    row = jnp.floor((values + 0.5) * (1.0 / GRID))
    return row, values - GRID * row


def distances(key_col, query_row, live_keys):
    row_q, col_q = place(query_row)
    row_k, col_k = place(key_col)
    gap_row = row_q - row_k
    gap_col = col_q - col_k
    distance = jnp.sqrt(gap_row * gap_row + gap_col * gap_col)
    slot = lax.broadcasted_iota(jnp.int32, distance.shape, 0)
    return jnp.where(slot < live_keys, distance, FAR)


def both_heads(pair):
    first = lax.broadcasted_iota(jnp.int32, pair.shape, 1) < HD
    zero = jnp.zeros_like(pair)
    return jnp.concatenate([jnp.where(first, pair, zero), jnp.where(first, zero, pair)], axis=0)


def one_pair(stacked):
    half = stacked.shape[0] // 2
    first = lax.broadcasted_iota(jnp.int32, (half, LANES), 1) < HD
    return jnp.where(first, stacked[:half], stacked[half:])


def by_size(plan, most_live, work):
    def step(image, carry):
        if plan.slots <= LANES:
            work(image, plan.slots)
        else:
            live = most_live(image)

            @pl.when(live <= LANES)
            def _():
                work(image, LANES)

            @pl.when(live > LANES)
            def _():
                work(image, plan.slots)

        return carry

    lax.fori_loop(0, plan.per, step, 0)


def rows_of(plan, image, first, size):
    return pl.ds(pl.multiple_of(image * plan.slots + first, 8), size)


def pair_lanes(base, pair):
    if isinstance(pair, int):
        return pl.ds(base + pair * LANES, LANES)
    return pl.ds(pl.multiple_of(base + pair * LANES, LANES), LANES)


def over_pairs(plan, work, size):
    unroll = PAIRS if size <= LANES else plan.unroll

    def step(at, carry):
        for part in range(unroll):
            work(at * unroll + part)
        return carry

    if unroll == PAIRS:
        step(0, 0)
    else:
        lax.fori_loop(0, PAIRS // unroll, step, 0)


def attend(plan, most_live, query, keys, values, spread, slopes, heard, weights):
    def work(image, size):
        rows = rows_of(plan, image, 0, size)
        if size < plan.slots:
            rest = rows_of(plan, image, size, plan.slots - size)
            heard[rest, :] = jnp.zeros((plan.slots - size, plan.width), F32)
        spread(image, size)
        gap_ref = spread.target

        def one(pair):
            q = both_heads(query[0][rows, pair_lanes(query[1], pair)]).astype(BF)
            k = keys[0][rows, pair_lanes(keys[1], pair)].astype(BF)
            v = values[0][rows, pair_lanes(values[1], pair)].astype(BF)
            first = lax.broadcasted_iota(jnp.int32, (1, 2 * size), 1) < size
            slope = jnp.where(first, slopes[2 * pair], slopes[2 * pair + 1])
            scores = dot_nt(k, q) - slope * gap_ref[image, :size, : 2 * size]
            scores = jnp.exp(scores - jnp.max(scores, axis=0, keepdims=True))
            totals = jnp.sum(scores, axis=0, keepdims=True)
            p = (scores * (1.0 / totals)).astype(BF)
            weights[image * PAIRS + pair, :size, : 2 * size] = p
            heard[rows, pair_lanes(0, pair)] = one_pair(dot_tn(p, v))

        over_pairs(plan, one, size)

    by_size(plan, most_live, work)


def attend_back(plan, most_live, query, keys, values, grad_heard, weights, grads):
    grad_q, grad_k, grad_v = grads

    def work(image, size):
        rows = rows_of(plan, image, 0, size)
        if size < plan.slots:
            rest = rows_of(plan, image, size, plan.slots - size)
            for ref, offset in grads:
                ref[rest, offset : offset + plan.width] = jnp.zeros((plan.slots - size, plan.width), F32)

        def one(pair):
            q = both_heads(query[0][rows, pair_lanes(query[1], pair)]).astype(BF)
            k = keys[0][rows, pair_lanes(keys[1], pair)].astype(BF)
            v = values[0][rows, pair_lanes(values[1], pair)].astype(BF)
            g = both_heads(grad_heard[rows, pair_lanes(0, pair)]).astype(BF)
            p = weights[image * PAIRS + pair, :size, : 2 * size]
            wide = p.astype(F32)
            product = dot_nt(v, g) * wide
            grad_s = (product - wide * jnp.sum(product, axis=0, keepdims=True)).astype(BF)
            grad_v[0][rows, pair_lanes(grad_v[1], pair)] = dot_nn(p, g)
            grad_k[0][rows, pair_lanes(grad_k[1], pair)] = dot_nn(grad_s, q)
            grad_q[0][rows, pair_lanes(grad_q[1], pair)] = one_pair(dot_tn(grad_s, k)) * SCORE_SCALE

        over_pairs(plan, one, size)

    by_size(plan, most_live, work)


def columns_of(positions):
    images = positions.shape[0]
    low = positions.astype(F32).astype(BF)
    row = lax.broadcasted_iota(jnp.int32, (images, LANES), 0)
    lane = lax.broadcasted_iota(jnp.int32, (images, LANES), 1)
    return dot_tn(low, (row == lane).astype(F32).astype(BF))


def twice(positions, size):
    slots = positions.shape[1]
    low = positions.astype(F32).astype(BF)
    row = lax.broadcasted_iota(jnp.int32, (slots, 2 * size), 0)
    lane = lax.broadcasted_iota(jnp.int32, (slots, 2 * size), 1)
    from_slot = jnp.where(lane < size, lane, lane - size)
    return dot_nn(low, (row == from_slot).astype(F32).astype(BF))


class Spread:
    def __init__(self, plan, r, target, k, key_positions, key_count):
        self.plan, self.r, self.target, self.k = plan, r, target, k
        self.key_positions, self.key_count = key_positions, key_count

    def __call__(self, image, size):
        at = self.k * self.plan.per + image
        query = twice(self.r[K.positions][pl.ds(at, 1), :], size)
        keys = columns_of(self.r[self.key_positions][pl.ds(at, 1), :])
        self.target[image, :size, : 2 * size] = distances(
            keys[:size, :1], query, self.r[self.key_count][at]
        )


def most_live(plan, r, k, names):
    def live(image):
        found = r[names[0]][k * plan.per + image]
        for name in names[1:]:
            found = jnp.maximum(found, r[name][k * plan.per + image])
        return found

    return live


def fill_rows(target, images, slots, counts, first_image, source):
    for image in range(images):
        live = counts[first_image + image]
        for at in range(0, slots, 8):
            span = slice(image * slots + at, image * slots + at + 8)
            row = at + lax.broadcasted_iota(jnp.int32, (8, source.shape[1]), 0)
            target[span, :] = jnp.where(row < live, source[span, :], 0.0)


class Plan:
    def __init__(self, batches, slots, width, hidden, halving, unroll=1):
        self.batches, self.slots, self.width, self.hidden = batches, slots, width, hidden
        self.halving = halving
        self.unroll = unroll
        self.per = 2 if batches % 2 == 0 else 1
        self.steps = batches // self.per
        self.rows = self.per * slots
        self.total = batches * slots

    def unrolled(self, unroll):
        return Plan(self.batches, self.slots, self.width, self.hidden, self.halving, unroll)


def small_shape(plan):
    rows = 13 + plan.hidden // plan.width
    return (-(-rows // 8) * 8, plan.width)


WEIGHT_NAMES = (K.wqkv, K.wout, K.wfc1, K.wfc2, K.wcqkv, K.wcout)


def scratch_shapes(plan):
    r, d, f = plan.rows, plan.width, plan.hidden
    w = {
        K.wqkv: ((d, 3 * d), BF),
        K.wout: ((d, d), BF),
        K.wfc1: ((d, f), BF),
        K.wfc2: ((f, d), BF),
        K.wcqkv: ((d, 3 * d), BF),
        K.wcout: ((d, d), BF),
        K.xb: ((r, d), BF),
        K.x: ((r, d), F32),
        K.n: ((r, d), BF),
        K.qkv: ((r, 3 * d), F32),
        K.p: ((plan.per * PAIRS, plan.slots, 2 * plan.slots), BF),
        K.dist: ((plan.per, plan.slots, 2 * plan.slots), F32),
        K.heard: ((r, d), F32),
        K.o: ((r, d), BF),
        K.h: ((r, d), F32),
        K.n2: ((r, d), BF),
        K.u: ((r, f), F32),
        K.a: ((r, f), BF),
        K.gp: ((r, f), BF),
        K.y: ((r, d), F32),
        K.yout: ((r, d), F32),
        K.ysend: ((r, d), BF),
        K.gin: ((r, d), BF),
        K.g: ((r, d), F32),
        K.gbr: ((r, d), BF),
        K.du: ((r, f), BF),
        K.dn: ((r, d), F32),
        K.dh: ((r, d), F32),
        K.gm: ((r, d), BF),
        K.go: ((r, d), F32),
        K.dqkv: ((r, 3 * d), F32),
        K.dqkvb: ((r, 3 * d), BF),
        K.dx: ((r, d), F32),
        K.dxb: ((r, d), BF),
        K.ln: ((8, d), F32),
        K.cdist: ((plan.per, plan.slots, 2 * plan.slots), F32),
        K.m: ((r, d), BF),
        K.cq: ((r, d), F32),
        K.ckvb: ((r, 2 * d), BF),
        K.ckv: ((r, 2 * d), F32),
        K.cp: ((plan.per * PAIRS, plan.slots, 2 * plan.slots), BF),
        K.cheard: ((r, d), F32),
        K.co: ((r, d), BF),
        K.h2: ((r, d), F32),
        K.gaf: ((r, d), BF),
        K.cgo: ((r, d), F32),
        K.dcqkv: ((r, 3 * d), F32),
        K.dcq: ((r, d), BF),
        K.dckv: ((r, 2 * d), BF),
        K.dm: ((r, d), F32),
        K.dmid: ((r, d), F32),
        K.gl: ((plan.total, f), BF),
        K.gr: ((plan.total, f + d), BF),
        K.gsums: ((8, f + d), F32),
        K.small: (small_shape(plan), F32),
        K.gnat: ((2, 16, d // 16, d) if plan.halving else (2, d, d), BF),
        K.gnat_tall: ((2, 4, d // 4, d), BF),
        K.gout: ((2, 2, 8, d // 16, d), BF),
        K.gout_tall: ((2, 2, 2, d // 4, d), BF),
        K.rdr: ((plan.total, d), F32),
        K.rb: ((plan.total, d), BF),
        K.rkv: ((plan.total, 2 * d), BF),
    }
    return w


def chunk_shape(plan, height, breadth):
    if not plan.halving:
        return (height, breadth), BF
    if height == plan.width:
        return (8, height // 16, breadth), BF
    return (2, 2, 2, height // 16, breadth), BF


def chunk_state(name, height, breadth):
    def size(plan, amount):
        return plan.hidden if amount is None else amount * plan.width

    def main(plan):
        return chunk_shape(plan, size(plan, height), size(plan, breadth))

    def sums(plan):
        return (8, size(plan, breadth)), F32

    return {name: main, SENT[name]: main, SUMS[name]: sums}


STATE = {
    K.n: lambda p: ((p.total, p.width), BF),
    K.o: lambda p: ((p.total, p.width), BF),
    K.n2: lambda p: ((p.total, p.width), BF),
    K.a: lambda p: ((p.total, p.hidden), BF),
    K.layer_out: lambda p: ((p.total, p.width), F32),
    K.qkv: lambda p: ((p.total, 3 * p.width), F32),
    K.p: lambda p: ((p.batches * PAIRS, p.slots, 2 * p.slots), BF),
    K.h: lambda p: ((p.total, p.width), F32),
    K.gp: lambda p: ((p.total, p.hidden), BF),
    K.ckv: lambda p: ((p.total, 2 * p.width), BF),
    K.gbr: lambda p: ((p.total, p.width), BF),
    K.du: lambda p: ((p.total, p.hidden), BF),
    K.gm: lambda p: ((p.total, p.width), BF),
    K.dqkv: lambda p: ((p.total, 3 * p.width), BF),
    K.input_grads: lambda p: ((p.total, p.width), F32),
    K.m: lambda p: ((p.total, p.width), BF),
    K.co: lambda p: ((p.total, p.width), BF),
    K.gaf: lambda p: ((p.total, p.width), BF),
    K.dcq: lambda p: ((p.total, p.width), BF),
    K.dckv: lambda p: ((p.total, 2 * p.width), BF),
    K.between: lambda p: ((p.rows, p.width), F32),
    K.send: lambda p: ((p.rows, p.width), BF),
    K.ln: lambda p: ((8, p.width), F32),
    K.small: lambda p: (small_shape(p), F32),
    **chunk_state(K.cross, 1, 4),
    **chunk_state(K.fc2, None, 1),
    **chunk_state(K.fc1, 1, 5),
    **chunk_state(K.attn, 1, 3),
}

FORWARD_0 = Job(
    reads=(K.streams,),
    writes=(K.n, K.o, K.n2, K.a, K.layer_out, K.qkv, K.p, K.h, K.gp, K.send),
    weights=(K.wqkv, K.wout, K.wfc1, K.wfc2),
    scratch=(K.xb, K.x, K.n, K.qkv, K.p, K.dist, K.heard, K.o, K.h, K.n2, K.u, K.a, K.gp, K.y, K.yout, K.ysend),
)
RADAR = Job(reads=(K.streams,), writes=(K.ckv,), weights=(K.wcqkv,), scratch=[K.rb, K.rkv])
MERGED = Job(
    reads=(K.received, K.cotangent, K.ckv),
    writes=(K.n, K.o, K.n2, K.a, K.layer_out, K.gbr, K.du, K.gm, K.dqkv, K.m, K.co, K.gaf, K.dcq, K.dckv, K.send, K.ln),
    weights=WEIGHT_NAMES,
    scratch=(K.xb, K.x, K.n, K.qkv, K.p, K.dist, K.heard, K.o, K.h, K.n2, K.u, K.a, K.gp, K.y, K.yout, K.gin, K.g, K.gbr, K.du, K.dn, K.dh, K.gm, K.go, K.dqkv, K.dqkvb, K.dxb, K.ln, K.cdist, K.m, K.cq, K.ckvb, K.ckv, K.cp, K.cheard, K.co, K.h2, K.gaf, K.cgo, K.dcqkv, K.dcq, K.dckv, K.dm, K.dmid,),
)
BACKWARD_0 = Job(
    reads=(K.streams, K.returned, K.qkv, K.p, K.h, K.gp),
    writes=(K.gbr, K.du, K.gm, K.dqkv, K.input_grads, K.ln),
    weights=(K.wfc2, K.wfc1, K.wout, K.wqkv),
    scratch=(K.xb, K.x, K.qkv, K.p, K.h, K.gp, K.gin, K.g, K.gbr, K.du, K.dn, K.dh, K.gm, K.go, K.dqkv, K.dqkvb, K.dx, K.ln),
)
BACKWARD_MLP = Job(
    reads=(K.returned, K.gp, K.h),
    writes=(K.du, K.gm, K.between, K.ln),
    weights=(K.wfc2, K.wfc1),
    scratch=(K.h, K.gp, K.gin, K.g, K.gbr, K.du, K.dn, K.dh, K.gm, K.ln),
)
BACKWARD_SELF = Job(
    reads=(K.between, K.streams, K.qkv, K.p),
    writes=(K.dqkv, K.input_grads, K.ln),
    weights=(K.wout, K.wqkv),
    scratch=(K.xb, K.x, K.qkv, K.p, K.dn, K.dh, K.gm, K.go, K.dqkv, K.dqkvb, K.dx, K.ln),
)
RADAR_BACK = Job(
    reads=(K.dckv,), writes=(K.input_grads,), weights=(K.wcqkv,), scratch=(K.rkv, K.rdr)
)
GRAD_SCRATCH = (K.gl, K.gr, K.gnat, K.gout, K.gsums)
GRADS_CROSS = Job(
    reads=(K.m, K.streams, K.co, K.dcq, K.dckv, K.gaf),
    writes=(K.cross, K.cross_send, K.cross_sums),
    weights=(),
    scratch=GRAD_SCRATCH,
)
GRADS_FC2 = Job(
    reads=(K.a, K.gbr, K.returned),
    writes=(K.fc2, K.fc2_send, K.fc2_sums),
    weights=(),
    scratch=(K.gl, K.gr, K.gnat, K.gnat_tall, K.gout_tall, K.gsums, K.gin, K.dn, K.g),
)
GRADS_FC1 = Job(
    reads=(K.n2, K.o, K.du, K.gm),
    writes=(K.fc1, K.fc1_send, K.fc1_sums),
    weights=(),
    scratch=GRAD_SCRATCH,
)
GRADS_ATTN = Job(
    reads=(K.n, K.dqkv, K.fc1_sums, K.fc2_sums, K.cross_sums),
    writes=(K.attn, K.attn_send, K.attn_sums, K.small),
    weights=(),
    scratch=GRAD_SCRATCH + (K.small,),
)
GRADS_EARLY = Job(
    reads=(K.a, K.gbr),
    writes=(K.fc2, K.fc2_send, K.fc2_sums),
    weights=(),
    scratch=(K.gl, K.gr, K.gnat, K.gnat_tall, K.gout_tall, K.gsums),
)
GRADS_LATE = Job(*(tuple(dict.fromkeys(one + two)) for one, two in zip(GRADS_CROSS, GRADS_FC1)))
JOBS = {
    K.forward: FORWARD_0,
    K.radar: RADAR,
    K.merged: MERGED,
    K.backward: BACKWARD_0,
    K.backward_mlp: BACKWARD_MLP,
    K.backward_self: BACKWARD_SELF,
    K.radar_back: RADAR_BACK,
    K.grads_cross: GRADS_CROSS,
    K.grads_fc2: GRADS_FC2,
    K.grads_fc1: GRADS_FC1,
    K.grads_attn: GRADS_ATTN,
    K.grads_early: GRADS_EARLY,
    K.grads_late: GRADS_LATE,
}
TILE = 768


def tiles(extent, tile=TILE):
    return [slice(at, min(at + tile, extent)) for at in range(0, extent, tile)]


def self_forward(plan, r, s, c, k, waits, save):
    d = plan.width
    rows = pl.ds(k * plan.rows, plan.rows)
    out = []
    gain, shift, bias = r[K.gains], r[K.shifts], r[K.attn_bias]
    norm_forward(s[K.x], gain[:, :d], shift[:, :d], s[K.n])
    out.append(c.start(s[K.n], r[K.n].at[rows]))
    waits[K.wqkv].wait()
    normed = s[K.n][...]
    s[K.qkv][:, :d] = (dot_nn(normed, s[K.wqkv][:, :d]) + bias[:, :d]).astype(BF).astype(F32) * SCORE_SCALE
    s[K.qkv][:, d : 2 * d] = dot_nn(normed, s[K.wqkv][:, d : 2 * d])
    s[K.qkv][:, 2 * d :] = dot_nn(normed, s[K.wqkv][:, 2 * d :]) + bias[:, d : 2 * d]
    if save:
        out.append(c.start(s[K.qkv], r[K.qkv].at[rows]))
    attend(
        plan,
        most_live(plan, r, k, (K.counts,)),
        (s[K.qkv], 0),
        (s[K.qkv], d),
        (s[K.qkv], 2 * d),
        Spread(plan, r, s[K.dist], k, K.positions, K.counts),
        r[K.slopes],
        s[K.heard],
        s[K.p],
    )
    if save:
        out.append(c.start(s[K.p], r[K.p].at[pl.ds(k * plan.per * PAIRS, plan.per * PAIRS)]))
    s[K.o][...] = s[K.heard][...].astype(BF)
    out.append(c.start(s[K.o], r[K.o].at[rows]))
    waits[K.wout].wait()
    s[K.h][...] = s[K.x][...] + dot_nn(s[K.o][...], s[K.wout][...]) + bias[:, 2 * d :]
    if save:
        out.append(c.start(s[K.h], r[K.h].at[rows]))
    return out


def mlp_forward(plan, r, s, c, k, waits, after, save):
    d, f = plan.width, plan.hidden
    rows = pl.ds(k * plan.rows, plan.rows)
    out = []
    norm_forward(after, r[K.gains][:, d:], r[K.shifts][:, d:], s[K.n2])
    out.append(c.start(s[K.n2], r[K.n2].at[rows]))
    waits[K.wfc1].wait()
    bias = r[K.mlp_bias]
    for tile in tiles(f):
        s[K.u][:, tile] = dot_nn(s[K.n2][...], s[K.wfc1][:, tile]) + bias[:, tile]
        for span in spans(plan.rows):
            active, slope = gelu_both(s[K.u][span, tile])
            s[K.a][span, tile] = active.astype(BF)
            s[K.gp][span, tile] = slope.astype(BF)
    out.append(c.start(s[K.a], r[K.a].at[rows]))
    if save:
        out.append(c.start(s[K.gp], r[K.gp].at[rows]))
    waits[K.wfc2].wait()
    s[K.y][...] = after[...] + dot_nn(s[K.a][...], s[K.wfc2][...]) + bias[:, f:]
    fill_rows(s[K.yout], plan.per, plan.slots, r[K.counts], k * plan.per, s[K.y])
    out.append(c.start(s[K.yout], r[K.layer_out].at[rows]))
    return out


def mlp_backward(plan, r, s, c, k, waits, after, target):
    d, f = plan.width, plan.hidden
    rows = pl.ds(k * plan.rows, plan.rows)
    out = []
    s[K.dn][...] = s[K.gin][...].astype(F32)
    fill_rows(s[K.g], plan.per, plan.slots, r[K.counts], k * plan.per, s[K.dn])
    s[K.gbr][...] = s[K.g][...].astype(BF)
    if K.gbr in r:
        out.append(c.start(s[K.gbr], r[K.gbr].at[rows]))
    if K.wfc2 in waits:
        waits[K.wfc2].wait()
    for tile in tiles(f):
        grad = dot_nt(s[K.gbr][...], s[K.wfc2][tile, :])
        s[K.du][:, tile] = (grad * s[K.gp][:, tile].astype(F32)).astype(BF)
    out.append(c.start(s[K.du], r[K.du].at[rows]))
    if K.wfc1 in waits:
        waits[K.wfc1].wait()
    s[K.dn][...] = dot_nt(s[K.du][...], s[K.wfc1][...])
    sums = norm_backward(after, r[K.gains][:, d:], s[K.dn], s[K.g], target)
    return out, sums


def self_backward(plan, r, s, c, k, waits, grad, target):
    d = plan.width
    rows = pl.ds(k * plan.rows, plan.rows)
    out = []
    s[K.gm][...] = grad[...].astype(BF)
    if K.gm in r:
        out.append(c.start(s[K.gm], r[K.gm].at[rows]))
    if K.wout in waits:
        waits[K.wout].wait()
    s[K.go][...] = dot_nt(s[K.gm][...], s[K.wout][...])
    attend_back(
        plan,
        most_live(plan, r, k, (K.counts,)),
        (s[K.qkv], 0),
        (s[K.qkv], d),
        (s[K.qkv], 2 * d),
        s[K.go],
        s[K.p],
        [(s[K.dqkv], part * d) for part in range(3)],
    )
    s[K.dqkvb][...] = s[K.dqkv][...].astype(BF)
    out.append(c.start(s[K.dqkvb], r[K.dqkv].at[rows]))
    if K.wqkv in waits:
        waits[K.wqkv].wait()
    s[K.dn][...] = dot_nt(s[K.dqkvb][...], s[K.wqkv][...])
    sums = norm_backward(s[K.x], r[K.gains][:, :d], s[K.dn], grad, target)
    return out, sums


def write_sums(s, c, r, parts):
    s[K.ln][...] = jnp.zeros_like(s[K.ln])
    for at, part in enumerate(parts):
        s[K.ln][at : at + 1, :] = part
    return c.start(s[K.ln], r[K.ln])


def start_weights(r, s, c, names):
    return {name: c.start(r[name], s[name]) for name in names}


def run_forward(plan, r, s, c, k):
    rows = pl.ds(k * plan.rows, plan.rows)
    arrive = c.start(r[K.streams].at[rows], s[K.xb])
    waits = start_weights(r, s, c, FORWARD_0.weights)
    arrive.wait()
    s[K.x][...] = s[K.xb][...].astype(F32)
    out = self_forward(plan, r, s, c, k, waits, True)
    out += mlp_forward(plan, r, s, c, k, waits, s[K.h], True)
    s[K.ysend][...] = s[K.yout][...].astype(BF)
    out.append(c.start(s[K.ysend], r[K.send]))
    for copy in out:
        copy.wait()


def run_radar(plan, r, s, c, k):
    d = plan.width
    arrive = c.start(r[K.streams], s[K.rb])
    weight = c.start(r[K.wcqkv], s[K.wcqkv])
    arrive.wait()
    weight.wait()
    s[K.rkv][:, :d] = dot_nn(s[K.rb][...], s[K.wcqkv][:, d : 2 * d]).astype(BF)
    s[K.rkv][:, d:] = (
        dot_nn(s[K.rb][...], s[K.wcqkv][:, 2 * d :]) + r[K.cross_bias][:, d : 2 * d]
    ).astype(BF)
    c.start(s[K.rkv], r[K.ckv]).wait()


def run_merged(plan, r, s, c, k):
    plan = plan.unrolled(3)
    d = plan.width
    rows = pl.ds(k * plan.rows, plan.rows)
    arrive = c.start(r[K.received], s[K.xb])
    waits = start_weights(r, s, c, (K.wqkv, K.wout, K.wcqkv, K.wcout, K.wfc1, K.wfc2))
    arrive_kv = c.start(r[K.ckv].at[rows], s[K.ckvb])
    arrive_grad = c.start(r[K.cotangent].at[rows], s[K.gin])
    arrive.wait()
    s[K.x][...] = s[K.xb][...].astype(F32)
    out = self_forward(plan, r, s, c, k, waits, False)
    bias = r[K.cross_bias]
    norm_forward(s[K.h], r[K.cross_gain][...], bias[:, 3 * d :], s[K.m])
    out.append(c.start(s[K.m], r[K.m].at[rows]))
    waits[K.wcqkv].wait()
    s[K.cq][...] = (dot_nn(s[K.m][...], s[K.wcqkv][:, :d]) + bias[:, :d]).astype(BF).astype(F32) * SCORE_SCALE
    arrive_kv.wait()
    s[K.ckv][...] = s[K.ckvb][...].astype(F32)
    live = most_live(plan, r, k, (K.counts, K.radar_counts))
    attend(
        plan,
        live,
        (s[K.cq], 0),
        (s[K.ckv], 0),
        (s[K.ckv], d),
        Spread(plan, r, s[K.cdist], k, K.radar_positions, K.radar_counts),
        r[K.slopes],
        s[K.cheard],
        s[K.cp],
    )
    s[K.co][...] = s[K.cheard][...].astype(BF)
    out.append(c.start(s[K.co], r[K.co].at[rows]))
    waits[K.wcout].wait()
    s[K.h2][...] = s[K.h][...] + dot_nn(s[K.co][...], s[K.wcout][...]) + bias[:, 2 * d : 3 * d]
    out += mlp_forward(plan, r, s, c, k, waits, s[K.h2], False)
    arrive_grad.wait()
    more, sums_two = mlp_backward(plan, r, s, c, k, {}, s[K.h2], s[K.dh])
    out += more
    s[K.gaf][...] = s[K.dh][...].astype(BF)
    out.append(c.start(s[K.gaf], r[K.gaf].at[rows]))
    s[K.cgo][...] = dot_nt(s[K.gaf][...], s[K.wcout][...])
    attend_back(
        plan,
        live,
        (s[K.cq], 0),
        (s[K.ckv], 0),
        (s[K.ckv], d),
        s[K.cgo],
        s[K.cp],
        [(s[K.dcqkv], part * d) for part in range(3)],
    )
    s[K.dcq][...] = s[K.dcqkv][:, :d].astype(BF)
    s[K.dckv][...] = s[K.dcqkv][:, d:].astype(BF)
    out.append(c.start(s[K.dcq], r[K.dcq].at[rows]))
    out.append(c.start(s[K.dckv], r[K.dckv].at[rows]))
    s[K.dm][...] = dot_nt(s[K.dcq][...], s[K.wcqkv][:, :d])
    sums_cross = norm_backward(s[K.h], r[K.cross_gain][...], s[K.dm], s[K.dh], s[K.dmid])
    more, sums_one = self_backward(plan, r, s, c, k, {}, s[K.dmid], s[K.dh])
    out += more
    s[K.dxb][...] = s[K.dh][...].astype(BF)
    out.append(c.start(s[K.dxb], r[K.send]))
    out.append(write_sums(s, c, r, sums_one + sums_two + sums_cross))
    for copy in out:
        copy.wait()


def load_mlp_back(plan, r, s, c, k):
    rows = pl.ds(k * plan.rows, plan.rows)
    arrive = [c.start(r[K.returned], s[K.gin])]
    waits = start_weights(r, s, c, (K.wfc2,))
    arrive.append(c.start(r[K.gp].at[rows], s[K.gp]))
    waits.update(start_weights(r, s, c, (K.wfc1,)))
    arrive.append(c.start(r[K.h].at[rows], s[K.h]))
    return arrive, waits


def load_self_back(plan, r, s, c, k):
    rows = pl.ds(k * plan.rows, plan.rows)
    waits = start_weights(r, s, c, (K.wout,))
    arrive = [
        c.start(r[K.qkv].at[rows], s[K.qkv]),
        c.start(r[K.p].at[pl.ds(k * plan.per * PAIRS, plan.per * PAIRS)], s[K.p]),
    ]
    waits.update(start_weights(r, s, c, (K.wqkv,)))
    arrive.append(c.start(r[K.streams].at[rows], s[K.xb]))
    return arrive, waits


def wait_all(copies):
    for copy in copies:
        copy.wait()


def run_backward(plan, r, s, c, k):
    rows = pl.ds(k * plan.rows, plan.rows)
    arrive, waits = load_mlp_back(plan, r, s, c, k)
    arrive_self, waits_self = load_self_back(plan, r, s, c, k)
    waits.update(waits_self)
    wait_all(arrive)
    out, sums_two = mlp_backward(plan, r, s, c, k, waits, s[K.h], s[K.dh])
    wait_all(arrive_self)
    s[K.x][...] = s[K.xb][...].astype(F32)
    more, sums_one = self_backward(plan, r, s, c, k, waits, s[K.dh], s[K.dx])
    out += more
    out.append(c.start(s[K.dx], r[K.input_grads].at[rows]))
    out.append(write_sums(s, c, r, sums_one + sums_two))
    wait_all(out)


def run_backward_mlp(plan, r, s, c, k):
    arrive, waits = load_mlp_back(plan, r, s, c, k)
    wait_all(arrive)
    out, sums_two = mlp_backward(plan, r, s, c, k, waits, s[K.h], s[K.dh])
    out.append(c.start(s[K.dh], r[K.between]))
    s[K.gm][...] = s[K.dh][...].astype(BF)
    out.append(c.start(s[K.gm], r[K.gm].at[pl.ds(k * plan.rows, plan.rows)]))
    nothing = jnp.zeros_like(sums_two[0])
    out.append(write_sums(s, c, r, (nothing, nothing) + sums_two))
    wait_all(out)


def run_backward_self(plan, r, s, c, k):
    rows = pl.ds(k * plan.rows, plan.rows)
    arrive = [c.start(r[K.between], s[K.dh])]
    more, waits = load_self_back(plan, r, s, c, k)
    wait_all(arrive + more)
    s[K.x][...] = s[K.xb][...].astype(F32)
    out, sums_one = self_backward(plan, r, s, c, k, waits, s[K.dh], s[K.dx])
    out.append(c.start(s[K.dx], r[K.input_grads].at[rows]))
    out.append(write_sums(s, c, r, sums_one))
    wait_all(out)


def run_radar_back(plan, r, s, c, k):
    d = plan.width
    arrive = c.start(r[K.dckv], s[K.rkv])
    weight = c.start(r[K.wcqkv], s[K.wcqkv])
    arrive.wait()
    weight.wait()
    s[K.rdr][...] = dot_nt(s[K.rkv][...], s[K.wcqkv][:, d:])
    c.start(s[K.rdr], r[K.input_grads]).wait()


def slot_of(relative):
    return ((relative >> 1) & 1) * 4 + ((relative >> 2) & 1) * 2 + ((relative >> 3) & 1)


def weight_grads(plan, r, s, c, lefts, rights, left_of, tall, name, fix=None):
    d, total = plan.width, plan.total

    def blocks(buffer, names):
        found = []
        for array in names:
            for tile in tiles(r[array].shape[1], d):
                at = len(found) * d
                found.append((r[array].at[:, tile], buffer.at[:, at : at + d]))
        return found

    left_blocks, right_blocks = blocks(s[K.gl], lefts), blocks(s[K.gr], rights)
    count = max(len(left_blocks), len(right_blocks))
    loads, seen = [], set()
    for t in range(count):
        wanted = [(0, 0 if tall else t), (1, left_of(t))]
        fresh = [key for key in wanted if key not in seen]
        seen.update(fresh)
        loads.append([c.start(*(right_blocks, left_blocks)[side][at]) for side, at in fresh])
    if fix is not None:
        wait_all(loads[0])
        loads[0] = []
        fix()
    mine = r[K.device][0]
    block = d // 4 if tall else d // 16
    natural = s[K.gnat_tall if tall and plan.halving else K.gnat]
    gout = s[K.gout_tall if tall else K.gout] if plan.halving else None
    sems = c.reserve(4)

    def columns(at):
        return pl.ds(pl.multiple_of(at * d, LANES), d)

    def copies_out(t):
        slot = lax.rem(t, 2)
        found = []
        for sent in range(2 if plan.halving else 1):
            ref = r[SENT[name] if sent else name]
            if not plan.halving:
                target = ref.at[columns(t), :] if tall else ref.at[:, columns(t)]
                source = natural.at[slot]
            elif tall:
                away = t ^ (mine >> 2)
                target, source = ref.at[:, away & 1, away >> 1], gout.at[slot, sent]
            else:
                target, source = ref.at[:, :, columns(t)], gout.at[slot, sent]
            found.append(pltpu.make_async_copy(source, target, sems(slot * 2 + sent)))
        return found

    def wait_out(t):
        wait_all(copies_out(t))

    def hand_on(t):
        for one in copies_out(t):
            one.start()

    def arrange(slot):
        if tall:
            for relative in range(4):
                gout[slot, relative & 1, relative >> 1] = natural[slot, (mine & 3) ^ relative]
        else:
            for relative in range(16):
                gout[slot, relative & 1, slot_of(relative)] = natural[slot, mine ^ relative]

    behind = 1 if plan.halving else 0

    def step(t, carry):
        for at, found in enumerate(loads):
            if found:
                pl.when(t == at)(lambda found=found: wait_all(found))
        pl.when(t >= 2 + behind)(lambda: wait_out(t - 2 - behind))
        slot = lax.rem(t, 2)
        grad = s[K.gr][:, columns(0 if tall else t)]
        low = dot_tn(s[K.gl][:, columns(left_of(t))], grad).astype(BF)
        if plan.halving:
            for part in range(d // block):
                natural[slot, part] = low[part * block : (part + 1) * block]
            arrange(1 - slot)
        else:
            natural[slot] = low
        sums = jnp.sum(grad.astype(F32).reshape(total // 8, 8, d), axis=0)
        s[K.gsums][:, columns(0 if tall else t)] = sums
        pl.when(t >= behind)(lambda: hand_on(t - behind))
        return carry

    lax.fori_loop(0, count, step, 0)
    if plan.halving:
        wait_out(count - 3)
        arrange((count - 1) % 2)
        hand_on(count - 1)
    breadth = len(right_blocks) * d
    last = c.start(s[K.gsums].at[:, :breadth], r[SUMS[name]])
    wait_out(count - 2)
    wait_out(count - 1)
    last.wait()


def run_grads_cross(plan, r, s, c, k):
    weight_grads(
        plan, r, s, c, (K.m, K.streams, K.co), (K.dcq, K.dckv, K.gaf),
        lambda t: (t + 1) // 2, False, K.cross,
    )


def run_grads_fc2(plan, r, s, c, k):
    last = plan.steps - 1
    arrive = c.start(r[K.returned], s[K.gin])

    def fix():
        arrive.wait()

        @pl.when(r[K.section][0] == 0)
        def _():
            s[K.dn][...] = s[K.gin][...].astype(F32)
            fill_rows(s[K.g], plan.per, plan.slots, r[K.counts], last * plan.per, s[K.dn])
            s[K.gr][last * plan.rows :, : plan.width] = s[K.g][...].astype(BF)

    weight_grads(plan, r, s, c, (K.a,), (K.gbr,), lambda t: t, True, K.fc2, fix)


def run_grads_fc1(plan, r, s, c, k):
    last = plan.hidden // plan.width
    weight_grads(plan, r, s, c, (K.n2, K.o), (K.du, K.gm), lambda t: t // last, False, K.fc1)


def run_grads_early(plan, r, s, c, k):
    weight_grads(plan, r, s, c, (K.a,), (K.gbr,), lambda t: t, True, K.fc2)


def run_grads_late(plan, r, s, c, k):
    run_grads_cross(plan, r, s, c, k)
    run_grads_fc1(plan, r, s, c, k)


def run_grads_attn(plan, r, s, c, k):
    weight_grads(plan, r, s, c, (K.n,), (K.dqkv,), lambda t: 0 * t, False, K.attn)
    d = plan.width
    first = sum(r[name][...] for name in r if name in FIRST)
    second = sum(r[name][...] for name in r if name in SECOND)
    norms = jnp.where(r[K.section][0] == 0, first, second)
    ratio = plan.hidden // d

    def column(ref, at):
        return jnp.sum(ref[:, at * d : (at + 1) * d], axis=0, keepdims=True)

    rows = [column(s[K.gsums], 0), column(s[K.gsums], 2), column(r[K.fc1_sums], ratio)]
    rows += [column(r[K.fc1_sums], at) for at in range(ratio)] + [column(r[K.fc2_sums], 0)]
    rows += [norms[0:1], norms[2:3], norms[1:2], norms[3:4], norms[4:5]]
    rows += [column(r[K.cross_sums], at) for at in (0, 2, 3)] + [norms[5:6]]
    s[K.small][...] = jnp.zeros_like(s[K.small])
    for at, row in enumerate(rows):
        s[K.small][at : at + 1, :] = row
    c.start(s[K.small], r[K.small]).wait()


RUN = {
    K.forward: run_forward,
    K.radar: run_radar,
    K.merged: run_merged,
    K.backward: run_backward,
    K.backward_mlp: run_backward_mlp,
    K.backward_self: run_backward_self,
    K.radar_back: run_radar_back,
    K.grads_cross: run_grads_cross,
    K.grads_fc2: run_grads_fc2,
    K.grads_fc1: run_grads_fc1,
    K.grads_attn: run_grads_attn,
    K.grads_early: run_grads_early,
    K.grads_late: run_grads_late,
}


def phase(plan, fixed, state, weights, first, second, after=()):
    jobs = [job for job in (first, second) if job is not None]
    shared = len(jobs) == 2 and jobs[0][0] == jobs[1][0]
    kinds = [JOBS[job[0]] for job in jobs]
    taken = {}
    for job in jobs:
        taken.update(job[2])
    writes = []
    for kind in kinds:
        writes += [name for name in kind.writes if name not in writes]
    reads = []
    for kind in kinds:
        for name in kind.reads:
            if name in state and name not in reads and name not in writes:
                reads.append(name)
            elif name in (K.streams, K.cotangent):
                taken[name] = fixed[name]
    used = [name for name in WEIGHT_NAMES if any(name in kind.weights for kind in kinds)]
    fresh = [name for name in writes if name not in state or name in (K.send, K.ln)]
    kept = [name for name in writes if name not in fresh]
    small = [name for name in fixed if name not in (K.streams, K.cotangent)]
    if all(job[0] in GRAD_JOBS for job in jobs):
        small = [K.section, K.device, K.counts]
    elif not any(job[0] in (K.radar, K.merged) for job in jobs):
        small = [name for name in small if name not in (K.cross_gain, K.cross_bias)]
    every = scratch_shapes(plan)
    need = list(used)
    for kind in kinds:
        need += [name for name in kind.scratch if name not in need]

    operands, specs, names = [], [], []
    for name in small:
        operands.append(fixed[name])
        specs.append(SM if name in (K.section, K.device, K.counts, K.radar_counts, K.slopes) else VM)
        names.append(name)
    for name in used:
        operands.append(weights[name])
        specs.append(ANY)
        names.append(name)
    for name, array in list(taken.items()) + [(name, state[name]) for name in reads]:
        operands.append(array)
        specs.append(VM if name in IN_VMEM else ANY)
        names.append(name)
    operands += after
    specs += [ANY] * len(after)
    names += [None] * len(after)
    alias = {}
    for at, name in enumerate(kept):
        alias[len(operands)] = at
        operands.append(state[name])
        specs.append(ANY)
        names.append(None)
    outs = kept + fresh
    shapes = [jax.ShapeDtypeStruct(*STATE[name](plan)) for name in outs]

    def kernel(*refs):
        r, s = {}, {}
        for name, ref in zip(names, refs):
            if name is not None:
                r[name] = ref
        refs = refs[len(names) :]
        for name, ref in zip(outs, refs):
            r[name] = ref
        refs = refs[len(outs) :]
        for name, ref in zip(need, refs):
            s[name] = ref
        sems = refs[len(need)]
        if shared:
            RUN[first[0]](plan, r, s, Copies(sems), first[1])
            return
        for which, job in ((0, first), (1, second)):
            if job is not None:

                @pl.when(r[K.section][0] == which)
                def _():
                    RUN[job[0]](plan, r, s, Copies(sems), job[1])

    results = pl.pallas_call(
        kernel,
        out_shape=shapes,
        in_specs=specs,
        out_specs=[ANY] * len(outs),
        scratch_shapes=[pltpu.VMEM(*every[name]) for name in need] + [pltpu.SemaphoreType.DMA((32,))],
        input_output_aliases=alias,
        compiler_params=pltpu.CompilerParams(vmem_limit_bytes=VMEM_LIMIT),
        cost_estimate=CHEAP,
        name="_".join(job[0].name + str(job[1]) for job in jobs),
    )(*operands)
    new = dict(zip(outs, results))
    for name in outs:
        if name not in (K.send, K.ln):
            state[name] = new[name]
    return new.get(K.send), new.get(K.ln)


def body(
    streams,
    cotangent,
    counts,
    positions,
    radar_counts,
    radar_positions,
    qkv_weight,
    out_weight,
    fc1_weight,
    fc2_weight,
    attn_bias,
    mlp_bias,
    norm_gains,
    norm_shifts,
    cross_qkv_weight,
    cross_out_weight,
    cross_gain,
    cross_bias,
):
    devices = lax.axis_size(BATCH)
    section_id = lax.axis_index(SECTION)
    me = lax.axis_index(BATCH)
    width = cotangent.shape[1]
    hidden = fc1_weight.shape[2]
    halving = devices == 16
    plan = Plan(counts.shape[0], positions.shape[1], width, hidden, halving)
    device = me.astype(jnp.int32).reshape(1)
    section = section_id.astype(jnp.int32).reshape(1)
    head_slopes = [2.0 ** (-8.0 * (head + 1.0) / H) for head in range(H)]
    fixed = {
        K.section: section,
        K.device: device,
        K.counts: counts,
        K.radar_counts: radar_counts,
        K.slopes: jnp.array(head_slopes, F32),
        K.positions: positions,
        K.radar_positions: radar_positions,
        K.attn_bias: attn_bias,
        K.mlp_bias: mlp_bias,
        K.gains: norm_gains,
        K.shifts: norm_shifts,
        K.cross_gain: cross_gain.reshape(1, width),
        K.cross_bias: cross_bias.reshape(1, 4 * width),
        K.streams: streams[0],
        K.cotangent: cotangent,
    }
    weights = dict(
        zip(
            WEIGHT_NAMES,
            (
                qkv_weight[0],
                out_weight[0],
                fc1_weight[0],
                fc2_weight[0],
                cross_qkv_weight,
                cross_out_weight,
            ),
        )
    )
    state = {}
    steps = plan.steps
    arrived = []
    for k in range(steps):
        second = (K.radar, 0, {}) if k == min(1, steps - 1) else None
        send, _ = phase(plan, fixed, state, weights, (K.forward, k, {}), second)
        arrived.append(lax.ppermute(send, SECTION, [(0, 1)]))
    returned, first_sums, second_sums = [], [], []
    for k in range(steps):
        send, sums = phase(
            plan, fixed, state, weights, None, (K.merged, k, {K.received: arrived[k]})
        )
        second_sums.append(sums)
        returned.append(lax.ppermute(send, SECTION, [(1, 0)]))
        if 0 < k < steps - 1:
            _, sums = phase(
                plan, fixed, state, weights, (K.backward, k - 1, {K.returned: returned[k - 1]}), None
            )
            first_sums.append(sums)

    route = {bit: [(at, at ^ bit) for at in range(devices)] for bit in (1, 2, 4, 8, 12)} if halving else {}

    def trade(block, bit):
        return lax.ppermute(block, BATCH, route[bit])

    def trade_second(block, bit):
        pairs = [(devices + left, devices + right) for left, right in route[bit]]
        return lax.ppermute(block, (SECTION, BATCH), pairs)

    is_first = section_id == 0

    def to_both(block):
        return jnp.where(is_first, lax.ppermute(block, SECTION, [(1, 0)]), block).astype(F32)

    def scatter(part):
        return lax.psum_scatter(part, BATCH, scatter_dimension=0, tiled=True).astype(F32)

    def run(first, second, after=()):
        _, sums = phase(plan, fixed, state, weights, first, second, after=list(after))
        if first is not None and first[0] in BACK_JOBS:
            first_sums.append(sums)

    def both(job, taken, after=()):
        run((job, 0, taken), (job, 0, taken), after)

    def add_up(parts, low, high):
        return sum(part[low:high].astype(F32) for part in parts)

    def begin(name, exchange, pieces=1):
        kept, sent = state[name], state[SENT[name]]
        kept, sent = (x.reshape(8, -1, x.shape[-1]) for x in (kept, sent))
        come = [exchange(piece, 1) for piece in jnp.split(sent, pieces)]
        return [kept, jnp.concatenate(come) if pieces > 1 else come[0]]

    def step(parts, exchange, bit):
        half = parts[-1].shape[0] // 2
        return parts + [exchange(add_up(parts, half, 2 * half).astype(BF), bit)]

    def along_z(parts):
        return [add_up(parts, at, at + 1).astype(BF) for at in (1, 2, 3)]

    def come_along_z(parts, sends, exchange):
        come = [exchange(part, bit) for part, bit in zip(sends, (8, 4, 12))]
        return [part[:1] for part in parts] + come

    def spread(parts, exchange):
        return come_along_z(parts, along_z(parts), exchange)

    def total(parts):
        return add_up(parts, 0, 1)[0]

    def taken_sums():
        return dict(zip(FIRST, first_sums)) | dict(zip(SECOND, second_sums))

    def once(*arrays):
        return lax.optimization_barrier(arrays)

    last = steps - 1
    queue = [(K.backward, k, {K.returned: returned[k]}) for k in range(max(last - 1, 0), last)] or [None]
    for job in queue[:-1]:
        run(job, None)
    run(queue[-1], (K.grads_early, 0, {}))
    if halving:
        taken = {K.returned: returned[last]}
        run((K.grads_fc2, 0, taken), None)
        fc2 = step(begin(K.fc2, trade), trade, 2)
        run((K.backward_mlp, last, taken), (K.grads_late, 0, {}), [fc2[1]])
        cross = begin(K.cross, trade_second)
        half = cross[0].shape[-1] // 2
        pair_sum = add_up(cross, 0, 8).astype(BF)
        mine, theirs = pair_sum[..., :half], pair_sum[..., half:]
        theirs = lax.ppermute(theirs, SECTION, [(1, 0)])
        run((K.grads_fc1, 0, {}), None)
        state[K.fc1], state[K.fc1_send], fc2[-1] = once(
            state[K.fc1], state[K.fc1_send], fc2[-1]
        )
        fc1 = begin(K.fc1, trade)
        fc2 = spread(fc2, trade)
        run((K.backward_self, last, {}), None, [fc1[-1]])
        fc1 = step(fc1, trade, 2)
        both(K.grads_attn, taken_sums())
        state[K.attn], state[K.attn_send], fc1[-1], theirs, *fc2[-3:] = once(
            state[K.attn], state[K.attn_send], fc1[-1], theirs, *fc2[-3:]
        )
        cross = step([jnp.where(is_first, theirs, mine)], trade, 2)
        attn = begin(K.attn, trade)
        ahead = add_up(attn, 4, 8).astype(BF)
        sends = along_z(fc1)
        ahead, small, *sends = once(ahead, state[K.small], *sends)
        attn.append(trade(ahead, 2))
        fc1 = come_along_z(fc1, sends, trade)
        small = small + trade(small, 1)
        next_small = trade(small, 2)
        run(None, (K.radar_back, 0, {}), [small])
        attn[-1], next_small, state[K.input_grads], cross[-1], *fc1[-3:] = once(
            attn[-1], next_small, state[K.input_grads], cross[-1], *fc1[-3:]
        )
        small = small + next_small
        attn = spread(attn, trade)
        cross = spread(cross, trade)
        small = small + sum(trade(small, bit) for bit in (4, 8, 12))
        mine, grad_fc2, grad_fc1, grad_attn = (total(x) for x in (cross, fc2, fc1, attn))
        mine = mine.astype(BF)
        theirs = lax.ppermute(mine, SECTION, [(0, 1), (1, 0)])
        ends = (jnp.where(is_first, theirs, mine), jnp.where(is_first, mine, theirs))
        cross_all = jnp.concatenate(ends, axis=1).astype(F32)
    else:
        taken = {K.returned: returned[last]}
        run((K.grads_fc2, 0, taken), None)
        run((K.backward_mlp, last, taken), (K.grads_late, 0, {}))
        run((K.grads_fc1, 0, {}), None)
        run((K.backward_self, last, {}), None)
        both(K.grads_attn, taken_sums())
        small = lax.psum(state[K.small], BATCH)
        run(None, (K.radar_back, 0, {}))
        cross_share, grad_fc2, grad_fc1, grad_attn = (
            scatter(state[name]) for name in (K.cross, K.fc2, K.fc1, K.attn)
        )
        cross_all = to_both(cross_share.astype(BF))
    split = qkv_weight.shape[2]

    ratio = hidden // width
    edges = [0, 3, 4 + ratio, 6 + ratio, 8 + ratio, 9 + ratio, 13 + ratio]
    cross_small = to_both(small[edges[4] : edges[6]])
    parts = []
    for low, high in zip(edges, edges[1:]):
        rows = small[low:high] if high <= edges[4] else cross_small[low - edges[4] : high - edges[4]]
        size = (high - low) * width // devices
        parts.append(lax.dynamic_slice(rows.reshape(-1), (me * size,), (size,)))
    return (
        state[K.layer_out][None],
        state[K.input_grads][None],
        grad_attn[None],
        grad_fc1[None, :, hidden:],
        grad_fc1[None, :, :hidden],
        grad_fc2[None],
        parts[0][None],
        parts[1][None],
        parts[2][None],
        parts[3][None],
        cross_all[:, :split],
        cross_all[:, split:],
        parts[4],
        parts[5],
    )


def solution(mesh):
    in_specs = (
        P(SECTION, BATCH, None),
        P(BATCH, None),
        P(BATCH),
        P(BATCH, None),
        P(BATCH),
        P(BATCH, None),
        P(SECTION, None, None),
        P(SECTION, None, None),
        P(SECTION, None, None),
        P(SECTION, None, None),
        P(SECTION, None),
        P(SECTION, None),
        P(SECTION, None),
        P(SECTION, None),
        P(),
        P(),
        P(),
        P(),
    )
    out_specs = (
        P(SECTION, BATCH, None),
        P(SECTION, BATCH, None),
        P(SECTION, BATCH, None),
        P(SECTION, BATCH, None),
        P(SECTION, BATCH, None),
        P(SECTION, BATCH, None),
        P(SECTION, BATCH),
        P(SECTION, BATCH),
        P(SECTION, BATCH),
        P(SECTION, BATCH),
        P(BATCH, None),
        P(BATCH, None),
        P(BATCH),
        P(BATCH),
    )
    return jax.shard_map(body, mesh=mesh, in_specs=in_specs, out_specs=out_specs, check_vma=False)
```
